32 devices in a mesh: dp: 8 (over z, x), mp: 4 (over y, core).
Axes of the slice: x: 2, y: 2, z: 4, core: 2. Of those that a mesh axis runs over, the one named last changes fastest.
Arguments:
- tokens: bfloat16 [8192, 2048], P('dp'), may hold values from -6 to 6
- cotangent: bfloat16 [8192, 2048], P('dp'), may hold values from -6 to 6
- segment_ids: int32 [8, 1024], P('dp'), may hold values from 0 to 7, never falling along the last dimension, each value on 1 to 512 neighbouring positions
- w_query: float32 [2048, 2048], P('dp', 'mp'), may hold values from -3 to 3
- w_key: float32 [2048, 1024], P('dp', 'mp'), may hold values from -3 to 3
- w_value: float32 [2048, 1024], P('dp', 'mp'), may hold values from -3 to 3
- w_out: float32 [2048, 2048], P(('mp', 'dp')), may hold values from -3 to 3
- w_gate_up: float32 [2, 2048, 8192], P(None, 'dp', 'mp'), may hold values from -3 to 3
- w_down: float32 [8192, 2048], P(('mp', 'dp')), may hold values from -3 to 3
- norm_gains: float32 [2, 2048], P(None, 'dp'), may hold values from 0.5 to 1.5
- query_moments: float32 [2, 2048, 2048], P(None, 'dp', 'mp'), may hold values from -65536 to 131072, as said below
- key_moments: float32 [2, 2048, 1024], P(None, 'dp', 'mp'), may hold values from -65536 to 131072, as said below
- value_moments: float32 [2, 2048, 1024], P(None, 'dp', 'mp'), may hold values from -65536 to 131072, as said below
- out_moments: float32 [2, 2048, 2048], P(None, ('mp', 'dp')), may hold values from -65536 to 131072, as said below
- gate_up_moments: float32 [2, 2, 2048, 8192], P(None, None, 'dp', 'mp'), may hold values from -65536 to 131072, as said below
- down_moments: float32 [2, 8192, 2048], P(None, ('mp', 'dp')), may hold values from -65536 to 131072, as said below
- gains_moments: float32 [2, 2, 2048], P(None, None, 'dp'), may hold values from -65536 to 131072, as said below
Outputs:
- block_output: bfloat16 [8192, 2048], P('dp')
- input_grad: float32 [8192, 2048], P('dp')
- grad_query: float32 [2048, 2048], P('dp', 'mp')
- grad_key: float32 [2048, 1024], P('dp', 'mp')
- grad_value: float32 [2048, 1024], P('dp', 'mp')
- grad_out: float32 [2048, 2048], P(('mp', 'dp'))
- grad_gate_up: float32 [2, 2048, 8192], P(None, 'dp', 'mp')
- grad_down: float32 [8192, 2048], P(('mp', 'dp'))
- grad_gains: float32 [2, 2048], P(None, 'dp')
- moments_query: float32 [2048, 2048], P('dp', 'mp')
- moments_key: float32 [2048, 1024], P('dp', 'mp')
- moments_value: float32 [2048, 1024], P('dp', 'mp')
- moments_out: float32 [2048, 2048], P(('mp', 'dp'))
- moments_gate_up: float32 [2, 2048, 8192], P(None, 'dp', 'mp')
- moments_down: float32 [8192, 2048], P(('mp', 'dp'))
- moments_gains: float32 [2, 2048], P(None, 'dp')
- new_query: float32 [2048, 2048], P('dp', 'mp')
- new_key: float32 [2048, 1024], P('dp', 'mp')
- new_value: float32 [2048, 1024], P('dp', 'mp')
- new_out: float32 [2048, 2048], P(('mp', 'dp'))
- new_gate_up: float32 [2, 2048, 8192], P(None, 'dp', 'mp')
- new_down: float32 [8192, 2048], P(('mp', 'dp'))
- new_gains: float32 [2, 2048], P(None, 'dp')
- copy_query: bfloat16 [2048, 2048], P('dp', 'mp')
- copy_key: bfloat16 [2048, 1024], P('dp', 'mp')
- copy_value: bfloat16 [2048, 1024], P('dp', 'mp')
- copy_out: bfloat16 [2048, 2048], P(('mp', 'dp'))
- copy_gate_up: bfloat16 [2, 2048, 8192], P(None, 'dp', 'mp')
- copy_down: bfloat16 [8192, 2048], P(('mp', 'dp'))
- copy_gains: bfloat16 [2, 2048], P(None, 'dp')
- norms: float32 [2, 7], replicated
- head_maxima: float32 [16], replicated
The draws below stay inside these ranges and needn't reach their ends.
Inputs may be any that keep to these rules, and one draw needn't show every extreme that they name: `segment_ids`: ids never fall along a sequence; a document spans at most 512 tokens, and one in every sequence spans exactly that many. `query_moments`: the second moments are positive. `key_moments`: the second moments are positive. `value_moments`: the second moments are positive. `out_moments`: the second moments are positive. `gate_up_moments`: the second moments are positive. `down_moments`: the second moments are positive. `gains_moments`: the second moments are positive.
All inputs are finite; a program needn't handle non-finite values.
Results may differ from the reference program's by a relative error of at most 0.015.
The reference program's roundings to bfloat16 on the way count: a program that leaves them out, or rounds other values in their place, can miss the bound.
Values may be sent and summed in bfloat16 or wider, within the bound.
A program may use at most 320 MiB of HBM per device.

```python
import math
import jax
import jax.numpy as jnp
import numpy as np
from jax import lax

D = 2048
HEADS = 16
KV_HEADS = 8
HEAD = 128
FF = 8192
SEQ = 1024
DOCS = 8
BLOCK = 512
CLIP = 10
SEQS = 8
TOKENS = 8192
N_MP = 4


def row_factors(rows, groups):
    span = rows // groups
    place = (jnp.arange(rows, dtype=jnp.int32) % span).astype(jnp.float32) / float(span)
    top = 3.0
    factor = 1.0 + (top - 1.0) * place
    mean_square = 1.0 + (top - 1.0) + (top - 1.0) * (top - 1.0) / 3.0
    return factor / math.sqrt(mean_square)


def rising_entries(key, salt, rows, columns, groups, fan_in):
    entry_key = jax.random.fold_in(key, salt)
    entries = jnp.clip(jax.random.normal(entry_key, (rows, columns), jnp.float32), -6.0, 6.0)
    return entries * row_factors(rows, groups)[:, None] / math.sqrt(fan_in)


def draw_w_query(key, part):
    head_key = jax.random.fold_in(key, 12)
    head_scales = jnp.exp(jax.random.uniform(head_key, (HEADS,), jnp.float32, 0.0, math.log(3.0)))
    column_scales = jnp.repeat(head_scales, HEAD)
    return rising_entries(key, 11, D, HEADS * HEAD, 1, D) * column_scales[None, :]


def draw_w_key(key, part):
    return rising_entries(key, 13, D, KV_HEADS * HEAD, 1, D)


def draw_w_value(key, part):
    return rising_entries(key, 14, D, KV_HEADS * HEAD, 1, D)


def draw_w_out(key, part):
    return rising_entries(key, 15, HEADS * HEAD, D, N_MP, HEADS * HEAD // 8)


def draw_w_gate_up(key, part):
    return jnp.stack([rising_entries(key, 16, D, FF, 1, D), rising_entries(key, 17, D, FF, 1, D)])


def draw_w_down(key, part):
    return rising_entries(key, 18, FF, D, N_MP, FF // 3)


def moment_pair(key, salt, array_shape, grad_size):
    first_key, second_key = jax.random.split(jax.random.fold_in(key, salt))
    first_moment = jnp.clip(jax.random.normal(first_key, array_shape, jnp.float32), -4.0, 4.0) * grad_size
    factor = jnp.exp(jax.random.uniform(second_key, array_shape, jnp.float32, 0.0, math.log(4.0)))
    return jnp.stack([first_moment, factor * grad_size * grad_size])


def draw_query_moments(key, part):
    return moment_pair(key, 31, (D, HEADS * HEAD), math.sqrt(TOKENS))


def draw_key_moments(key, part):
    return moment_pair(key, 32, (D, KV_HEADS * HEAD), 1.5 * math.sqrt(TOKENS))


def draw_value_moments(key, part):
    return moment_pair(key, 33, (D, KV_HEADS * HEAD), 1.5 * math.sqrt(TOKENS))


def draw_out_moments(key, part):
    return moment_pair(key, 34, (HEADS * HEAD, D), 0.6 * math.sqrt(TOKENS))


def draw_gate_up_moments(key, part):
    return moment_pair(key, 35, (2, D, FF), 0.5 * math.sqrt(TOKENS))


def draw_down_moments(key, part):
    return moment_pair(key, 36, (FF, D), 0.6 * math.sqrt(TOKENS))


def draw_gains_moments(key, part):
    return moment_pair(key, 37, (2, D), 2.0 * math.sqrt(TOKENS))


def steps_of(own_key, extent, cuts, smallest, high):
    factor_of = 1.0
    for dim, shards_of in cuts:
        draws = jax.random.uniform(jax.random.fold_in(jax.random.fold_in(own_key, 6), dim), (shards_of,), jnp.float32, smallest / len(cuts), high / len(cuts))
        factor_of = factor_of * jnp.repeat(jnp.exp(draws), extent[dim] // shards_of).reshape((-1,) + (1,) * (len(extent) - 1 - dim))
    return factor_of


def length_profile(amount, total, reach, skew):
    weights = [(1 << 20) // math.isqrt(standing ** skew) + 1 for standing in range(2, amount + 1)]
    surplus, counts = total - reach - (amount - 1), [1] * (amount - 1)
    while surplus > 0:
        free = [i for i in range(amount - 1) if counts[i] < reach]
        pool, left = sum([weights[i] for i in free]), surplus
        for i in free:
            addition = min(reach - counts[i], max(1, left * weights[i] // pool), surplus)
            counts[i] = counts[i] + addition
            surplus = surplus - addition
    return np.array([reach] + counts)


def ragged_sizes(own_key, count, total, most, slope):
    if count == 2:
        one = jax.random.randint(own_key, (), max(1, total - most), min(most, total - 1) + 1)
        return jnp.stack([one, total - one])
    sizes = jnp.asarray(length_profile(count, total, most, slope), jnp.int32)
    couples = (count - 1) // 2
    source_of, sink = sizes[1:1 + 2 * couples:2], sizes[2:2 + 2 * couples:2]
    slack = jnp.minimum(source_of - 1, most - sink)
    moved = jax.random.randint(jax.random.fold_in(own_key, 1), (couples,), 0, 1 << 20) % (slack + 1)
    sizes = sizes.at[1:1 + 2 * couples:2].set(source_of - moved).at[2:2 + 2 * couples:2].set(sink + moved)
    return sizes[jax.random.permutation(jax.random.fold_in(own_key, 2), count)]


def noise(key, extent, spread, reach, pieces=(), kind=jnp.bfloat16):
    values = spread * jax.random.normal(key, extent, jnp.float32)
    if pieces:
        values = values * steps_of(key, extent, pieces, -0.22, 0.18)
    return jnp.clip(values, -reach, reach).astype(kind)


def setup_inputs(seed: int = 0) -> dict:
    key_list = jax.random.split(jax.random.key(seed), 18)
    return {
        "tokens": noise(key_list[0], (TOKENS, D), 1.0, 6.0, ((0, 8),)),
        "cotangent": noise(key_list[1], (TOKENS, D), 1.0, 6.0, ((0, 8),)),
        "segment_ids": jax.vmap(lambda own: jnp.searchsorted(jnp.cumsum(ragged_sizes(own, DOCS, SEQ, SEQ // 2, 2)), jnp.arange(SEQ), side="right"))(jax.random.split(key_list[2], SEQS)).reshape((SEQS, SEQ)).astype(jnp.int32),
        "w_query": draw_w_query(jax.random.fold_in(key_list[17], 71), 0),
        "w_key": draw_w_key(jax.random.fold_in(key_list[17], 71), 0),
        "w_value": draw_w_value(jax.random.fold_in(key_list[17], 71), 0),
        "w_out": draw_w_out(jax.random.fold_in(key_list[17], 71), 0),
        "w_gate_up": draw_w_gate_up(jax.random.fold_in(key_list[17], 71), 0),
        "w_down": draw_w_down(jax.random.fold_in(key_list[17], 71), 0),
        "norm_gains": jnp.clip(1.0 + 0.1 * jax.random.normal(key_list[9], (2, D), jnp.float32), 0.5, 1.5),
        "query_moments": draw_query_moments(jax.random.fold_in(key_list[17], 71), 0),
        "key_moments": draw_key_moments(jax.random.fold_in(key_list[17], 71), 0),
        "value_moments": draw_value_moments(jax.random.fold_in(key_list[17], 71), 0),
        "out_moments": draw_out_moments(jax.random.fold_in(key_list[17], 71), 0),
        "gate_up_moments": draw_gate_up_moments(jax.random.fold_in(key_list[17], 71), 0),
        "down_moments": draw_down_moments(jax.random.fold_in(key_list[17], 71), 0),
        "gains_moments": draw_gains_moments(jax.random.fold_in(key_list[17], 71), 0),
    }


NORM_EPS = 1e-05
ROPE_BASE = 1000000.0
RATE = 0.4
DECAY = 0.5
WEIGHT_DECAY = 0.01
STEP_EPS = 1e-06
MASKED = -1e+30

@jax.custom_vjp
def low(v):
    return lax.optimization_barrier(v.astype(jnp.bfloat16)).astype(jnp.float32)

@jax.custom_vjp
def low_back(v):
    return v

def low_keep(v):
    return (low(v), None)

def low_pass(kept, grad):
    return (grad,)

def back_keep(v):
    return (v, None)

def back_low(kept, grad):
    return (low(grad),)
low.defvjp(low_keep, low_pass)
low_back.defvjp(back_keep, back_low)

def matmul_high(left, right):
    return jnp.dot(left, right, precision=lax.Precision.HIGHEST, preferred_element_type=jnp.float32)

def rope_tables(length):
    positions = jnp.arange(length, dtype=jnp.float32)
    frequency = ROPE_BASE ** (-(jnp.arange(HEAD // 2, dtype=jnp.float32) * 2.0) / HEAD)
    angles = positions[:, None] * frequency[None, :]
    return (jnp.concatenate([jnp.cos(angles), jnp.cos(angles)], 1), jnp.concatenate([jnp.sin(angles), jnp.sin(angles)], 1))

def rotate(values, cosine_table, sine_table):
    half_width = values.shape[-1] // 2
    turned = jnp.concatenate([-values[..., half_width:], values[..., :half_width]], -1)
    return values * cosine_table[:, None, :] + turned * sine_table[:, None, :]

def rms_scale(values, gain_row):
    return values * lax.rsqrt(lax.optimization_barrier(jnp.mean(values * values, -1, keepdims=True)) + NORM_EPS) * gain_row

def gated_unit(gate_part, up_part):
    return jax.nn.silu(gate_part) * up_part

def forward(inputs, copies, segments):
    query_w, key_w, value_w, out_w, gate_up_w, down_w, gain_rows = copies
    cosine_table, sine_table = rope_tables(SEQ)
    group_size = HEADS // KV_HEADS
    normed_one = low(rms_scale(inputs, gain_rows[0]))
    queries = low_back(matmul_high(normed_one, query_w)).reshape(SEQ, HEADS, HEAD)
    key_rows = low_back(matmul_high(normed_one, key_w)).reshape(SEQ, KV_HEADS, HEAD)
    value_rows = low(low_back(matmul_high(normed_one, value_w))).reshape(SEQ, KV_HEADS, HEAD)
    query_rot = low(rotate(queries, cosine_table, sine_table))
    key_rot = jnp.repeat(low(rotate(key_rows, cosine_table, sine_table)), group_size, axis=1)
    value_all = jnp.repeat(value_rows, group_size, axis=1)
    positions = jnp.arange(SEQ, dtype=jnp.int32)

    def attend(block_start):
        query_block = lax.dynamic_slice_in_dim(query_rot, block_start, BLOCK, 0)
        seg_block = lax.dynamic_slice_in_dim(segments, block_start, BLOCK, 0)
        pos_block = block_start + jnp.arange(BLOCK, dtype=jnp.int32)
        scores = low_back(jnp.einsum('qhd,khd->hqk', query_block, key_rot, precision=lax.Precision.HIGHEST) * (1.0 / math.sqrt(HEAD)))
        allowed = (positions[None, :] <= pos_block[:, None]) & (seg_block[:, None] == segments[None, :])
        masked = jnp.where(allowed[None], scores, MASKED)
        attn_probs = jax.nn.softmax(masked, axis=-1)
        mixed_rows = jnp.einsum('hqk,khd->qhd', low(attn_probs), value_all, precision=lax.Precision.HIGHEST)
        return (mixed_rows, lax.optimization_barrier(jnp.max(masked, axis=(1, 2))))
    starts = jnp.arange(SEQ // BLOCK, dtype=jnp.int32) * BLOCK
    mixed_all, block_peaks = lax.map(jax.checkpoint(attend), starts)
    attended = low(low_back(mixed_all.reshape(SEQ, HEADS * HEAD)))
    middle = inputs + low_back(matmul_high(attended, out_w))
    normed_two = low(rms_scale(middle, gain_rows[1]))
    gate_act = low_back(matmul_high(normed_two, gate_up_w[0]))
    up_act = low_back(matmul_high(normed_two, gate_up_w[1]))
    hidden = low(gated_unit(gate_act, up_act))
    result = middle + low_back(matmul_high(hidden, down_w))
    return (result, lax.optimization_barrier(jnp.max(block_peaks, 0)))

def reference(tokens, cotangent, segment_ids, w_query, w_key, w_value, w_out, w_gate_up, w_down, norm_gains, query_moments, key_moments, value_moments, out_moments, gate_up_moments, down_moments, gains_moments):
    masters = (w_query, w_key, w_value, w_out, w_gate_up, w_down, norm_gains)
    moment_list = (query_moments, key_moments, value_moments, out_moments, gate_up_moments, down_moments, gains_moments)
    copies = tuple((lax.optimization_barrier(master.astype(jnp.bfloat16)).astype(jnp.float32) for master in masters))
    inputs = tokens.astype(jnp.float32).reshape(SEQS, SEQ, D)
    seq_cotangent = cotangent.astype(jnp.float32).reshape(SEQS, SEQ, D)

    def advance(carried, element):
        totals, highest = carried
        seq_inputs, seq_grads, segments = element

        def one_sequence(values, weights):
            return forward(values, weights, segments)
        result, pull, seq_peaks = jax.vjp(one_sequence, seq_inputs, copies, has_aux=True)
        grad_inputs, grad_weights = pull(seq_grads)
        totals = tuple((total_part + grad_part for total_part, grad_part in zip(totals, grad_weights)))
        return ((totals, jnp.maximum(highest, seq_peaks)), (result.astype(jnp.bfloat16), grad_inputs))
    start_totals = tuple((jnp.zeros_like(single) for single in copies))
    start_peak = jnp.full((HEADS,), MASKED, jnp.float32)
    (grads, peak_all), (seq_outputs, seq_input_grads) = lax.scan(advance, (start_totals, start_peak), (inputs, seq_cotangent, segment_ids))
    block_output = seq_outputs.reshape(TOKENS, D)
    input_grad = seq_input_grads.reshape(TOKENS, D)
    new_moments = []
    directions = []
    weight_sq = []
    update_sq = []
    for master, grad_sum, moment in zip(masters, grads, moment_list):
        first_moment = DECAY * moment[0] + (1.0 - DECAY) * grad_sum
        second_moment = DECAY * moment[1] + (1.0 - DECAY) * grad_sum * grad_sum
        direction = first_moment / (jnp.sqrt(second_moment) + STEP_EPS) + WEIGHT_DECAY * master
        new_moments.append(second_moment)
        directions.append(direction)
        weight_sq.append(jnp.sum(master * master))
        update_sq.append(jnp.sum(direction * direction))
    weight_norm = jnp.sqrt(jnp.stack(weight_sq))
    update_norm = jnp.sqrt(jnp.stack(update_sq))
    ratio = weight_norm / (update_norm + STEP_EPS)
    stepped = [masters[number] - RATE * ratio[number] * directions[number] for number in range(7)]
    gamma = CLIP / jnp.maximum(peak_all, CLIP)
    query_scale = jnp.sqrt(gamma)
    key_scale = jnp.sqrt(lax.optimization_barrier(jnp.min(gamma.reshape(KV_HEADS, HEADS // KV_HEADS), 1)))
    new_query = (stepped[0].reshape(D, HEADS, HEAD) * query_scale[None, :, None]).reshape(D, HEADS * HEAD)
    new_key = (stepped[1].reshape(D, KV_HEADS, HEAD) * key_scale[None, :, None]).reshape(D, KV_HEADS * HEAD)
    new_value = stepped[2]
    new_out = stepped[3]
    new_gate_up = stepped[4]
    new_down = stepped[5]
    new_gains = stepped[6]
    norms = jnp.stack([weight_norm, update_norm])
    return (block_output, input_grad, grads[0], grads[1], grads[2], grads[3], grads[4], grads[5], grads[6], new_moments[0], new_moments[1], new_moments[2], new_moments[3], new_moments[4], new_moments[5], new_moments[6], new_query, new_key, new_value, new_out, new_gate_up, new_down, new_gains, new_query.astype(jnp.bfloat16), new_key.astype(jnp.bfloat16), new_value.astype(jnp.bfloat16), new_out.astype(jnp.bfloat16), new_gate_up.astype(jnp.bfloat16), new_down.astype(jnp.bfloat16), new_gains.astype(jnp.bfloat16), norms, peak_all)
```

```python
import functools
import math

import jax
import jax.numpy as jnp
from jax import lax
from jax.experimental import pallas as pl
from jax.experimental.pallas import tpu as pltpu
from jax.sharding import PartitionSpec as P

HEADS = 16
HEAD = 128
BLOCK = 512
CLIP = 10
TILE = 256
SLICES = 2

NORM_EPS = 1e-05
ROPE_BASE = 1000000.0
RATE = 0.4
DECAY = 0.5
WEIGHT_DECAY = 0.01
STEP_EPS = 1e-06
MASKED = -1e30

F32 = jnp.float32
BF16 = jnp.bfloat16


def rope_tables(length):
    positions = jnp.arange(length, dtype=F32)
    frequency = ROPE_BASE ** (-(jnp.arange(HEAD // 2, dtype=F32) * 2.0) / HEAD)
    angles = positions[:, None] * frequency[None, :]
    cosine, sine = jnp.cos(angles), jnp.sin(angles)
    return jnp.concatenate([cosine, cosine], 1), jnp.concatenate([-sine, sine], 1)


def turn(values, cosine, sine):
    return values * cosine + pltpu.roll(values, HEAD // 2, 1) * sine


def allowed_mask(seg_row_ref, seg_col_ref, row_start, low, high):
    query_pos = row_start + lax.broadcasted_iota(jnp.int32, (TILE, high - low), 0)
    key_pos = low + lax.broadcasted_iota(jnp.int32, (TILE, high - low), 1)
    same = seg_col_ref[row_start : row_start + TILE, :] == seg_row_ref[0, :, low:high]
    return (key_pos <= query_pos) & same


def dot_nt(left, right):
    return lax.dot_general(left, right, (((1,), (1,)), ((), ())), preferred_element_type=F32)


def dot_nn(left, right):
    return lax.dot_general(left, right, (((1,), (0,)), ((), ())), preferred_element_type=F32)


def dot_tn(left, right):
    return lax.dot_general(left, right, (((0,), (0,)), ((), ())), preferred_element_type=F32)


def attend_forward(group, qkv_ref, cos_ref, sin_ref, seg_row_ref, seg_col_ref, out_ref, rot_ref, lse_ref, peak_ref):
    length = qkv_ref.shape[0]
    scale = 1.0 / math.sqrt(HEAD)
    for part in range(group + 1):
        columns = slice(part * HEAD, (part + 1) * HEAD)
        rot_ref[:, columns] = turn(qkv_ref[:, columns], cos_ref[...], sin_ref[...]).astype(BF16)
    value_columns = slice((group + 1) * HEAD, (group + 2) * HEAD)
    rot_ref[:, value_columns] = qkv_ref[:, value_columns].astype(BF16)
    key_columns = slice(group * HEAD, (group + 1) * HEAD)
    peak_ref[...] = jnp.full(peak_ref.shape, MASKED, F32)
    peaks = [None] * group
    for start in range(0, length, TILE):
        low, high = max(0, start - BLOCK), start + TILE
        rows = slice(start, start + TILE)
        mask = allowed_mask(seg_row_ref, seg_col_ref, start, low, high)
        keys = rot_ref[low:high, key_columns]
        values = rot_ref[low:high, value_columns]
        for head in range(group):
            columns = slice(head * HEAD, (head + 1) * HEAD)
            scores = jnp.where(mask, dot_nt(rot_ref[rows, columns], keys) * scale, MASKED)
            top = jnp.max(scores, 1, keepdims=True)
            exponent = jnp.exp(scores - top)
            total = jnp.sum(exponent, 1, keepdims=True)
            probs = (exponent * (1.0 / total)).astype(BF16)
            out_ref[rows, columns] = dot_nn(probs, values).astype(BF16)
            lse_ref[rows, columns] = jnp.broadcast_to(top + jnp.log(total), (TILE, HEAD))
            peak = jnp.max(top, 0, keepdims=True)
            peaks[head] = peak if peaks[head] is None else jnp.maximum(peaks[head], peak)
    for head in range(group):
        peak_ref[0, head : head + 1, :] = jnp.broadcast_to(peaks[head], (1, HEAD))


def attend_backward(group, rot_ref, grad_ref, lse_ref, cos_ref, sin_ref, seg_row_ref, seg_col_ref, out_ref, dk_ref, dv_ref):
    length = rot_ref.shape[0]
    scale = 1.0 / math.sqrt(HEAD)
    key_columns = slice(group * HEAD, (group + 1) * HEAD)
    value_columns = slice((group + 1) * HEAD, (group + 2) * HEAD)
    dk_ref[...] = jnp.zeros(dk_ref.shape, F32)
    dv_ref[...] = jnp.zeros(dv_ref.shape, F32)
    for start in range(0, length, TILE):
        low, high = max(0, start - BLOCK), start + TILE
        rows = slice(start, start + TILE)
        mask = allowed_mask(seg_row_ref, seg_col_ref, start, low, high)
        keys = rot_ref[low:high, key_columns]
        values = rot_ref[low:high, value_columns]
        for head in range(group):
            columns = slice(head * HEAD, (head + 1) * HEAD)
            queries = rot_ref[rows, columns]
            grads = grad_ref[rows, columns]
            scores = dot_nt(queries, keys) * scale
            probs = jnp.exp(jnp.where(mask, scores - lse_ref[rows, columns][:, :1], MASKED))
            grad_probs = dot_nt(grads, values)
            inner = jnp.sum(probs * grad_probs, 1, keepdims=True)
            grad_scores = (probs * (grad_probs - inner)).astype(BF16)
            dv_ref[low:high, :] += dot_tn(probs.astype(BF16), grads)
            dk_ref[low:high, :] += dot_tn(grad_scores, queries)
            grad_query = dot_nn(grad_scores, keys) * scale
            out_ref[rows, columns] = turn(grad_query, cos_ref[rows, :], -sin_ref[rows, :]).astype(BF16)
    out_ref[:, key_columns] = turn(dk_ref[...] * scale, cos_ref[...], -sin_ref[...]).astype(BF16)
    out_ref[:, value_columns] = dv_ref[...].astype(BF16)


def attention_specs(length, group):
    wide = pl.BlockSpec((length, (group + 2) * HEAD), lambda seq, kv: (seq, kv))
    narrow = pl.BlockSpec((length, group * HEAD), lambda seq, kv: (seq, kv))
    table = pl.BlockSpec((length, HEAD), lambda seq, kv: (0, 0))
    seg_row = pl.BlockSpec((1, 1, length), lambda seq, kv: (seq, 0, 0))
    seg_col = pl.BlockSpec((length, 1), lambda seq, kv: (seq, 0))
    return wide, narrow, table, seg_row, seg_col


def attention_forward(qkv, cosine, sine, segments, group, kv_count):
    count, length = segments.shape
    rows = count * length
    wide, narrow, table, seg_row, seg_col = attention_specs(length, group)
    return pl.pallas_call(
        functools.partial(attend_forward, group),
        grid=(count, kv_count),
        in_specs=[wide, table, table, seg_row, seg_col],
        out_specs=[
            narrow,
            wide,
            narrow,
            pl.BlockSpec((1, 8, HEAD), lambda seq, kv: (seq * kv_count + kv, 0, 0)),
        ],
        out_shape=[
            jax.ShapeDtypeStruct((rows, kv_count * group * HEAD), BF16),
            jax.ShapeDtypeStruct((rows, kv_count * (group + 2) * HEAD), BF16),
            jax.ShapeDtypeStruct((rows, kv_count * group * HEAD), F32),
            jax.ShapeDtypeStruct((count * kv_count, 8, HEAD), F32),
        ],
        compiler_params=pltpu.CompilerParams(vmem_limit_bytes=48 * 2**20),
        name="attention_forward",
    )(qkv, cosine, sine, segments.reshape(count, 1, length), segments.reshape(rows, 1))


def attention_backward(rotated, grads, lse, cosine, sine, segments, group, kv_count):
    count, length = segments.shape
    rows = count * length
    wide, narrow, table, seg_row, seg_col = attention_specs(length, group)
    return pl.pallas_call(
        functools.partial(attend_backward, group),
        grid=(count, kv_count),
        in_specs=[wide, narrow, narrow, table, table, seg_row, seg_col],
        out_specs=wide,
        out_shape=jax.ShapeDtypeStruct((rows, kv_count * (group + 2) * HEAD), BF16),
        scratch_shapes=[pltpu.VMEM((length, HEAD), F32), pltpu.VMEM((length, HEAD), F32)],
        compiler_params=pltpu.CompilerParams(vmem_limit_bytes=48 * 2**20),
        name="attention_backward",
    )(rotated, grads, lse, cosine, sine, segments.reshape(count, 1, length), segments.reshape(rows, 1))


class Links:
    def __init__(self, dp_size, mp_size):
        self.dp, self.mp, self.line = dp_size, mp_size, dp_size // 2
        self.index = lax.axis_index("dp")
        self.place, self.side, self.rank = self.index // 2, self.index % 2, lax.axis_index("mp")

    def swap_mp(self, value, bit):
        return lax.ppermute(value, "mp", [(i, i ^ bit) for i in range(self.mp)])

    def swap_side(self, value, places=None):
        places = range(self.line) if places is None else places
        return lax.ppermute(value, "dp", [(p * 2 + s, p * 2 + 1 - s) for p in places for s in range(2)])

    def move(self, value, places, by):
        return lax.ppermute(value, "dp", [(p * 2 + s, (p + by) * 2 + s) for p in places for s in range(2)])


    def spread(self, own):
        ups, downs = {}, {}
        up = down = own
        for step in range(1, self.line):
            up = ups[step] = self.move(up, range(step - 1, self.line - 1), 1)
            down = downs[step] = self.move(down, range(1, self.line - step + 1), -1)
        return ups, downs

    def from_below(self, step):
        return range(step, self.line)

    def from_above(self, step):
        return range(0, self.line - step)

    def pick(self, ups, downs, step):
        return jnp.where(self.place >= step, ups[step], downs[self.line - step])

    def gather_line(self, own):
        ups, downs = self.spread(own)
        rows = own.shape[0]
        full = jnp.zeros((self.line * rows, own.shape[1]), own.dtype)
        full = lax.dynamic_update_slice(full, own, (self.place * rows, 0))
        for step in range(1, self.line):
            slot = (self.place - step) % self.line
            full = lax.dynamic_update_slice(full, self.pick(ups, downs, step), (slot * rows, 0))
        return full

    def gather_dp(self, own):
        ups, downs = self.spread(own)
        other = self.swap_side(own)
        other_ups = {s: self.swap_side(v, self.from_below(s)) for s, v in ups.items()}
        other_downs = {s: self.swap_side(v, self.from_above(s)) for s, v in downs.items()}
        rows = own.shape[0]
        full = jnp.zeros((self.dp * rows, own.shape[1]), own.dtype)

        def put(full, value, place, side):
            return lax.dynamic_update_slice(full, value, ((place * 2 + side) * rows, 0))

        full = put(full, own, self.place, self.side)
        full = put(full, other, self.place, 1 - self.side)
        for step in range(1, self.line):
            slot = (self.place - step) % self.line
            full = put(full, self.pick(ups, downs, step), slot, self.side)
            full = put(full, self.pick(other_ups, other_downs, step), slot, 1 - self.side)
        return full

    def sum_line(self, part):
        up = down = None
        for step in range(self.line - 1, 0, -1):
            term = part(jnp.minimum(self.place + step, self.line - 1)).astype(F32)
            term = term if up is None else term + up.astype(F32)
            up = self.move(term.astype(BF16), range(0, self.line - step), 1)
            term = part(jnp.maximum(self.place - step, 0)).astype(F32)
            term = term if down is None else term + down.astype(F32)
            down = self.move(term.astype(BF16), range(step, self.line), -1)
        return part(self.place).astype(F32) + up.astype(F32) + down.astype(F32)

    def sum_dp(self, partial):
        rows = partial.shape[0] // self.dp

        def cut(place, side):
            return lax.dynamic_slice_in_dim(partial, (place * 2 + side) * rows, rows, 0)

        def paired(place, places):
            received = self.swap_side(cut(place, 1 - self.side), places)
            return cut(place, self.side).astype(F32) + received.astype(F32)

        last = self.line - 1
        up = down = None
        for step in range(last, 0, -1):
            term = paired(jnp.minimum(self.place + step, last), range(0, self.line - step))
            term = term if up is None else term + up.astype(F32)
            up = self.move(term.astype(BF16), range(0, self.line - step), 1)
            term = paired(jnp.maximum(self.place - step, 0), range(step, self.line))
            term = term if down is None else term + down.astype(F32)
            down = self.move(term.astype(BF16), range(step, self.line), -1)
        return paired(self.place, None) + up.astype(F32) + down.astype(F32)


    def to_slots(self, values):
        rows = values.shape[0] // self.mp
        return jnp.concatenate(
            [lax.dynamic_slice_in_dim(values, (self.rank ^ k) * rows, rows, 0) for k in range(self.mp)], 0
        )

    def from_slots(self, values):
        rows = values.shape[0] // self.mp
        cuts = [values[k * rows : (k + 1) * rows] for k in range(self.mp)]
        odd = (self.rank & 1) == 1
        high = (self.rank & 2) == 2
        cuts = [jnp.where(odd, cuts[k ^ 1], cuts[k]) for k in range(self.mp)]
        cuts = [jnp.where(high, cuts[k ^ 2], cuts[k]) for k in range(self.mp)]
        return jnp.concatenate(cuts, 0)

    def own_quarter(self, values):
        rows = values.shape[0] // self.mp
        return lax.dynamic_slice_in_dim(values, self.rank * rows, rows, 0)

    def sum_core(self, slots):
        rows = slots.shape[0] // 4
        cut = lambda k: slots[k * rows : (k + 1) * rows]
        received = self.swap_mp(jnp.concatenate([cut(1), cut(3)], 0).astype(BF16), 1)
        return jnp.concatenate([cut(0), cut(2)], 0).astype(F32) + received.astype(F32)

    def sum_far(self, pair):
        rows = pair.shape[0] // 2
        received = self.swap_mp(pair[rows:].astype(BF16), 2)
        return pair[:rows].astype(F32) + received.astype(F32)

    def gather_mp(self, quarter):
        rows = quarter.shape[0]
        pair = jnp.concatenate([quarter, self.swap_mp(quarter, 2)], 0)
        near = self.swap_mp(pair, 1)
        return jnp.concatenate([pair[:rows], near[:rows], pair[rows:], near[rows:]], 0)

    def gather_pair(self, quarter):
        rows, columns = quarter.shape
        half = columns // 2
        left, right = quarter[:, :half], quarter[:, half:]
        left_side = self.swap_side(left)
        right_far = self.swap_mp(right, 2)
        left_far = self.swap_mp(jnp.concatenate([left, left_side], 0), 2)
        right_side = self.swap_side(jnp.concatenate([right, right_far], 0))
        left_all = jnp.concatenate([left, left_far[:rows], left_side, left_far[rows:]], 0)
        right_all = jnp.concatenate([right, right_far, right_side[:rows], right_side[rows:]], 0)
        even = jnp.concatenate([left_all, right_all], 1)
        near = self.swap_mp(even, 1)
        cut = lambda v, k: v[k * rows : (k + 1) * rows]
        return jnp.concatenate([cut(v, k) for k in range(4) for v in (even, near)], 0)

    def sum_pair(self, slots):
        total, columns = slots.shape
        rows, half = total // 8, columns // 2
        cut = lambda k: slots[k * rows : (k + 1) * rows]
        near = self.swap_mp(jnp.concatenate([cut(1), cut(3), cut(5), cut(7)], 0).astype(BF16), 1)
        mine = jnp.concatenate([cut(0), cut(2), cut(4), cut(6)], 0).astype(F32) + near.astype(F32)
        mine = mine.astype(BF16)
        left, right = mine[:, :half], mine[:, half:]
        cut = lambda v, k: v[k * rows : (k + 1) * rows]
        left = left[: 2 * rows].astype(F32) + self.swap_side(left[2 * rows :]).astype(F32)
        far = self.swap_mp(jnp.concatenate([cut(right, 1), cut(right, 3)], 0), 2)
        right = jnp.concatenate([cut(right, 0), cut(right, 2)], 0).astype(F32) + far.astype(F32)
        left = left[:rows] + self.swap_mp(left[rows:].astype(BF16), 2).astype(F32)
        right = right[:rows] + self.swap_side(right[rows:].astype(BF16)).astype(F32)
        return jnp.concatenate([left, right], 1)


def after(value, *others):
    return lax.optimization_barrier((value, *others))[0]


def inverse_rms(values):
    return lax.rsqrt(jnp.mean(values * values, -1, keepdims=True) + NORM_EPS)


def norm_pull(values, scale, gain, grad):
    turned = grad * gain
    back = scale * turned - (scale * scale * scale) * values * jnp.mean(turned * values, -1, keepdims=True)
    return back, jnp.sum(grad * values * scale, 0)


def body(
    dp_size,
    mp_size,
    tokens,
    cotangent,
    segment_ids,
    w_query,
    w_key,
    w_value,
    w_out,
    w_gate_up,
    w_down,
    norm_gains,
    query_moments,
    key_moments,
    value_moments,
    out_moments,
    gate_up_moments,
    down_moments,
    gains_moments,
):
    links = Links(dp_size, mp_size)
    line, side = links.line, links.side
    heads = w_query.shape[1] // HEAD
    kvs = w_key.shape[1] // HEAD
    group = heads // kvs
    width = tokens.shape[1]
    shard = w_query.shape[0]
    units = w_gate_up.shape[2]
    block = units // (line * 2)
    piece = block // SLICES

    def interleave(query, key, value):
        parts = []
        for kv in range(kvs):
            parts.append(query[..., kv * group * HEAD : (kv + 1) * group * HEAD])
            parts.append(key[..., kv * HEAD : (kv + 1) * HEAD])
            parts.append(value[..., kv * HEAD : (kv + 1) * HEAD])
        return jnp.concatenate(parts, -1)

    def untangle(values):
        step = (group + 2) * HEAD
        cut = lambda low, high: jnp.concatenate(
            [values[..., kv * step + low * HEAD : kv * step + high * HEAD] for kv in range(kvs)], -1
        )
        return cut(0, group), cut(group, group + 1), cut(group + 1, group + 2)

    qkv_full = links.gather_dp(interleave(w_query, w_key, w_value).astype(BF16))
    gains_full = lax.all_gather(norm_gains.astype(BF16), "dp", axis=1, tiled=True).astype(F32)

    by_side = w_gate_up.reshape(2, shard, line, 2, block)

    def side_units(which):
        cut = lax.dynamic_index_in_dim(by_side, which, 3, keepdims=False).astype(BF16)
        return [cut[..., j * piece : (j + 1) * piece] for j in range(SLICES)]

    def flat(cut):
        return jnp.concatenate([cut[0].reshape(shard, -1), cut[1].reshape(shard, -1)], 1)

    own_units = [flat(cut) for cut in side_units(side)]
    sent_units = [links.swap_side(flat(cut)) for cut in side_units(1 - side)]
    out_full = links.gather_dp(after(w_out.astype(BF16), qkv_full))
    down_low = w_down.astype(BF16)
    gate_up_full, down_full = [], []
    for j in range(SLICES):
        mine, theirs = own_units[j], sent_units[j]
        rows_pair = jnp.where(
            side == 0, jnp.concatenate([mine, theirs], 0), jnp.concatenate([theirs, mine], 0)
        )
        gate_up_full.append(links.gather_line(after(rows_pair, out_full)))
        down_full.append(links.gather_line(after(down_low[j * piece : (j + 1) * piece], out_full)))

    grad_own = links.to_slots(cotangent)
    quarter = grad_own.shape[0] // 4
    cut = lambda v, k: v[k * quarter : (k + 1) * quarter]
    grad_side = links.swap_side(jnp.concatenate([cut(grad_own, 0), cut(grad_own, 2)], 0))
    grad_near = links.swap_mp(grad_side, 1)
    grad_rows = jnp.concatenate(
        [grad_own, grad_side[:quarter], grad_near[:quarter], grad_side[quarter:], grad_near[quarter:]], 0
    )

    cosine, sine = rope_tables(segment_ids.shape[1])
    inputs = tokens.astype(F32)
    normed_one = (inputs * inverse_rms(inputs) * gains_full[0]).astype(BF16)
    qkv = jnp.dot(normed_one, qkv_full, preferred_element_type=F32)
    mixed, rotated, lse, peaks = attention_forward(qkv, cosine, sine, segment_ids, group, kvs)
    mixed_slots = links.to_slots(mixed)
    attended = links.sum_far(links.sum_core(jnp.dot(mixed_slots, out_full, preferred_element_type=F32)))
    inputs_own = links.own_quarter(tokens).astype(F32)
    middle = inputs_own + attended
    scale_two = inverse_rms(middle)
    normed_two = (middle * scale_two * gains_full[1]).astype(BF16)
    rows_two = links.gather_pair(normed_two)

    output_part = grad_normed_part = None
    grad_gate_up_parts, grad_down_parts = [], []
    for j in range(SLICES):
        columns = line * piece
        both = jnp.dot(rows_two, gate_up_full[j], preferred_element_type=F32)
        gate, up = both[:, :columns], both[:, columns:]
        sigmoid = jax.nn.sigmoid(gate)
        hidden = (gate * sigmoid * up).astype(BF16)
        grad_hidden = dot_nt(grad_rows, down_full[j])
        grad_gate = (grad_hidden * up * sigmoid * (1.0 + gate * (1.0 - sigmoid))).astype(BF16)
        grad_up = (grad_hidden * gate * sigmoid).astype(BF16)
        grad_both = jnp.concatenate([grad_gate, grad_up], 1)
        grad_down_parts.append(dot_tn(hidden, grad_rows).astype(BF16))
        grad_gate_up_parts.append(dot_tn(rows_two, grad_both).astype(BF16))
        back = dot_nt(grad_both, gate_up_full[j])
        grad_normed_part = back if grad_normed_part is None else grad_normed_part + back
        forth = jnp.dot(hidden, down_full[j], preferred_element_type=F32)
        output_part = forth if output_part is None else output_part + forth
    grad_normed_two = links.sum_pair(grad_normed_part)

    back_two, gain_two = norm_pull(middle, scale_two, gains_full[1], grad_normed_two)
    grad_middle = links.own_quarter(cotangent).astype(F32) + back_two
    grad_middle_slots = links.gather_mp(grad_middle.astype(BF16))
    grad_mixed = links.from_slots(dot_nt(grad_middle_slots, out_full).astype(BF16))
    grad_out_part = dot_tn(mixed_slots, grad_middle_slots).astype(BF16)

    grad_qkv = attention_backward(rotated, grad_mixed, lse, cosine, sine, segment_ids, group, kvs)
    grad_qkv_part = dot_tn(normed_one, grad_qkv).astype(BF16)
    grad_normed_one = links.sum_far(links.sum_core(dot_nt(links.to_slots(grad_qkv), qkv_full)))
    back_one, gain_one = norm_pull(inputs_own, inverse_rms(inputs_own), gains_full[0], grad_normed_one)
    input_grad = links.from_slots(links.gather_mp((grad_middle + back_one).astype(BF16))).astype(F32)

    output_own = middle + links.sum_pair(output_part)
    block_output = links.from_slots(links.gather_mp(output_own.astype(BF16)))

    gate_up_pieces, down_pieces = [], []
    for j in range(SLICES):
        gate_up_part, down_part = grad_gate_up_parts[j], grad_down_parts[j]
        pair_rows = 2 * shard
        summed = links.sum_line(
            lambda place: lax.dynamic_slice_in_dim(gate_up_part, place * pair_rows, pair_rows, 0)
        )
        mine = lax.dynamic_slice_in_dim(summed, side * shard, shard, 0)
        theirs = links.swap_side(lax.dynamic_slice_in_dim(summed, (1 - side) * shard, shard, 0).astype(BF16))
        theirs = theirs.astype(F32)
        gate_up_pieces.append(
            jnp.stack(
                [jnp.where(side == 0, mine, theirs), jnp.where(side == 0, theirs, mine)], 0
            ).reshape(2, shard, 2, line, piece)
        )
        down_pieces.append(
            links.sum_line(lambda place: lax.dynamic_slice_in_dim(down_part, place * piece, piece, 0))
        )
    grad_gate_up = jnp.transpose(jnp.stack(gate_up_pieces, 4), (2, 1, 3, 0, 4, 5)).reshape(w_gate_up.shape)
    grad_down = jnp.concatenate(down_pieces, 0)
    grad_out = links.sum_dp(grad_out_part)
    grad_query, grad_key, grad_value = untangle(links.sum_dp(grad_qkv_part))
    gain_terms = lax.psum(jnp.stack([gain_one, gain_two]), ("dp", "mp"))
    gain_width = norm_gains.shape[1]
    grad_gains = lax.dynamic_slice_in_dim(gain_terms, links.index * gain_width, gain_width, 1)

    count = segment_ids.shape[0]
    local_peak = jnp.max(peaks.reshape(count, kvs, 8, HEAD)[:, :, :group, 0], 0).reshape(heads)
    peak_vector = lax.dynamic_update_slice(
        jnp.full((HEADS,), MASKED, F32), local_peak, (links.rank * heads,)
    )
    peak_all = lax.pmax(peak_vector, ("dp", "mp"))

    reduced = (grad_query, grad_key, grad_value, grad_out, grad_gate_up, grad_down, grad_gains)
    masters = (w_query, w_key, w_value, w_out, w_gate_up, w_down, norm_gains)
    moment_list = (
        query_moments,
        key_moments,
        value_moments,
        out_moments,
        gate_up_moments,
        down_moments,
        gains_moments,
    )
    owner = (links.rank == 0).astype(F32)
    new_moments, directions, weight_sq, update_sq = [], [], [], []
    for number in range(7):
        master, grad_sum, moment = masters[number], reduced[number], moment_list[number]
        share = owner if number == 6 else 1.0
        first_moment = DECAY * moment[0] + (1.0 - DECAY) * grad_sum
        second_moment = DECAY * moment[1] + (1.0 - DECAY) * grad_sum * grad_sum
        direction = first_moment / (jnp.sqrt(second_moment) + STEP_EPS) + WEIGHT_DECAY * master
        new_moments.append(second_moment)
        directions.append(direction)
        weight_sq.append(jnp.sum(master * master) * share)
        update_sq.append(jnp.sum(direction * direction) * share)
    totals = lax.psum(jnp.stack(weight_sq + update_sq), ("dp", "mp"))
    weight_norm, update_norm = jnp.sqrt(totals[:7]), jnp.sqrt(totals[7:])
    ratio = weight_norm / (update_norm + STEP_EPS)
    stepped = [masters[number] - RATE * ratio[number] * directions[number] for number in range(7)]
    gamma = CLIP / jnp.maximum(peak_all, CLIP)
    local_gamma = lax.dynamic_slice_in_dim(gamma, links.rank * heads, heads, 0)
    query_scale = jnp.repeat(jnp.sqrt(local_gamma), HEAD)
    key_scale = jnp.repeat(jnp.sqrt(jnp.min(local_gamma.reshape(kvs, group), 1)), HEAD)
    stepped[0] = stepped[0] * query_scale[None, :]
    stepped[1] = stepped[1] * key_scale[None, :]
    copies = [value.astype(BF16) for value in stepped]
    norms = jnp.stack([weight_norm, update_norm])
    return (block_output, input_grad, *reduced, *new_moments, *stepped, *copies, norms, peak_all)


def solution(mesh):
    column = P("dp", "mp")
    row = P(("mp", "dp"), None)
    gate_up = P(None, "dp", "mp")
    gains = P(None, "dp")
    params = (column, column, column, row, gate_up, row, gains)
    moments = (
        P(None, "dp", "mp"),
        P(None, "dp", "mp"),
        P(None, "dp", "mp"),
        P(None, ("mp", "dp"), None),
        P(None, None, "dp", "mp"),
        P(None, ("mp", "dp"), None),
        P(None, None, "dp"),
    )
    tokens = P("dp", None)
    return jax.shard_map(
        functools.partial(body, mesh.shape["dp"], mesh.shape["mp"]),
        mesh=mesh,
        in_specs=(tokens, tokens, tokens, *params, *moments),
        out_specs=(tokens, tokens, *params, *params, *params, *params, P(), P()),
        check_vma=False,
    )
```

```python
import functools
import math

import jax
import jax.numpy as jnp
from jax import lax
from jax.experimental import pallas as pl
from jax.experimental.pallas import tpu as pltpu
from jax.sharding import PartitionSpec as P

HEADS = 16
HEAD = 128
BLOCK = 512
CLIP = 10
TILE = 256
SLICES = 2

NORM_EPS = 1e-05
ROPE_BASE = 1000000.0
RATE = 0.4
DECAY = 0.5
WEIGHT_DECAY = 0.01
STEP_EPS = 1e-06
MASKED = -1e30

F32 = jnp.float32
BF16 = jnp.bfloat16


def rope_tables(length):
    positions = jnp.arange(length, dtype=F32)
    frequency = ROPE_BASE ** (-(jnp.arange(HEAD // 2, dtype=F32) * 2.0) / HEAD)
    angles = positions[:, None] * frequency[None, :]
    cosine, sine = jnp.cos(angles), jnp.sin(angles)
    return jnp.concatenate([cosine, cosine], 1), jnp.concatenate([-sine, sine], 1)


def turn(values, cosine, sine):
    return values * cosine + pltpu.roll(values, HEAD // 2, 1) * sine


def allowed_mask(seg_row_ref, seg_col_ref, row_start, low, high):
    query_pos = row_start + lax.broadcasted_iota(jnp.int32, (TILE, high - low), 0)
    key_pos = low + lax.broadcasted_iota(jnp.int32, (TILE, high - low), 1)
    same = seg_col_ref[row_start : row_start + TILE, :] == seg_row_ref[0, :, low:high]
    return (key_pos <= query_pos) & same


def dot_nt(left, right):
    return lax.dot_general(left, right, (((1,), (1,)), ((), ())), preferred_element_type=F32)


def dot_nn(left, right):
    return lax.dot_general(left, right, (((1,), (0,)), ((), ())), preferred_element_type=F32)


def dot_tn(left, right):
    return lax.dot_general(left, right, (((0,), (0,)), ((), ())), preferred_element_type=F32)


def attend_forward(group, qkv_ref, cos_ref, sin_ref, seg_row_ref, seg_col_ref, out_ref, rot_ref, lse_ref, peak_ref):
    length = qkv_ref.shape[0]
    scale = 1.0 / math.sqrt(HEAD)
    for part in range(group + 1):
        columns = slice(part * HEAD, (part + 1) * HEAD)
        rot_ref[:, columns] = turn(qkv_ref[:, columns], cos_ref[...], sin_ref[...]).astype(BF16)
    value_columns = slice((group + 1) * HEAD, (group + 2) * HEAD)
    rot_ref[:, value_columns] = qkv_ref[:, value_columns].astype(BF16)
    key_columns = slice(group * HEAD, (group + 1) * HEAD)
    peak_ref[...] = jnp.full(peak_ref.shape, MASKED, F32)
    peaks = [None] * group
    for start in range(0, length, TILE):
        low, high = max(0, start - BLOCK), start + TILE
        rows = slice(start, start + TILE)
        mask = allowed_mask(seg_row_ref, seg_col_ref, start, low, high)
        keys = rot_ref[low:high, key_columns]
        values = rot_ref[low:high, value_columns]
        for head in range(group):
            columns = slice(head * HEAD, (head + 1) * HEAD)
            scores = jnp.where(mask, dot_nt(rot_ref[rows, columns], keys) * scale, MASKED)
            top = jnp.max(scores, 1, keepdims=True)
            exponent = jnp.exp(scores - top)
            total = jnp.sum(exponent, 1, keepdims=True)
            probs = (exponent * (1.0 / total)).astype(BF16)
            out_ref[rows, columns] = dot_nn(probs, values).astype(BF16)
            lse_ref[rows, columns] = jnp.broadcast_to(top + jnp.log(total), (TILE, HEAD))
            peak = jnp.max(top, 0, keepdims=True)
            peaks[head] = peak if peaks[head] is None else jnp.maximum(peaks[head], peak)
    for head in range(group):
        peak_ref[0, head : head + 1, :] = jnp.broadcast_to(peaks[head], (1, HEAD))


def attend_backward(group, rot_ref, grad_ref, lse_ref, cos_ref, sin_ref, seg_row_ref, seg_col_ref, out_ref, dk_ref, dv_ref):
    length = rot_ref.shape[0]
    scale = 1.0 / math.sqrt(HEAD)
    key_columns = slice(group * HEAD, (group + 1) * HEAD)
    value_columns = slice((group + 1) * HEAD, (group + 2) * HEAD)
    dk_ref[...] = jnp.zeros(dk_ref.shape, F32)
    dv_ref[...] = jnp.zeros(dv_ref.shape, F32)
    for start in range(0, length, TILE):
        low, high = max(0, start - BLOCK), start + TILE
        rows = slice(start, start + TILE)
        mask = allowed_mask(seg_row_ref, seg_col_ref, start, low, high)
        keys = rot_ref[low:high, key_columns]
        values = rot_ref[low:high, value_columns]
        for head in range(group):
            columns = slice(head * HEAD, (head + 1) * HEAD)
            queries = rot_ref[rows, columns]
            grads = grad_ref[rows, columns]
            scores = dot_nt(queries, keys) * scale
            probs = jnp.exp(jnp.where(mask, scores - lse_ref[rows, columns][:, :1], MASKED))
            grad_probs = dot_nt(grads, values)
            inner = jnp.sum(probs * grad_probs, 1, keepdims=True)
            grad_scores = (probs * (grad_probs - inner)).astype(BF16)
            dv_ref[low:high, :] += dot_tn(probs.astype(BF16), grads)
            dk_ref[low:high, :] += dot_tn(grad_scores, queries)
            grad_query = dot_nn(grad_scores, keys) * scale
            out_ref[rows, columns] = turn(grad_query, cos_ref[rows, :], -sin_ref[rows, :]).astype(BF16)
    out_ref[:, key_columns] = turn(dk_ref[...] * scale, cos_ref[...], -sin_ref[...]).astype(BF16)
    out_ref[:, value_columns] = dv_ref[...].astype(BF16)


def attention_specs(length, group):
    wide = pl.BlockSpec((length, (group + 2) * HEAD), lambda seq, kv: (seq, kv))
    narrow = pl.BlockSpec((length, group * HEAD), lambda seq, kv: (seq, kv))
    table = pl.BlockSpec((length, HEAD), lambda seq, kv: (0, 0))
    seg_row = pl.BlockSpec((1, 1, length), lambda seq, kv: (seq, 0, 0))
    seg_col = pl.BlockSpec((length, 1), lambda seq, kv: (seq, 0))
    return wide, narrow, table, seg_row, seg_col


def attention_forward(qkv, cosine, sine, segments, group, kv_count):
    count, length = segments.shape
    rows = count * length
    wide, narrow, table, seg_row, seg_col = attention_specs(length, group)
    return pl.pallas_call(
        functools.partial(attend_forward, group),
        grid=(count, kv_count),
        in_specs=[wide, table, table, seg_row, seg_col],
        out_specs=[
            narrow,
            wide,
            narrow,
            pl.BlockSpec((1, 8, HEAD), lambda seq, kv: (seq * kv_count + kv, 0, 0)),
        ],
        out_shape=[
            jax.ShapeDtypeStruct((rows, kv_count * group * HEAD), BF16),
            jax.ShapeDtypeStruct((rows, kv_count * (group + 2) * HEAD), BF16),
            jax.ShapeDtypeStruct((rows, kv_count * group * HEAD), F32),
            jax.ShapeDtypeStruct((count * kv_count, 8, HEAD), F32),
        ],
        compiler_params=pltpu.CompilerParams(vmem_limit_bytes=48 * 2**20),
        name="attention_forward",
    )(qkv, cosine, sine, segments.reshape(count, 1, length), segments.reshape(rows, 1))


def attention_backward(rotated, grads, lse, cosine, sine, segments, group, kv_count):
    count, length = segments.shape
    rows = count * length
    wide, narrow, table, seg_row, seg_col = attention_specs(length, group)
    return pl.pallas_call(
        functools.partial(attend_backward, group),
        grid=(count, kv_count),
        in_specs=[wide, narrow, narrow, table, table, seg_row, seg_col],
        out_specs=wide,
        out_shape=jax.ShapeDtypeStruct((rows, kv_count * (group + 2) * HEAD), BF16),
        scratch_shapes=[pltpu.VMEM((length, HEAD), F32), pltpu.VMEM((length, HEAD), F32)],
        compiler_params=pltpu.CompilerParams(vmem_limit_bytes=48 * 2**20),
        name="attention_backward",
    )(rotated, grads, lse, cosine, sine, segments.reshape(count, 1, length), segments.reshape(rows, 1))


MESH = pl.DeviceIdType.MESH
WHOLE = pl.BlockSpec(memory_space=pltpu.VMEM)
CHUNKS = 4


def greet(partners):
    barrier = pltpu.get_barrier_semaphore()
    for partner in partners:
        pl.semaphore_signal(barrier, inc=1, device_id=partner, device_id_type=MESH)
    pl.semaphore_wait(barrier, len(partners))


def sender(send_sems, recv_sems, log):
    def copy(kind, chunk, source, target, device):
        made = pltpu.make_async_remote_copy(
            src_ref=source,
            dst_ref=target,
            send_sem=send_sems.at[kind, chunk],
            recv_sem=recv_sems.at[kind, chunk],
            device_id=device,
            device_id_type=MESH,
        )
        log.append(made)
        return made

    return copy


def partners_of():
    rank, index = lax.axis_index("mp"), lax.axis_index("dp")
    return {"mp": rank ^ 1}, {"mp": rank ^ 2}, {"dp": index ^ 1}


def spread_forward(part_ref, tokens_ref, gain_ref, rows_ref, middle_ref, near_ref, out_ref, far_ref, send_sems, recv_sems):
    core, far, pair = partners_of()
    quarter, _ = tokens_ref.shape
    size = quarter // CHUNKS
    at = lambda slot, i: pl.ds(slot * quarter + i * size, size)
    greet([core, far, pair])
    log = []
    copy = sender(send_sems, recv_sems, log)
    near = {}
    for i in range(CHUNKS):
        for k in range(2):
            near[k, i] = copy(k, i, part_ref.at[at(2 * k + 1, i)], near_ref.at[at(k, i)], core)
            near[k, i].start()
    sums = {}
    for i in range(CHUNKS):
        near[1, i].wait_recv()
        total = part_ref[at(2, i), :].astype(F32) + near_ref[at(1, i), :].astype(F32)
        out_ref[at(0, i), :] = total.astype(BF16)
        sums[i] = copy(2, i, out_ref.at[at(0, i)], far_ref.at[at(0, i)], far)
        sums[i].start()
    moves = {}
    for i in range(CHUNKS + 2):
        if i < CHUNKS:
            near[0, i].wait_recv()
            sums[i].wait_recv()
            middle = tokens_ref[at(0, i), :].astype(F32) + (
                part_ref[at(0, i), :].astype(F32)
                + near_ref[at(0, i), :].astype(F32)
                + far_ref[at(0, i), :].astype(F32)
            )
            middle_ref[at(0, i), :] = middle
            rows_ref[at(0, i), :] = (middle * inverse_rms(middle) * gain_ref[0:1, :]).astype(BF16)
            own = rows_ref.at[at(0, i)]
            for kind, slot, device in ((3, 2, far), (4, 4, pair), (6, 1, core)):
                moves[kind, i] = copy(kind, i, own, rows_ref.at[at(slot, i)], device)
                moves[kind, i].start()
        j = i - 1
        if 0 <= j < CHUNKS:
            moves[3, j].wait_recv()
            for kind, slot, device in ((5, 6, pair), (7, 3, core)):
                moves[kind, j] = copy(kind, j, rows_ref.at[at(2, j)], rows_ref.at[at(slot, j)], device)
                moves[kind, j].start()
            moves[4, j].wait_recv()
            moves[8, j] = copy(8, j, rows_ref.at[at(4, j)], rows_ref.at[at(5, j)], core)
            moves[8, j].start()
        j = i - 2
        if 0 <= j < CHUNKS:
            moves[5, j].wait_recv()
            moves[9, j] = copy(9, j, rows_ref.at[at(6, j)], rows_ref.at[at(7, j)], core)
            moves[9, j].start()
    for i in range(CHUNKS):
        for kind in (6, 7, 8, 9):
            moves[kind, i].wait_recv()
    for made in log:
        made.wait_send()


def call_spread_forward(part, tokens_own, gain):
    quarter, width = tokens_own.shape
    return pl.pallas_call(
        spread_forward,
        in_specs=[WHOLE] * 3,
        out_specs=[WHOLE] * 2,
        out_shape=[
            jax.ShapeDtypeStruct((8 * quarter, width), BF16),
            jax.ShapeDtypeStruct((quarter, width), F32),
        ],
        scratch_shapes=[
            pltpu.VMEM((2 * quarter, width), BF16),
            pltpu.VMEM((quarter, width), BF16),
            pltpu.VMEM((quarter, width), BF16),
            pltpu.SemaphoreType.DMA((10, CHUNKS)),
            pltpu.SemaphoreType.DMA((10, CHUNKS)),
        ],
        compiler_params=pltpu.CompilerParams(
            collective_id=1, has_side_effects=True, vmem_limit_bytes=50 * 2**20
        ),
        name="spread_forward",
    )(part, tokens_own, gain)


def pull_chunk(values, scale_gain, grad):
    scale = inverse_rms(values)
    turned = grad * scale_gain
    inner = jnp.mean(turned * values, -1, keepdims=True)
    return scale * turned - (scale * scale * scale) * values * inner, grad * values * scale


def spread_backward(part_ref, middle_ref, grad_ref, gain_ref, rows_ref, total_ref, gain_out_ref, near_ref, side_out_ref, side_in_ref, far_out_ref, far_in_ref, send_sems, recv_sems):
    core, far, pair = partners_of()
    quarter, width = middle_ref.shape
    size = quarter // CHUNKS
    at = lambda slot, i: pl.ds(slot * quarter + i * size, size)
    greet([core, far, pair])
    log = []
    copy = sender(send_sems, recv_sems, log)
    near, side, sums, moves = {}, {}, {}, {}
    for i in range(CHUNKS):
        for k in (2, 3, 0, 1):
            near[k, i] = copy(k, i, part_ref.at[at(2 * k + 1, i)], near_ref.at[at(k, i)], core)
            near[k, i].start()

    def pairs(k, i):
        return part_ref[at(2 * k, i), :].astype(F32) + near_ref[at(k, i), :].astype(F32)

    for i in range(CHUNKS):
        for k in (1, 0):
            near[2 + k, i].wait_recv()
            side_out_ref[at(k, i), :] = pairs(2 + k, i).astype(BF16)
            side[k, i] = copy(4 + k, i, side_out_ref.at[at(k, i)], side_in_ref.at[at(k, i)], pair)
            side[k, i].start()
    gain_sum = jnp.zeros((1, width), F32)
    for i in range(CHUNKS + 2):
        if i < CHUNKS:
            near[1, i].wait_recv()
            side[1, i].wait_recv()
            far_out_ref[at(0, i), :] = (pairs(1, i) + side_in_ref[at(1, i), :].astype(F32)).astype(BF16)
            sums[i] = copy(6, i, far_out_ref.at[at(0, i)], far_in_ref.at[at(0, i)], far)
            sums[i].start()
        j = i - 1
        if 0 <= j < CHUNKS:
            near[0, j].wait_recv()
            side[0, j].wait_recv()
            sums[j].wait_recv()
            grad = pairs(0, j) + side_in_ref[at(0, j), :].astype(F32) + far_in_ref[at(0, j), :].astype(F32)
            back, gain_part = pull_chunk(middle_ref[at(0, j), :], gain_ref[0:1, :], grad)
            gain_sum = gain_sum + jnp.sum(gain_part, 0, keepdims=True)
            total = grad_ref[at(0, j), :].astype(F32) + back
            total_ref[at(0, j), :] = total
            rows_ref[at(0, j), :] = total.astype(BF16)
            own = rows_ref.at[at(0, j)]
            for kind, slot, device in ((7, 2, far), (8, 1, core)):
                moves[kind, j] = copy(kind, j, own, rows_ref.at[at(slot, j)], device)
                moves[kind, j].start()
        j = i - 2
        if 0 <= j < CHUNKS:
            moves[7, j].wait_recv()
            moves[9, j] = copy(9, j, rows_ref.at[at(2, j)], rows_ref.at[at(3, j)], core)
            moves[9, j].start()
    gain_out_ref[...] = jnp.broadcast_to(gain_sum, gain_out_ref.shape)
    for i in range(CHUNKS):
        for kind in (8, 9):
            moves[kind, i].wait_recv()
    for made in log:
        made.wait_send()


def call_spread_backward(part, middle, grad_own, gain):
    quarter, width = middle.shape
    return pl.pallas_call(
        spread_backward,
        in_specs=[WHOLE] * 4,
        out_specs=[WHOLE] * 3,
        out_shape=[
            jax.ShapeDtypeStruct((4 * quarter, width), BF16),
            jax.ShapeDtypeStruct((quarter, width), F32),
            jax.ShapeDtypeStruct((8, width), F32),
        ],
        scratch_shapes=[
            pltpu.VMEM((4 * quarter, width), BF16),
            pltpu.VMEM((2 * quarter, width), BF16),
            pltpu.VMEM((2 * quarter, width), BF16),
            pltpu.VMEM((quarter, width), BF16),
            pltpu.VMEM((quarter, width), BF16),
            pltpu.SemaphoreType.DMA((10, CHUNKS)),
            pltpu.SemaphoreType.DMA((10, CHUNKS)),
        ],
        compiler_params=pltpu.CompilerParams(
            collective_id=2, has_side_effects=True, vmem_limit_bytes=56 * 2**20
        ),
        name="spread_backward",
    )(part, middle, grad_own, gain)


def finish(line, part_ref, tokens_ref, total_ref, gain_ref, grads_ref, rows_ref, gain_out_ref, owned_ref, near_ref, far_out_ref, far_in_ref, side_in_ref, up_out_ref, up_in_ref, down_out_ref, down_in_ref, send_sems, recv_sems, side_send, side_recv, line_send, line_recv):
    core, far, pair = partners_of()
    index = lax.axis_index("dp")
    place, side = index // 2, index % 2
    above, below = {"dp": index + 2}, {"dp": index - 2}
    quarter, width = tokens_ref.shape
    size = quarter // CHUNKS
    shard = owned_ref.shape[0]
    last = line - 1
    at = lambda slot, i: pl.ds(slot * quarter + i * size, size)
    block = lambda where, which: pl.ds((where * 2 + which) * shard, shard)

    barrier = pltpu.get_barrier_semaphore()
    for partner in (core, far, pair):
        pl.semaphore_signal(barrier, inc=1, device_id=partner, device_id_type=MESH)

    @pl.when(place < last)
    def _():
        pl.semaphore_signal(barrier, inc=1, device_id=above, device_id_type=MESH)

    @pl.when(place > 0)
    def _():
        pl.semaphore_signal(barrier, inc=1, device_id=below, device_id_type=MESH)

    pl.semaphore_wait(barrier, 3 + (place < last).astype(jnp.int32) + (place > 0).astype(jnp.int32))

    log = []
    copy = sender(send_sems, recv_sems, log)
    near, sums, moves = {}, {}, {}
    for i in range(CHUNKS):
        for k in (1, 0):
            near[k, i] = copy(k, i, part_ref.at[at(2 * k + 1, i)], near_ref.at[at(k, i)], core)
            near[k, i].start()

    def side_copy(where):
        return pltpu.make_async_remote_copy(
            src_ref=grads_ref.at[block(where, 1 - side)],
            dst_ref=side_in_ref.at[where],
            send_sem=side_send.at[where],
            recv_sem=side_recv.at[where],
            device_id=pair,
            device_id_type=MESH,
        )

    def line_copy(upward, step):
        out_ref, in_ref = (up_out_ref, up_in_ref) if upward else (down_out_ref, down_in_ref)
        way = 0 if upward else 1
        return pltpu.make_async_remote_copy(
            src_ref=out_ref.at[step - 1],
            dst_ref=in_ref.at[step - 1],
            send_sem=line_send.at[way, step - 1],
            recv_sem=line_recv.at[way, step - 1],
            device_id=above if upward else below,
            device_id_type=MESH,
        )

    for step in range(last, 0, -1):

        @pl.when(place + step <= last)
        def _(step=step):
            side_copy(place + step).start()

        @pl.when(place - step >= 0)
        def _(step=step):
            side_copy(place - step).start()

    side_copy(place).start()

    for i in range(CHUNKS):
        near[1, i].wait_recv()
        summed = part_ref[at(2, i), :].astype(F32) + near_ref[at(1, i), :].astype(F32)
        far_out_ref[at(0, i), :] = summed.astype(BF16)
        sums[i] = copy(2, i, far_out_ref.at[at(0, i)], far_in_ref.at[at(0, i)], far)
        sums[i].start()

    def term(where):
        return grads_ref[block(where, side), :].astype(F32) + side_in_ref[where].astype(F32)

    def line_step(step):
        @pl.when(place + step <= last)
        def _():
            side_copy(place + step).wait_recv()
            value = term(place + step)

            up_out_ref[step - 1] = value.astype(BF16)
            if step < last:

                @pl.when(place > 0)
                def _():
                    line_copy(True, step + 1).wait_recv()
                    up_out_ref[step - 1] = (value + up_in_ref[step].astype(F32)).astype(BF16)

            line_copy(True, step).start()

        @pl.when(place - step >= 0)
        def _():
            side_copy(place - step).wait_recv()
            value = term(place - step)

            down_out_ref[step - 1] = value.astype(BF16)
            if step < last:

                @pl.when(place < last)
                def _():
                    line_copy(False, step + 1).wait_recv()
                    down_out_ref[step - 1] = (value + down_in_ref[step].astype(F32)).astype(BF16)

            line_copy(False, step).start()

    gain_sum = jnp.zeros((1, width), F32)
    steps = list(range(last, 0, -1))
    for i in range(CHUNKS + 1):
        if i < CHUNKS:
            near[0, i].wait_recv()
            sums[i].wait_recv()
            grad = (
                part_ref[at(0, i), :].astype(F32)
                + near_ref[at(0, i), :].astype(F32)
                + far_in_ref[at(0, i), :].astype(F32)
            )
            back, gain_part = pull_chunk(tokens_ref[at(0, i), :].astype(F32), gain_ref[0:1, :], grad)
            gain_sum = gain_sum + jnp.sum(gain_part, 0, keepdims=True)
            rows_ref[at(0, i), :] = (total_ref[at(0, i), :] + back).astype(BF16)
            own = rows_ref.at[at(0, i)]
            for kind, slot, device in ((3, 2, far), (4, 1, core)):
                moves[kind, i] = copy(kind, i, own, rows_ref.at[at(slot, i)], device)
                moves[kind, i].start()
        if steps:
            line_step(steps.pop(0))
        j = i - 1
        if 0 <= j < CHUNKS:
            moves[3, j].wait_recv()
            moves[5, j] = copy(5, j, rows_ref.at[at(2, j)], rows_ref.at[at(3, j)], core)
            moves[5, j].start()
    while steps:
        line_step(steps.pop(0))
    gain_out_ref[...] = jnp.broadcast_to(gain_sum, gain_out_ref.shape)

    side_copy(place).wait_recv()
    owned_ref[...] = term(place)

    @pl.when(place > 0)
    def _():
        line_copy(True, 1).wait_recv()
        owned_ref[...] += up_in_ref[0].astype(F32)

    @pl.when(place < last)
    def _():
        line_copy(False, 1).wait_recv()
        owned_ref[...] += down_in_ref[0].astype(F32)

    for i in range(CHUNKS):
        for kind in (4, 5):
            moves[kind, i].wait_recv()
    for made in log:
        made.wait_send()
    for where in range(line):
        side_copy(where).wait_send()
    for step in range(last, 0, -1):

        @pl.when(place + step <= last)
        def _(step=step):
            line_copy(True, step).wait_send()

        @pl.when(place - step >= 0)
        def _(step=step):
            line_copy(False, step).wait_send()


def call_finish(dp_size, part, tokens_own, total, gain, grads):
    quarter, width = tokens_own.shape
    line = dp_size // 2
    shard, columns = grads.shape[0] // dp_size, grads.shape[1]
    hops = pltpu.VMEM((line - 1, shard, columns), BF16)
    return pl.pallas_call(
        functools.partial(finish, line),
        in_specs=[WHOLE] * 5,
        out_specs=[WHOLE] * 3,
        out_shape=[
            jax.ShapeDtypeStruct((4 * quarter, width), BF16),
            jax.ShapeDtypeStruct((8, width), F32),
            jax.ShapeDtypeStruct((shard, columns), F32),
        ],
        scratch_shapes=[
            pltpu.VMEM((2 * quarter, width), BF16),
            pltpu.VMEM((quarter, width), BF16),
            pltpu.VMEM((quarter, width), BF16),
            pltpu.VMEM((line, shard, columns), BF16),
            hops,
            hops,
            hops,
            hops,
            pltpu.SemaphoreType.DMA((6, CHUNKS)),
            pltpu.SemaphoreType.DMA((6, CHUNKS)),
            pltpu.SemaphoreType.DMA((line,)),
            pltpu.SemaphoreType.DMA((line,)),
            pltpu.SemaphoreType.DMA((2, line)),
            pltpu.SemaphoreType.DMA((2, line)),
        ],
        compiler_params=pltpu.CompilerParams(
            collective_id=3, has_side_effects=True, vmem_limit_bytes=50 * 2**20
        ),
        name="finish",
    )(part, tokens_own, total, gain, grads)


def gather_weights(line, own_ref, gains_ref, full_ref, gains_full_ref, local_sems, side_send, side_recv, line_send, line_recv):
    index = lax.axis_index("dp")
    place, side = index // 2, index % 2
    pair, above, below = {"dp": index ^ 1}, {"dp": index + 2}, {"dp": index - 2}
    last = line - 1
    shard = own_ref.shape[0]
    block = lambda where, which: pl.ds((where * 2 + which) * shard, shard)

    barrier = pltpu.get_barrier_semaphore()
    pl.semaphore_signal(barrier, inc=1, device_id=pair, device_id_type=MESH)

    @pl.when(place < last)
    def _():
        pl.semaphore_signal(barrier, inc=1, device_id=above, device_id_type=MESH)

    @pl.when(place > 0)
    def _():
        pl.semaphore_signal(barrier, inc=1, device_id=below, device_id_type=MESH)

    pl.semaphore_wait(barrier, 1 + (place < last).astype(jnp.int32) + (place > 0).astype(jnp.int32))

    def views(which, where):
        if which == 0:
            return full_ref.at[block(where, side)]
        return gains_full_ref.at[where * 2 + side]

    def source(which, where, first):
        if first:
            return own_ref if which == 0 else gains_ref
        return views(which, where)

    def line_copy(which, upward, where, first=False):
        way = 0 if upward else 1
        return pltpu.make_async_remote_copy(
            src_ref=source(which, where, first),
            dst_ref=views(which, where),
            send_sem=line_send.at[which, way, where],
            recv_sem=line_recv.at[which, way, where],
            device_id=above if upward else below,
            device_id_type=MESH,
        )

    def side_copy(which, where, first=False):
        return pltpu.make_async_remote_copy(
            src_ref=source(which, where, first),
            dst_ref=views(which, where),
            send_sem=side_send.at[which, where],
            recv_sem=side_recv.at[which, where],
            device_id=pair,
            device_id_type=MESH,
        )

    def side_arrival(which, where):
        target = full_ref.at[block(where, 1 - side)] if which == 0 else gains_full_ref.at[where * 2 + 1 - side]
        return pltpu.make_async_remote_copy(
            src_ref=target,
            dst_ref=target,
            send_sem=side_send.at[which, where],
            recv_sem=side_recv.at[which, where],
            device_id=pair,
            device_id_type=MESH,
        )

    @pl.when(place < last)
    def _():
        for which in (0, 1):
            line_copy(which, True, place, True).start()

    @pl.when(place > 0)
    def _():
        for which in (0, 1):
            line_copy(which, False, place, True).start()

    for which in (0, 1):
        side_copy(which, place, True).start()
    here = [pltpu.make_async_copy(source(w, place, True), views(w, place), local_sems.at[w]) for w in (0, 1)]
    for made in here:
        made.start()

    for step in range(1, line):

        @pl.when(place - step >= 0)
        def _(step=step):
            where = place - step
            for which in (0, 1):
                line_copy(which, True, where).wait_recv()

                @pl.when(place < last)
                def _(which=which):
                    line_copy(which, True, where).start()

                side_copy(which, where).start()

        @pl.when(place + step <= last)
        def _(step=step):
            where = place + step
            for which in (0, 1):
                line_copy(which, False, where).wait_recv()

                @pl.when(place > 0)
                def _(which=which):
                    line_copy(which, False, where).start()

                side_copy(which, where).start()

    for made in here:
        made.wait()
    for where in range(line):
        for which in (0, 1):
            side_arrival(which, where).wait_recv()
            side_copy(which, where).wait_send()

            @pl.when((where <= place) & (place < last))
            def _(which=which, where=where):
                line_copy(which, True, where).wait_send()

            @pl.when((where >= place) & (place > 0))
            def _(which=which, where=where):
                line_copy(which, False, where).wait_send()


def call_gather_weights(dp_size, own, gains):
    line = dp_size // 2
    hbm = pl.BlockSpec(memory_space=pl.ANY)
    return pl.pallas_call(
        functools.partial(gather_weights, line),
        in_specs=[hbm] * 2,
        out_specs=[hbm] * 2,
        out_shape=[
            jax.ShapeDtypeStruct((dp_size * own.shape[0], own.shape[1]), own.dtype),
            jax.ShapeDtypeStruct((dp_size, *gains.shape), gains.dtype),
        ],
        scratch_shapes=[
            pltpu.SemaphoreType.DMA((2,)),
            pltpu.SemaphoreType.DMA((2, line)),
            pltpu.SemaphoreType.DMA((2, line)),
            pltpu.SemaphoreType.DMA((2, 2, line)),
            pltpu.SemaphoreType.DMA((2, 2, line)),
        ],
        compiler_params=pltpu.CompilerParams(collective_id=4, has_side_effects=True),
        name="gather_weights",
    )(own, gains)


def combine_all(line, sum_rows, value_ref, out_ref, inbox_ref, outbox_ref, send_sems, recv_sems):
    index = lax.axis_index("dp")
    partners = list(partners_of())
    step = 1
    while step < line:
        partners.append({"dp": index ^ (2 * step)})
        step *= 2
    greet(partners)
    adds = lax.broadcasted_iota(jnp.int32, value_ref.shape, 0) < sum_rows
    value = value_ref[...]
    for number, partner in enumerate(partners):
        outbox_ref[number] = value
        made = pltpu.make_async_remote_copy(
            src_ref=outbox_ref.at[number],
            dst_ref=inbox_ref.at[number],
            send_sem=send_sems.at[number],
            recv_sem=recv_sems.at[number],
            device_id=partner,
            device_id_type=MESH,
        )
        made.start()
        made.wait()
        other = inbox_ref[number]
        value = jnp.where(adds, value + other, jnp.maximum(value, other))
    out_ref[...] = value


def call_combine_all(dp_size, value, sum_rows, collective_id):
    line = dp_size // 2
    rounds = 3 + max(0, (line - 1).bit_length())
    return pl.pallas_call(
        functools.partial(combine_all, line, sum_rows),
        in_specs=[WHOLE],
        out_specs=WHOLE,
        out_shape=jax.ShapeDtypeStruct(value.shape, F32),
        scratch_shapes=[
            pltpu.VMEM((rounds, *value.shape), F32),
            pltpu.VMEM((rounds, *value.shape), F32),
            pltpu.SemaphoreType.DMA((rounds,)),
            pltpu.SemaphoreType.DMA((rounds,)),
        ],
        compiler_params=pltpu.CompilerParams(collective_id=collective_id, has_side_effects=True),
        name="combine_all",
    )(value)


class Links:
    def __init__(self, dp_size, mp_size):
        self.dp, self.mp, self.line = dp_size, mp_size, dp_size // 2
        self.index = lax.axis_index("dp")
        self.place, self.side, self.rank = self.index // 2, self.index % 2, lax.axis_index("mp")
        self.lines = [[place * 2 + side for place in range(self.line)] for side in range(2)]

    def swap_mp(self, value, bit):
        return lax.ppermute(value, "mp", [(i, i ^ bit) for i in range(self.mp)])

    def swap_side(self, value):
        return lax.ppermute(value, "dp", [(i, i ^ 1) for i in range(self.dp)])

    def gather_line(self, own):
        return lax.all_gather(own, "dp", axis=0, tiled=True, axis_index_groups=self.lines)

    def sum_line(self, parts):
        return lax.psum_scatter(parts, "dp", scatter_dimension=0, tiled=True, axis_index_groups=self.lines)


    def to_slots(self, values):
        rows = values.shape[0] // self.mp
        return jnp.concatenate(
            [lax.dynamic_slice_in_dim(values, (self.rank ^ k) * rows, rows, 0) for k in range(self.mp)], 0
        )

    def from_slots(self, values):
        rows = values.shape[0] // self.mp
        cuts = [values[k * rows : (k + 1) * rows] for k in range(self.mp)]
        odd = (self.rank & 1) == 1
        high = (self.rank & 2) == 2
        cuts = [jnp.where(odd, cuts[k ^ 1], cuts[k]) for k in range(self.mp)]
        cuts = [jnp.where(high, cuts[k ^ 2], cuts[k]) for k in range(self.mp)]
        return jnp.concatenate(cuts, 0)

    def own_quarter(self, values):
        rows = values.shape[0] // self.mp
        return lax.dynamic_slice_in_dim(values, self.rank * rows, rows, 0)

    def gather_mp(self, quarter):
        rows = quarter.shape[0]
        pair = jnp.concatenate([quarter, self.swap_mp(quarter, 2)], 0)
        near = self.swap_mp(pair, 1)
        return jnp.concatenate([pair[:rows], near[:rows], pair[rows:], near[rows:]], 0)

    def sum_pair(self, slots):
        rows = slots.shape[0] // 8
        cut = lambda v, k: v[k * rows : (k + 1) * rows]
        picked = lambda ks: jnp.concatenate([cut(slots, k) for k in ks], 0)
        near = self.swap_mp(picked((1, 3, 5, 7)).astype(BF16), 1)
        mine = (picked((0, 2, 4, 6)).astype(F32) + near.astype(F32)).astype(BF16)
        mine = mine[: 2 * rows].astype(F32) + self.swap_side(mine[2 * rows :]).astype(F32)
        return mine[:rows] + self.swap_mp(mine[rows:].astype(BF16), 2).astype(F32)


def inverse_rms(values):
    return lax.rsqrt(jnp.mean(values * values, -1, keepdims=True) + NORM_EPS)


def body(
    dp_size,
    mp_size,
    tokens,
    cotangent,
    segment_ids,
    w_query,
    w_key,
    w_value,
    w_out,
    w_gate_up,
    w_down,
    norm_gains,
    query_moments,
    key_moments,
    value_moments,
    out_moments,
    gate_up_moments,
    down_moments,
    gains_moments,
):
    links = Links(dp_size, mp_size)
    line, side = links.line, links.side
    heads = w_query.shape[1] // HEAD
    kvs = w_key.shape[1] // HEAD
    group = heads // kvs
    width = tokens.shape[1]
    shard = w_query.shape[0]
    units = w_gate_up.shape[2]
    block = units // (line * 2)
    piece = block // SLICES

    def interleave(query, key, value):
        parts = []
        for kv in range(kvs):
            parts.append(query[..., kv * group * HEAD : (kv + 1) * group * HEAD])
            parts.append(key[..., kv * HEAD : (kv + 1) * HEAD])
            parts.append(value[..., kv * HEAD : (kv + 1) * HEAD])
        return jnp.concatenate(parts, -1)

    def untangle(values):
        step = (group + 2) * HEAD
        cut = lambda low, high: jnp.concatenate(
            [values[..., kv * step + low * HEAD : kv * step + high * HEAD] for kv in range(kvs)], -1
        )
        return cut(0, group), cut(group, group + 1), cut(group + 1, group + 2)

    by_side = w_gate_up.reshape(2, shard, line, 2, block)

    def side_units(which):
        cut = lax.dynamic_index_in_dim(by_side, which, 3, keepdims=False).astype(BF16)
        return [cut[..., j * piece : (j + 1) * piece] for j in range(SLICES)]

    def flat(cut):
        return jnp.concatenate([cut[0].reshape(shard, -1), cut[1].reshape(shard, -1)], 1)

    own_units = [flat(cut) for cut in side_units(side)]
    sent_units = [links.swap_side(flat(cut)) for cut in side_units(1 - side)]
    out_full = lax.all_gather(w_out.astype(BF16), "dp", axis=0, tiled=True)
    down_low = w_down.astype(BF16)
    gate_up_full, down_full = [], []
    for j in range(SLICES):
        mine, theirs = own_units[j], sent_units[j]
        rows_pair = jnp.where(
            side == 0, jnp.concatenate([mine, theirs], 0), jnp.concatenate([theirs, mine], 0)
        )
        gate_up_full.append(links.gather_line(rows_pair))
        down_full.append(links.gather_line(down_low[j * piece : (j + 1) * piece]))
    gains_low = norm_gains.astype(BF16).astype(F32)
    gains_rows = jnp.concatenate([gains_low, jnp.zeros((6, gains_low.shape[1]), F32)], 0)
    qkv_full, gains_shards = call_gather_weights(
        dp_size, interleave(w_query, w_key, w_value).astype(BF16), gains_rows
    )
    gains_full = jnp.transpose(gains_shards, (1, 0, 2)).reshape(8, width)

    grad_own = links.to_slots(cotangent)
    quarter = grad_own.shape[0] // 4
    cut = lambda v, k: v[k * quarter : (k + 1) * quarter]
    grad_side = links.swap_side(jnp.concatenate([cut(grad_own, 0), cut(grad_own, 2)], 0))
    grad_near = links.swap_mp(grad_side, 1)
    grad_rows = jnp.concatenate(
        [grad_own, grad_side[:quarter], grad_near[:quarter], grad_side[quarter:], grad_near[quarter:]], 0
    )

    cosine, sine = rope_tables(segment_ids.shape[1])
    inputs = tokens.astype(F32)
    normed_one = (inputs * inverse_rms(inputs) * gains_full[0]).astype(BF16)
    qkv = jnp.dot(normed_one, qkv_full, preferred_element_type=F32)
    mixed, rotated, lse, peaks = attention_forward(qkv, cosine, sine, segment_ids, group, kvs)
    mixed_slots = links.to_slots(mixed)
    tokens_own = links.own_quarter(tokens)
    rows_two, middle = call_spread_forward(
        jnp.dot(mixed_slots, out_full, preferred_element_type=F32).astype(BF16), tokens_own, gains_full[1:2]
    )

    output_part = grad_normed_part = None
    grad_gate_up_parts, grad_down_parts = [], []
    for j in range(SLICES):
        columns = line * piece
        both = jnp.dot(rows_two, gate_up_full[j], preferred_element_type=F32)
        gate, up = both[:, :columns], both[:, columns:]
        sigmoid = jax.nn.sigmoid(gate)
        hidden = (gate * sigmoid * up).astype(BF16)
        grad_hidden = dot_nt(grad_rows, down_full[j])
        grad_gate = (grad_hidden * up * sigmoid * (1.0 + gate * (1.0 - sigmoid))).astype(BF16)
        grad_up = (grad_hidden * gate * sigmoid).astype(BF16)
        grad_both = jnp.concatenate([grad_gate, grad_up], 1)
        grad_down_parts.append(dot_tn(hidden, grad_rows).astype(BF16))
        grad_gate_up_parts.append(dot_tn(rows_two, grad_both).astype(BF16))
        back = dot_nt(grad_both, gate_up_full[j])
        grad_normed_part = back if grad_normed_part is None else grad_normed_part + back
        forth = jnp.dot(hidden, down_full[j], preferred_element_type=F32)
        output_part = forth if output_part is None else output_part + forth
    grad_middle_slots, grad_middle, gain_two = call_spread_backward(
        grad_normed_part.astype(BF16), middle, links.own_quarter(cotangent), gains_full[1:2]
    )
    grad_mixed = links.from_slots(dot_nt(grad_middle_slots, out_full).astype(BF16))
    grad_out_part = dot_tn(mixed_slots, grad_middle_slots).astype(BF16)

    grad_qkv = attention_backward(rotated, grad_mixed, lse, cosine, sine, segment_ids, group, kvs)
    grad_qkv_part = dot_tn(normed_one, grad_qkv).astype(BF16)
    grad_normed_one = dot_nt(links.to_slots(grad_qkv), qkv_full).astype(BF16)
    input_slots, gain_one, grad_qkv_own = call_finish(
        dp_size, grad_normed_one, tokens_own, grad_middle, gains_full[0:1], grad_qkv_part
    )
    input_grad = links.from_slots(input_slots).astype(F32)

    output_own = middle + links.sum_pair(output_part)
    block_output = links.from_slots(links.gather_mp(output_own.astype(BF16)))

    gate_up_pieces, down_pieces = [], []
    for j in range(SLICES):
        gate_up_part, down_part = grad_gate_up_parts[j], grad_down_parts[j]
        summed = links.sum_line(gate_up_part)
        mine = lax.dynamic_slice_in_dim(summed, side * shard, shard, 0).astype(F32)
        theirs = links.swap_side(lax.dynamic_slice_in_dim(summed, (1 - side) * shard, shard, 0))
        theirs = theirs.astype(F32)
        gate_up_pieces.append(
            jnp.stack(
                [jnp.where(side == 0, mine, theirs), jnp.where(side == 0, theirs, mine)], 0
            ).reshape(2, shard, 2, line, piece)
        )
        down_pieces.append(links.sum_line(down_part).astype(F32))
    grad_gate_up = jnp.transpose(jnp.stack(gate_up_pieces, 4), (2, 1, 3, 0, 4, 5)).reshape(w_gate_up.shape)
    grad_down = jnp.concatenate(down_pieces, 0)
    grad_out = lax.psum_scatter(grad_out_part, "dp", scatter_dimension=0, tiled=True).astype(F32)
    grad_query, grad_key, grad_value = untangle(grad_qkv_own)
    gain_terms = jnp.concatenate([gain_one[:1].reshape(-1, HEAD), gain_two[:1].reshape(-1, HEAD)], 0)
    gain_terms = call_combine_all(dp_size, gain_terms, gain_terms.shape[0], 5).reshape(2, width)
    gain_width = norm_gains.shape[1]
    grad_gains = lax.dynamic_slice_in_dim(gain_terms, links.index * gain_width, gain_width, 1)

    count = segment_ids.shape[0]
    local_peak = jnp.max(peaks.reshape(count, kvs, 8, HEAD)[:, :, :group, 0], 0).reshape(heads)
    peak_vector = lax.dynamic_update_slice(
        jnp.full((HEADS,), MASKED, F32), local_peak, (links.rank * heads,)
    )

    reduced = (grad_query, grad_key, grad_value, grad_out, grad_gate_up, grad_down, grad_gains)
    masters = (w_query, w_key, w_value, w_out, w_gate_up, w_down, norm_gains)
    moment_list = (
        query_moments,
        key_moments,
        value_moments,
        out_moments,
        gate_up_moments,
        down_moments,
        gains_moments,
    )
    owner = (links.rank == 0).astype(F32)
    new_moments, directions, weight_sq, update_sq = [], [], [], []
    for number in range(7):
        master, grad_sum, moment = masters[number], reduced[number], moment_list[number]
        share = owner if number == 6 else 1.0
        first_moment = DECAY * moment[0] + (1.0 - DECAY) * grad_sum
        second_moment = DECAY * moment[1] + (1.0 - DECAY) * grad_sum * grad_sum
        direction = first_moment / (jnp.sqrt(second_moment) + STEP_EPS) + WEIGHT_DECAY * master
        new_moments.append(second_moment)
        directions.append(direction)
        weight_sq.append(jnp.sum(master * master) * share)
        update_sq.append(jnp.sum(direction * direction) * share)
    sums = jnp.stack(weight_sq + update_sq)
    pad = lambda vector, fill: jnp.pad(vector, (0, HEAD - vector.shape[0]), constant_values=fill)
    packed = jnp.concatenate(
        [jnp.broadcast_to(pad(sums, 0.0), (8, HEAD)), jnp.broadcast_to(pad(peak_vector, MASKED), (8, HEAD))], 0
    )
    packed = call_combine_all(dp_size, packed, 8, 6)
    peak_all = packed[8, :HEADS]
    weight_norm, update_norm = jnp.sqrt(packed[0, :7]), jnp.sqrt(packed[0, 7:14])
    ratio = weight_norm / (update_norm + STEP_EPS)
    stepped = [masters[number] - RATE * ratio[number] * directions[number] for number in range(7)]
    gamma = CLIP / jnp.maximum(peak_all, CLIP)
    local_gamma = lax.dynamic_slice_in_dim(gamma, links.rank * heads, heads, 0)
    query_scale = jnp.repeat(jnp.sqrt(local_gamma), HEAD)
    key_scale = jnp.repeat(jnp.sqrt(jnp.min(local_gamma.reshape(kvs, group), 1)), HEAD)
    stepped[0] = stepped[0] * query_scale[None, :]
    stepped[1] = stepped[1] * key_scale[None, :]
    copies = [value.astype(BF16) for value in stepped]
    norms = jnp.stack([weight_norm, update_norm])
    return (block_output, input_grad, *reduced, *new_moments, *stepped, *copies, norms, peak_all)


def solution(mesh):
    column = P("dp", "mp")
    row = P(("mp", "dp"), None)
    gate_up = P(None, "dp", "mp")
    gains = P(None, "dp")
    params = (column, column, column, row, gate_up, row, gains)
    moments = (
        P(None, "dp", "mp"),
        P(None, "dp", "mp"),
        P(None, "dp", "mp"),
        P(None, ("mp", "dp"), None),
        P(None, None, "dp", "mp"),
        P(None, ("mp", "dp"), None),
        P(None, None, "dp"),
    )
    tokens = P("dp", None)
    return jax.shard_map(
        functools.partial(body, mesh.shape["dp"], mesh.shape["mp"]),
        mesh=mesh,
        in_specs=(tokens, tokens, tokens, *params, *moments),
        out_specs=(tokens, tokens, *params, *params, *params, *params, P(), P()),
        check_vma=False,
    )
```

```python
import functools
import math

import jax
import jax.numpy as jnp
from jax import lax
from jax.experimental import pallas as pl
from jax.experimental.pallas import tpu as pltpu
from jax.sharding import PartitionSpec as P

HEADS = 16
HEAD = 128
BLOCK = 512
CLIP = 10
TILE = 256

NORM_EPS = 1e-05
ROPE_BASE = 1000000.0
RATE = 0.4
DECAY = 0.5
WEIGHT_DECAY = 0.01
STEP_EPS = 1e-06
MASKED = -1e30

F32 = jnp.float32
BF16 = jnp.bfloat16


def rope_tables(length):
    positions = jnp.arange(length, dtype=F32)
    frequency = ROPE_BASE ** (-(jnp.arange(HEAD // 2, dtype=F32) * 2.0) / HEAD)
    angles = positions[:, None] * frequency[None, :]
    cosine, sine = jnp.cos(angles), jnp.sin(angles)
    return jnp.concatenate([cosine, cosine], 1), jnp.concatenate([-sine, sine], 1)


def lasting(microseconds):
    return pl.CostEstimate(flops=0, bytes_accessed=int(microseconds * 3e6), transcendentals=0)


def turn(values, cosine, sine):
    return values * cosine + pltpu.roll(values, HEAD // 2, 1) * sine


def allowed_mask(seg_row_ref, seg_col_ref, row_start, low, high):
    query_pos = row_start + lax.broadcasted_iota(jnp.int32, (TILE, high - low), 0)
    key_pos = low + lax.broadcasted_iota(jnp.int32, (TILE, high - low), 1)
    same = seg_col_ref[row_start : row_start + TILE, :] == seg_row_ref[0, :, low:high]
    return (key_pos <= query_pos) & same


def dot_nt(left, right):
    return lax.dot_general(left, right, (((1,), (1,)), ((), ())), preferred_element_type=F32)


def dot_nn(left, right):
    return lax.dot_general(left, right, (((1,), (0,)), ((), ())), preferred_element_type=F32)


def dot_tn(left, right):
    return lax.dot_general(left, right, (((0,), (0,)), ((), ())), preferred_element_type=F32)


def slot_rows(rank_ref, start):
    return pl.ds(pl.multiple_of(((start // TILE) ^ rank_ref[0]) * TILE, TILE), TILE)


def attend_forward(group, rank_ref, qkv_ref, cos_ref, sin_ref, seg_row_ref, seg_col_ref, out_ref, rot_ref, lse_ref, peak_ref):
    length = qkv_ref.shape[0]
    scale = 1.0 / math.sqrt(HEAD)
    for part in range(group + 1):
        columns = slice(part * HEAD, (part + 1) * HEAD)
        rot_ref[:, columns] = turn(qkv_ref[:, columns], cos_ref[...], sin_ref[...]).astype(BF16)
    value_columns = slice((group + 1) * HEAD, (group + 2) * HEAD)
    rot_ref[:, value_columns] = qkv_ref[:, value_columns].astype(BF16)
    key_columns = slice(group * HEAD, (group + 1) * HEAD)
    peak_ref[...] = jnp.full(peak_ref.shape, MASKED, F32)
    peaks = [None] * group
    for start in range(0, length, TILE):
        low, high = max(0, start - BLOCK), start + TILE
        rows = slice(start, start + TILE)
        mask = allowed_mask(seg_row_ref, seg_col_ref, start, low, high)
        keys = rot_ref[low:high, key_columns]
        values = rot_ref[low:high, value_columns]
        for head in range(group):
            columns = slice(head * HEAD, (head + 1) * HEAD)
            scores = jnp.where(mask, dot_nt(rot_ref[rows, columns], keys) * scale, MASKED)
            top = jnp.max(scores, 1, keepdims=True)
            exponent = jnp.exp(scores - top)
            total = jnp.sum(exponent, 1, keepdims=True)
            probs = (exponent * (1.0 / total)).astype(BF16)
            out_ref[slot_rows(rank_ref, start), columns] = dot_nn(probs, values).astype(BF16)
            lse_ref[rows, columns] = jnp.broadcast_to(top + jnp.log(total), (TILE, HEAD))
            peak = jnp.max(top, 0, keepdims=True)
            peaks[head] = peak if peaks[head] is None else jnp.maximum(peaks[head], peak)
    for head in range(group):
        peak_ref[0, head : head + 1, :] = jnp.broadcast_to(peaks[head], (1, HEAD))


def attend_backward(group, rank_ref, rot_ref, grad_ref, lse_ref, cos_ref, sin_ref, seg_row_ref, seg_col_ref, out_ref, dk_ref, dv_ref):
    length = rot_ref.shape[0]
    scale = 1.0 / math.sqrt(HEAD)
    key_columns = slice(group * HEAD, (group + 1) * HEAD)
    value_columns = slice((group + 1) * HEAD, (group + 2) * HEAD)
    dk_ref[...] = jnp.zeros(dk_ref.shape, F32)
    dv_ref[...] = jnp.zeros(dv_ref.shape, F32)
    for start in range(0, length, TILE):
        low, high = max(0, start - BLOCK), start + TILE
        rows = slice(start, start + TILE)
        mask = allowed_mask(seg_row_ref, seg_col_ref, start, low, high)
        keys = rot_ref[low:high, key_columns]
        values = rot_ref[low:high, value_columns]
        for head in range(group):
            columns = slice(head * HEAD, (head + 1) * HEAD)
            queries = rot_ref[rows, columns]
            grads = grad_ref[slot_rows(rank_ref, start), columns]
            scores = dot_nt(queries, keys) * scale
            probs = jnp.exp(jnp.where(mask, scores - lse_ref[rows, columns][:, :1], MASKED))
            grad_probs = dot_nt(grads, values)
            inner = jnp.sum(probs * grad_probs, 1, keepdims=True)
            grad_scores = (probs * (grad_probs - inner)).astype(BF16)
            dv_ref[low:high, :] += dot_tn(probs.astype(BF16), grads)
            dk_ref[low:high, :] += dot_tn(grad_scores, queries)
            grad_query = dot_nn(grad_scores, keys) * scale
            turned = turn(grad_query, cos_ref[rows, :], -sin_ref[rows, :])
            out_ref[slot_rows(rank_ref, start), columns] = turned.astype(BF16)
    for start in range(0, length, TILE):
        rows = slice(start, start + TILE)
        turned = turn(dk_ref[rows, :] * scale, cos_ref[rows, :], -sin_ref[rows, :])
        out_ref[slot_rows(rank_ref, start), key_columns] = turned.astype(BF16)
        out_ref[slot_rows(rank_ref, start), value_columns] = dv_ref[rows, :].astype(BF16)


def attention_specs(length, group):
    wide = pl.BlockSpec((length, (group + 2) * HEAD), lambda kv, rank: (0, kv))
    narrow = pl.BlockSpec((length, group * HEAD), lambda kv, rank: (0, kv))
    table = pl.BlockSpec((length, HEAD), lambda kv, rank: (0, 0))
    seg_row = pl.BlockSpec((1, 1, length), lambda kv, rank: (0, 0, 0))
    seg_col = pl.BlockSpec((length, 1), lambda kv, rank: (0, 0))
    return wide, narrow, table, seg_row, seg_col


def attention_forward(rank, qkv, cosine, sine, segments, group, kv_count):
    length = segments.shape[1]
    wide, narrow, table, seg_row, seg_col = attention_specs(length, group)
    return pl.pallas_call(
        functools.partial(attend_forward, group),
        grid_spec=pltpu.PrefetchScalarGridSpec(
            num_scalar_prefetch=1,
            grid=(kv_count,),
            in_specs=[wide, table, table, seg_row, seg_col],
            out_specs=[narrow, wide, narrow, pl.BlockSpec((1, 8, HEAD), lambda kv, rank: (kv, 0, 0))],
        ),
        out_shape=[
            jax.ShapeDtypeStruct((length, kv_count * group * HEAD), BF16),
            jax.ShapeDtypeStruct((length, kv_count * (group + 2) * HEAD), BF16),
            jax.ShapeDtypeStruct((length, kv_count * group * HEAD), F32),
            jax.ShapeDtypeStruct((kv_count, 8, HEAD), F32),
        ],
        compiler_params=pltpu.CompilerParams(vmem_limit_bytes=48 * 2**20),
        cost_estimate=lasting(12),
        name="attention_forward",
    )(rank, qkv, cosine, sine, segments.reshape(1, 1, length), segments.reshape(length, 1))


def attention_backward(rank, rotated, grads, lse, cosine, sine, segments, group, kv_count):
    length = segments.shape[1]
    wide, narrow, table, seg_row, seg_col = attention_specs(length, group)
    return pl.pallas_call(
        functools.partial(attend_backward, group),
        grid_spec=pltpu.PrefetchScalarGridSpec(
            num_scalar_prefetch=1,
            grid=(kv_count,),
            in_specs=[wide, narrow, narrow, table, table, seg_row, seg_col],
            out_specs=wide,
            scratch_shapes=[pltpu.VMEM((length, HEAD), F32), pltpu.VMEM((length, HEAD), F32)],
        ),
        out_shape=jax.ShapeDtypeStruct((length, kv_count * (group + 2) * HEAD), BF16),
        compiler_params=pltpu.CompilerParams(vmem_limit_bytes=48 * 2**20),
        cost_estimate=lasting(13),
        name="attention_backward",
    )(rank, rotated, grads, lse, cosine, sine, segments.reshape(1, 1, length), segments.reshape(length, 1))


def lamb_direction(master, first, second, grad):
    first_moment = DECAY * first + (1.0 - DECAY) * grad
    second_moment = DECAY * second + (1.0 - DECAY) * grad * grad
    return second_moment, first_moment / (jnp.sqrt(second_moment) + STEP_EPS) + WEIGHT_DECAY * master


def gate_up_step(side_ref, master_ref, moment_ref, *refs):
    (gate_mine, up_mine, gate_theirs, up_theirs), (grad_ref, second_ref, direction_ref, sums_ref) = refs[:4], refs[4:]
    part, place, which = pl.program_id(0), pl.program_id(1), pl.program_id(2)
    mine = jnp.where(part == 0, gate_mine[...], up_mine[...])
    theirs = jnp.where(part == 0, gate_theirs[...], up_theirs[...])
    grad = jnp.where(which == side_ref[0], mine, theirs).astype(F32)
    second, direction = lamb_direction(master_ref[0], moment_ref[0, 0], moment_ref[1, 0], grad)
    grad_ref[0], second_ref[0], direction_ref[0] = grad, second, direction

    @pl.when((part == 0) & (place == 0) & (which == 0))
    def _():
        sums_ref[...] = jnp.zeros(sums_ref.shape, F32)

    sums_ref[...] += jnp.sum((direction * direction).reshape(-1, 8, direction.shape[1]), 0)


def call_gate_up_step(line, side, master, moments, summed, theirs):
    _, shard, units = master.shape
    block = units // (2 * line)
    whole = pl.BlockSpec((1, shard, block), lambda g, p, w, side: (g, 0, p * 2 + w))
    shape = jax.ShapeDtypeStruct(master.shape, F32)
    gate_place = lambda g, p: jnp.where(g == 0, p, line - 1)
    up_place = lambda g, p: jnp.where(g == 1, p, 0)
    return pl.pallas_call(
        gate_up_step,
        grid_spec=pltpu.PrefetchScalarGridSpec(
            num_scalar_prefetch=1,
            grid=(2, line, 2),
            in_specs=[
                whole,
                pl.BlockSpec((2, 1, shard, block), lambda g, p, w, side: (0, g, 0, p * 2 + w)),
                pl.BlockSpec((shard, block), lambda g, p, w, side: (side[0], gate_place(g, p))),
                pl.BlockSpec((shard, block), lambda g, p, w, side: (side[0], up_place(g, p))),
                pl.BlockSpec((shard, block), lambda g, p, w, side: (0, gate_place(g, p))),
                pl.BlockSpec((shard, block), lambda g, p, w, side: (0, up_place(g, p))),
            ],
            out_specs=[whole, whole, whole, pl.BlockSpec((8, block), lambda g, p, w, side: (0, 0))],
        ),
        out_shape=[shape, shape, shape, jax.ShapeDtypeStruct((8, block), F32)],
        cost_estimate=lasting(16),
        name="gate_up_step",
    )(side, master, moments, *summed, *theirs)


VMEM_ALL = pl.BlockSpec(memory_space=pltpu.VMEM)
SMALL = 5


def small_step(group, kvs, owner_ref, grad_qkv_ref, grad_out_ref, grad_gains_ref, *refs):
    masters, moments, refs = refs[:SMALL], refs[SMALL : 2 * SMALL], refs[2 * SMALL :]
    grads, seconds, directions, sums_ref = refs[:3], refs[3:8], refs[8:13], refs[13]
    step = (group + 2) * HEAD
    for kv in range(kvs):
        low = kv * step
        for ref, start, columns in ((grads[0], 0, group * HEAD), (grads[1], group * HEAD, HEAD), (grads[2], (group + 1) * HEAD, HEAD)):
            ref[:, kv * columns : (kv + 1) * columns] = grad_qkv_ref[:, low + start : low + start + columns]
    sums_ref[...] = jnp.zeros(sums_ref.shape, F32)
    for number in range(SMALL):
        grad = (grads[0], grads[1], grads[2], grad_out_ref, grad_gains_ref)[number][...]
        moment = moments[number]
        second, direction = lamb_direction(masters[number][...], moment[0], moment[1], grad)
        seconds[number][...] = second
        directions[number][...] = direction
        total = jnp.sum(jnp.sum(direction * direction, 0, keepdims=True), 1, keepdims=True)
        row = jnp.broadcast_to(total, (1, HEAD))
        sums_ref[number : number + 1, :] = row * owner_ref[...] if number == SMALL - 1 else row


def call_small_step(group, kvs, owner, grad_qkv, grad_out, grad_gains, masters, moments):
    like = lambda arrays: [jax.ShapeDtypeStruct(array.shape, F32) for array in arrays]
    return pl.pallas_call(
        functools.partial(small_step, group, kvs),
        in_specs=[VMEM_ALL] * (4 + 2 * SMALL),
        out_specs=[VMEM_ALL] * 14,
        out_shape=[*like(masters[:3]), *like(masters), *like(masters), jax.ShapeDtypeStruct((8, HEAD), F32)],
        compiler_params=pltpu.CompilerParams(vmem_limit_bytes=40 * 2**20),
        cost_estimate=lasting(6),
        name="small_step",
    )(owner, grad_qkv, grad_out, grad_gains, *masters, *moments)


def pick_lane(row, lane):
    lanes = lax.broadcasted_iota(jnp.int32, row.shape, 1)
    return jnp.sum(jnp.where(lanes == lane, row, 0.0), 1, keepdims=True)


def rate_of(packed_ref, number):
    squares = packed_ref[0:1, :]
    weight, update = jnp.sqrt(pick_lane(squares, number)), jnp.sqrt(pick_lane(squares, 7 + number))
    return RATE * (weight / (update + STEP_EPS))


def small_update(group, kvs, rank_ref, packed_ref, *refs):
    masters, directions, news, copies = (refs[k * SMALL : (k + 1) * SMALL] for k in range(4))
    gamma = CLIP / jnp.maximum(packed_ref[8:9, :], float(CLIP))
    heads = [pick_lane(gamma, rank_ref[0] * (group * kvs) + head) for head in range(group * kvs)]
    for place, number in enumerate((0, 1, 2, 3, 6)):
        rate = rate_of(packed_ref, number)
        if place > 1:
            stepped = masters[place][...] - rate * directions[place][...]
            news[place][...] = stepped
            copies[place][...] = stepped.astype(BF16)
            continue
        for head in range(group * kvs if place == 0 else kvs):
            scale = heads[head]
            if place == 1:
                scale = functools.reduce(jnp.minimum, heads[head * group : (head + 1) * group])
            columns = slice(head * HEAD, (head + 1) * HEAD)
            stepped = masters[place][:, columns] - rate * directions[place][:, columns]
            stepped = stepped * jnp.sqrt(scale)
            news[place][:, columns] = stepped
            copies[place][:, columns] = stepped.astype(BF16)


def call_small_update(group, kvs, rank, packed, masters, directions):
    like = lambda kind: [jax.ShapeDtypeStruct(array.shape, kind) for array in masters]
    return pl.pallas_call(
        functools.partial(small_update, group, kvs),
        in_specs=[pl.BlockSpec(memory_space=pltpu.SMEM), *[VMEM_ALL] * (1 + 2 * SMALL)],
        out_specs=[VMEM_ALL] * (2 * SMALL),
        out_shape=[*like(F32), *like(BF16)],
        compiler_params=pltpu.CompilerParams(vmem_limit_bytes=40 * 2**20),
        cost_estimate=lasting(5),
        name="small_update",
    )(rank, packed, *masters, *directions)


def large_update(number, packed_ref, master_ref, direction_ref, new_ref, copy_ref):
    stepped = master_ref[...] - rate_of(packed_ref, number) * direction_ref[...]
    new_ref[...] = stepped
    copy_ref[...] = stepped.astype(BF16)


def call_large_update(number, packed, master, direction):
    rows, columns = master.shape
    tile = min(rows, 128)
    blocks = pl.BlockSpec((tile, columns), lambda i: (i, 0))
    return pl.pallas_call(
        functools.partial(large_update, number),
        grid=(rows // tile,),
        in_specs=[pl.BlockSpec((16, HEAD), lambda i: (0, 0)), blocks, blocks],
        out_specs=[blocks, blocks],
        out_shape=[jax.ShapeDtypeStruct(master.shape, F32), jax.ShapeDtypeStruct(master.shape, BF16)],
        cost_estimate=lasting(4),
        name="large_update",
    )(packed, master, direction)


MESH = pl.DeviceIdType.MESH
WHOLE = pl.BlockSpec(memory_space=pltpu.VMEM)
CHUNKS = 8
AHEAD = 1


def greet(partners):
    barrier = pltpu.get_barrier_semaphore()
    for partner in partners:
        pl.semaphore_signal(barrier, inc=1, device_id=partner, device_id_type=MESH)
    pl.semaphore_wait(barrier, len(partners))


def sender(send_sems, recv_sems, log):
    def copy(kind, chunk, source, target, device):
        made = pltpu.make_async_remote_copy(
            src_ref=source,
            dst_ref=target,
            send_sem=send_sems.at[kind, chunk],
            recv_sem=recv_sems.at[kind, chunk],
            device_id=device,
            device_id_type=MESH,
        )
        log.append(made)
        return made

    return copy


def partners_of():
    rank, index = lax.axis_index("mp"), lax.axis_index("dp")
    return {"mp": rank ^ 1}, {"mp": rank ^ 2}, {"dp": index ^ 1}


class Everyone:
    def __init__(self, line, near_ref, line_ref, near_send, near_recv, line_send, line_recv):
        self.line, self.near_ref, self.line_ref = line, near_ref, line_ref
        self.near_send, self.near_recv, self.line_send, self.line_recv = near_send, near_recv, line_send, line_recv
        self.index, self.rank = lax.axis_index("dp"), lax.axis_index("mp")
        self.place, self.side = self.index // 2, self.index % 2
        self.code = self.side * 4 + self.rank

    @staticmethod
    def scratch(line, shape):
        return [
            pltpu.VMEM((8, *shape), F32),
            pltpu.VMEM((line, *shape), F32),
            pltpu.SemaphoreType.DMA((8,)),
            pltpu.SemaphoreType.DMA((8,)),
            pltpu.SemaphoreType.DMA((line,)),
            pltpu.SemaphoreType.DMA((line,)),
        ]

    def peer(self, k):
        return {"dp": self.index ^ (k // 4), "mp": self.rank ^ (k % 4)}

    def along(self, k):
        return {"dp": ((self.place + k) % self.line) * 2 + self.side}

    def partners(self):
        return [self.peer(k) for k in range(1, 8)] + [self.along(k) for k in range(1, self.line)]

    @staticmethod
    def add(left, right):
        return left + right

    def near_copy(self, k, slot):
        return pltpu.make_async_remote_copy(
            src_ref=self.near_ref.at[self.code],
            dst_ref=self.near_ref.at[slot],
            send_sem=self.near_send.at[k],
            recv_sem=self.near_recv.at[slot],
            device_id=self.peer(k),
            device_id_type=MESH,
        )

    def line_copy(self, k, slot):
        return pltpu.make_async_remote_copy(
            src_ref=self.line_ref.at[self.place],
            dst_ref=self.line_ref.at[slot],
            send_sem=self.line_send.at[k],
            recv_sem=self.line_recv.at[slot],
            device_id=self.along(k),
            device_id_type=MESH,
        )

    @staticmethod
    def total(ref, count, fold):
        value = ref[0]
        for k in range(1, count):
            value = fold(value, ref[k])
        return value

    def send_near(self):
        for k in range(1, 8):
            self.near_copy(k, self.code).start()

    def send_line(self, fold):
        for k in range(1, 8):
            self.near_copy(k, self.code ^ k).wait_recv()
        self.line_ref[self.place] = self.total(self.near_ref, 8, fold)
        for k in range(1, self.line):
            self.line_copy(k, self.place).start()

    def result(self, fold):
        for k in range(1, self.line):
            self.line_copy(k, (self.place + k) % self.line).wait_recv()
        value = self.total(self.line_ref, self.line, fold)
        for k in range(1, 8):
            self.near_copy(k, self.code).wait_send()
        for k in range(1, self.line):
            self.line_copy(k, self.place).wait_send()
        return value


def spread_forward(part_ref, tokens_ref, gain_ref, rows_ref, middle_ref, near_ref, out_ref, far_ref, send_sems, recv_sems):
    core, far, pair = partners_of()
    quarter, _ = tokens_ref.shape
    size = quarter // CHUNKS
    at = lambda slot, i: pl.ds(slot * quarter + i * size, size)
    greet([core, far, pair])
    log = []
    copy = sender(send_sems, recv_sems, log)
    near = {}
    for i in range(CHUNKS):
        for k in range(2):
            near[k, i] = copy(k, i, part_ref.at[at(2 * k + 1, i)], near_ref.at[at(k, i)], core)
            near[k, i].start()
    sums = {}

    def send_sum(i):
        near[1, i].wait_recv()
        total = part_ref[at(2, i), :].astype(F32) + near_ref[at(1, i), :].astype(F32)
        out_ref[at(0, i), :] = total.astype(BF16)
        sums[i] = copy(2, i, out_ref.at[at(0, i)], far_ref.at[at(0, i)], far)
        sums[i].start()

    for i in range(AHEAD):
        send_sum(i)
    moves = {}
    for i in range(CHUNKS + 2):
        if i + AHEAD < CHUNKS:
            send_sum(i + AHEAD)
        if i < CHUNKS:
            near[0, i].wait_recv()
            sums[i].wait_recv()
            middle = tokens_ref[at(0, i), :].astype(F32) + (
                part_ref[at(0, i), :].astype(F32)
                + near_ref[at(0, i), :].astype(F32)
                + far_ref[at(0, i), :].astype(F32)
            )
            middle_ref[at(0, i), :] = middle
            rows_ref[at(0, i), :] = (middle * inverse_rms(middle) * gain_ref[0:1, :]).astype(BF16)
            own = rows_ref.at[at(0, i)]
            for kind, slot, device in ((3, 2, far), (4, 4, pair), (6, 1, core)):
                moves[kind, i] = copy(kind, i, own, rows_ref.at[at(slot, i)], device)
                moves[kind, i].start()
        j = i - 1
        if 0 <= j < CHUNKS:
            moves[3, j].wait_recv()
            for kind, slot, device in ((5, 6, pair), (7, 3, core)):
                moves[kind, j] = copy(kind, j, rows_ref.at[at(2, j)], rows_ref.at[at(slot, j)], device)
                moves[kind, j].start()
            moves[4, j].wait_recv()
            moves[8, j] = copy(8, j, rows_ref.at[at(4, j)], rows_ref.at[at(5, j)], core)
            moves[8, j].start()
        j = i - 2
        if 0 <= j < CHUNKS:
            moves[5, j].wait_recv()
            moves[9, j] = copy(9, j, rows_ref.at[at(6, j)], rows_ref.at[at(7, j)], core)
            moves[9, j].start()
    for i in range(CHUNKS):
        for kind in (6, 7, 8, 9):
            moves[kind, i].wait_recv()
    for made in log:
        made.wait_send()


def call_spread_forward(part, tokens_own, gain):
    quarter, width = tokens_own.shape
    return pl.pallas_call(
        spread_forward,
        in_specs=[WHOLE] * 3,
        out_specs=[WHOLE] * 2,
        out_shape=[
            jax.ShapeDtypeStruct((8 * quarter, width), BF16),
            jax.ShapeDtypeStruct((quarter, width), F32),
        ],
        scratch_shapes=[
            pltpu.VMEM((2 * quarter, width), BF16),
            pltpu.VMEM((quarter, width), BF16),
            pltpu.VMEM((quarter, width), BF16),
            pltpu.SemaphoreType.DMA((10, CHUNKS)),
            pltpu.SemaphoreType.DMA((10, CHUNKS)),
        ],
        compiler_params=pltpu.CompilerParams(
            collective_id=1, has_side_effects=True, vmem_limit_bytes=50 * 2**20
        ),
        cost_estimate=lasting(64),
        name="spread_forward",
    )(part, tokens_own, gain)


def pull_chunk(values, scale_gain, grad):
    scale = inverse_rms(values)
    turned = grad * scale_gain
    inner = jnp.mean(turned * values, -1, keepdims=True)
    return scale * turned - (scale * scale * scale) * values * inner, grad * values * scale


def spread_backward(part_ref, middle_ref, grad_ref, gain_ref, rows_ref, total_ref, gain_out_ref, near_ref, side_out_ref, side_in_ref, far_out_ref, far_in_ref, send_sems, recv_sems):
    core, far, pair = partners_of()
    quarter, width = middle_ref.shape
    size = quarter // CHUNKS
    at = lambda slot, i: pl.ds(slot * quarter + i * size, size)
    greet([core, far, pair])
    log = []
    copy = sender(send_sems, recv_sems, log)
    near, side, sums, moves = {}, {}, {}, {}
    for i in range(CHUNKS):
        for k in (2, 3, 0, 1):
            near[k, i] = copy(k, i, part_ref.at[at(2 * k + 1, i)], near_ref.at[at(k, i)], core)
            near[k, i].start()

    def pairs(k, i):
        return part_ref[at(2 * k, i), :].astype(F32) + near_ref[at(k, i), :].astype(F32)

    def send_side(i):
        for k in (1, 0):
            near[2 + k, i].wait_recv()
            side_out_ref[at(k, i), :] = pairs(2 + k, i).astype(BF16)
            side[k, i] = copy(4 + k, i, side_out_ref.at[at(k, i)], side_in_ref.at[at(k, i)], pair)
            side[k, i].start()

    for i in range(AHEAD):
        send_side(i)
    gain_sum = jnp.zeros((1, width), F32)
    for i in range(CHUNKS + 2):
        if i + AHEAD < CHUNKS:
            send_side(i + AHEAD)
        if i < CHUNKS:
            near[1, i].wait_recv()
            side[1, i].wait_recv()
            far_out_ref[at(0, i), :] = (pairs(1, i) + side_in_ref[at(1, i), :].astype(F32)).astype(BF16)
            sums[i] = copy(6, i, far_out_ref.at[at(0, i)], far_in_ref.at[at(0, i)], far)
            sums[i].start()
        j = i - 1
        if 0 <= j < CHUNKS:
            near[0, j].wait_recv()
            side[0, j].wait_recv()
            sums[j].wait_recv()
            grad = pairs(0, j) + side_in_ref[at(0, j), :].astype(F32) + far_in_ref[at(0, j), :].astype(F32)
            back, gain_part = pull_chunk(middle_ref[at(0, j), :], gain_ref[0:1, :], grad)
            gain_sum = gain_sum + jnp.sum(gain_part, 0, keepdims=True)
            total = grad_ref[at(0, j), :].astype(F32) + back
            total_ref[at(0, j), :] = total
            rows_ref[at(0, j), :] = total.astype(BF16)
            own = rows_ref.at[at(0, j)]
            for kind, slot, device in ((7, 2, far), (8, 1, core)):
                moves[kind, j] = copy(kind, j, own, rows_ref.at[at(slot, j)], device)
                moves[kind, j].start()
        j = i - 2
        if 0 <= j < CHUNKS:
            moves[7, j].wait_recv()
            moves[9, j] = copy(9, j, rows_ref.at[at(2, j)], rows_ref.at[at(3, j)], core)
            moves[9, j].start()
    gain_out_ref[...] = jnp.broadcast_to(gain_sum, gain_out_ref.shape)
    for i in range(CHUNKS):
        for kind in (8, 9):
            moves[kind, i].wait_recv()
    for made in log:
        made.wait_send()


def call_spread_backward(part, middle, grad_own, gain):
    quarter, width = middle.shape
    return pl.pallas_call(
        spread_backward,
        in_specs=[WHOLE] * 4,
        out_specs=[WHOLE] * 3,
        out_shape=[
            jax.ShapeDtypeStruct((4 * quarter, width), BF16),
            jax.ShapeDtypeStruct((quarter, width), F32),
            jax.ShapeDtypeStruct((8, width), F32),
        ],
        scratch_shapes=[
            pltpu.VMEM((4 * quarter, width), BF16),
            pltpu.VMEM((2 * quarter, width), BF16),
            pltpu.VMEM((2 * quarter, width), BF16),
            pltpu.VMEM((quarter, width), BF16),
            pltpu.VMEM((quarter, width), BF16),
            pltpu.SemaphoreType.DMA((10, CHUNKS)),
            pltpu.SemaphoreType.DMA((10, CHUNKS)),
        ],
        compiler_params=pltpu.CompilerParams(
            collective_id=2, has_side_effects=True, vmem_limit_bytes=56 * 2**20
        ),
        cost_estimate=lasting(68),
        name="spread_backward",
    )(part, middle, grad_own, gain)


def finish(line, part_ref, tokens_ref, total_ref, gain_ref, *refs):
    gain_two_ref, grads_refs, refs = refs[0], refs[1:3], refs[3:]
    rows_ref, gain_out_ref, *owned_refs = refs[:4]
    near_ref, far_out_ref, far_in_ref = refs[4:7]
    side_in_refs, up_out_refs, up_in_refs, down_out_refs, down_in_refs = (refs[k : k + 2] for k in range(7, 17, 2))
    send_sems, recv_sems, side_send, side_recv, line_send, line_recv, *exchange = refs[17:]
    core, far, pair = partners_of()
    index = lax.axis_index("dp")
    place, side = index // 2, index % 2
    above, below = {"dp": index + 2}, {"dp": index - 2}
    quarter, width = tokens_ref.shape
    size = quarter // CHUNKS
    last = line - 1
    at = lambda slot, i: pl.ds(slot * quarter + i * size, size)

    def block(w, where, which):
        rows = owned_refs[w].shape[0]
        return pl.ds((where * 2 + which) * rows, rows)


    everyone = Everyone(line, *exchange)
    greet(everyone.partners())
    log = []
    copy = sender(send_sems, recv_sems, log)
    near, sums, moves = {}, {}, {}
    for i in range(CHUNKS):
        for k in (1, 0):
            near[k, i] = copy(k, i, part_ref.at[at(2 * k + 1, i)], near_ref.at[at(k, i)], core)
            near[k, i].start()

    def side_copy(w, where):
        return pltpu.make_async_remote_copy(
            src_ref=grads_refs[w].at[block(w, where, 1 - side)],
            dst_ref=side_in_refs[w].at[where],
            send_sem=side_send.at[w, where],
            recv_sem=side_recv.at[w, where],
            device_id=pair,
            device_id_type=MESH,
        )

    def line_copy(w, upward, step):
        out_ref, in_ref = (up_out_refs[w], up_in_refs[w]) if upward else (down_out_refs[w], down_in_refs[w])
        way = 0 if upward else 1
        return pltpu.make_async_remote_copy(
            src_ref=out_ref.at[step - 1],
            dst_ref=in_ref.at[step - 1],
            send_sem=line_send.at[w, way, step - 1],
            recv_sem=line_recv.at[w, way, step - 1],
            device_id=above if upward else below,
            device_id_type=MESH,
        )

    for step in range(last, 0, -1):

        @pl.when(place + step <= last)
        def _(step=step):
            for w in range(2):
                side_copy(w, place + step).start()

        @pl.when(place - step >= 0)
        def _(step=step):
            for w in range(2):
                side_copy(w, place - step).start()

    for w in range(2):
        side_copy(w, place).start()

    for i in range(CHUNKS):
        near[1, i].wait_recv()
        summed = part_ref[at(2, i), :].astype(F32) + near_ref[at(1, i), :].astype(F32)
        far_out_ref[at(0, i), :] = summed.astype(BF16)
        sums[i] = copy(2, i, far_out_ref.at[at(0, i)], far_in_ref.at[at(0, i)], far)
        sums[i].start()

    def term(w, where):
        return grads_refs[w][block(w, where, side), :].astype(F32) + side_in_refs[w][where].astype(F32)

    def line_step(step):
        for w in range(2):

            @pl.when(place + step <= last)
            def _(w=w):
                side_copy(w, place + step).wait_recv()
                value = term(w, place + step)
                up_out_refs[w][step - 1] = value.astype(BF16)
                if step < last:

                    @pl.when(place > 0)
                    def _():
                        line_copy(w, True, step + 1).wait_recv()
                        up_out_refs[w][step - 1] = (value + up_in_refs[w][step].astype(F32)).astype(BF16)

                line_copy(w, True, step).start()

            @pl.when(place - step >= 0)
            def _(w=w):
                side_copy(w, place - step).wait_recv()
                value = term(w, place - step)
                down_out_refs[w][step - 1] = value.astype(BF16)
                if step < last:

                    @pl.when(place < last)
                    def _():
                        line_copy(w, False, step + 1).wait_recv()
                        down_out_refs[w][step - 1] = (value + down_in_refs[w][step].astype(F32)).astype(BF16)

                line_copy(w, False, step).start()

    gain_sum = jnp.zeros((1, width), F32)
    steps = list(range(last, 0, -1))
    for i in range(CHUNKS + 1):
        if i < CHUNKS:
            near[0, i].wait_recv()
            sums[i].wait_recv()
            grad = (
                part_ref[at(0, i), :].astype(F32)
                + near_ref[at(0, i), :].astype(F32)
                + far_in_ref[at(0, i), :].astype(F32)
            )
            back, gain_part = pull_chunk(tokens_ref[at(0, i), :].astype(F32), gain_ref[0:1, :], grad)
            gain_sum = gain_sum + jnp.sum(gain_part, 0, keepdims=True)
            rows_ref[at(0, i), :] = (total_ref[at(0, i), :] + back).astype(BF16)
            own = rows_ref.at[at(0, i)]
            for kind, slot, device in ((3, 2, far), (4, 1, core)):
                moves[kind, i] = copy(kind, i, own, rows_ref.at[at(slot, i)], device)
                moves[kind, i].start()
        if steps:
            line_step(steps.pop(0))
        j = i - 1
        if 0 <= j < CHUNKS:
            moves[3, j].wait_recv()
            moves[5, j] = copy(5, j, rows_ref.at[at(2, j)], rows_ref.at[at(3, j)], core)
            moves[5, j].start()
    while steps:
        line_step(steps.pop(0))
    columns = gain_out_ref.shape[1]
    for r in range(4):
        cut = slice(r * columns, (r + 1) * columns)
        everyone.near_ref[everyone.code, r : r + 1, :] = gain_sum[:, cut]
        everyone.near_ref[everyone.code, r + 4 : r + 5, :] = gain_two_ref[0:1, cut]
    everyone.send_near()
    everyone.send_line(everyone.add)
    for w in range(2):
        side_copy(w, place).wait_recv()
        owned_refs[w][...] = term(w, place)

        @pl.when(place > 0)
        def _(w=w):
            line_copy(w, True, 1).wait_recv()
            owned_refs[w][...] += up_in_refs[w][0].astype(F32)

        @pl.when(place < last)
        def _(w=w):
            line_copy(w, False, 1).wait_recv()
            owned_refs[w][...] += down_in_refs[w][0].astype(F32)

    gain_out_ref[...] = everyone.result(everyone.add)
    for i in range(CHUNKS):
        for kind in (4, 5):
            moves[kind, i].wait_recv()
    for made in log:
        made.wait_send()
    for w in range(2):
        for where in range(line):
            side_copy(w, where).wait_send()
        for step in range(last, 0, -1):

            @pl.when(place + step <= last)
            def _(w=w, step=step):
                line_copy(w, True, step).wait_send()

            @pl.when(place - step >= 0)
            def _(w=w, step=step):
                line_copy(w, False, step).wait_send()


def call_finish(dp_size, part, tokens_own, total, gain, gain_two, *grads):
    quarter, width = tokens_own.shape
    line = dp_size // 2
    owned = [(grad.shape[0] // dp_size, grad.shape[1]) for grad in grads]
    stacks = lambda count: [pltpu.VMEM((count, *shape), BF16) for shape in owned]
    return pl.pallas_call(
        functools.partial(finish, line),
        in_specs=[WHOLE] * 7,
        out_specs=[WHOLE] * 4,
        out_shape=[
            jax.ShapeDtypeStruct((4 * quarter, width), BF16),
            jax.ShapeDtypeStruct((8, width // 4), F32),
            *[jax.ShapeDtypeStruct(shape, F32) for shape in owned],
        ],
        scratch_shapes=[
            pltpu.VMEM((2 * quarter, width), BF16),
            pltpu.VMEM((quarter, width), BF16),
            pltpu.VMEM((quarter, width), BF16),
            *stacks(line),
            *stacks(line - 1),
            *stacks(line - 1),
            *stacks(line - 1),
            *stacks(line - 1),
            pltpu.SemaphoreType.DMA((6, CHUNKS)),
            pltpu.SemaphoreType.DMA((6, CHUNKS)),
            pltpu.SemaphoreType.DMA((2, line)),
            pltpu.SemaphoreType.DMA((2, line)),
            pltpu.SemaphoreType.DMA((2, 2, line)),
            pltpu.SemaphoreType.DMA((2, 2, line)),
            *Everyone.scratch(line, (8, width // 4)),
        ],
        compiler_params=pltpu.CompilerParams(
            collective_id=3, has_side_effects=True, vmem_limit_bytes=56 * 2**20
        ),
        cost_estimate=lasting(85),
        name="finish",
    )(part, tokens_own, total, gain, gain_two, *grads)


def gather_weights(line, own_ref, out_ref, gains_ref, grad_ref, full_ref, out_full_ref, gains_full_ref, rows_ref, local_sems, side_send, side_recv, line_send, line_recv, rows_send, rows_recv, staged_ref):
    index = lax.axis_index("dp")
    place, side = index // 2, index % 2
    pair, above, below = {"dp": index ^ 1}, {"dp": index + 2}, {"dp": index - 2}
    rank = lax.axis_index("mp")
    core, far = {"mp": rank ^ 1}, {"mp": rank ^ 2}
    quarter = grad_ref.shape[0] // 4
    slot_of = lambda k: rows_ref.at[pl.ds(k * quarter, quarter)]
    quarter_of = lambda k: grad_ref.at[pl.ds((rank ^ k) * quarter, quarter)]
    last = line - 1
    owns, fulls = (own_ref, out_ref, gains_ref), (full_ref, out_full_ref, gains_full_ref)
    all_three = range(3)

    barrier = pltpu.get_barrier_semaphore()
    pl.semaphore_signal(barrier, inc=1, device_id=pair, device_id_type=MESH)
    pl.semaphore_signal(barrier, inc=1, device_id=core, device_id_type=MESH)
    pl.semaphore_signal(barrier, inc=1, device_id=far, device_id_type=MESH)

    @pl.when(place < last)
    def _():
        pl.semaphore_signal(barrier, inc=1, device_id=above, device_id_type=MESH)

    @pl.when(place > 0)
    def _():
        pl.semaphore_signal(barrier, inc=1, device_id=below, device_id_type=MESH)

    pl.semaphore_wait(barrier, 3 + (place < last).astype(jnp.int32) + (place > 0).astype(jnp.int32))

    def slot(which, where, side):
        rows = owns[which].shape[0]
        return fulls[which].at[pl.ds((where * 2 + side) * rows, rows)]

    def views(which, where):
        return slot(which, where, side)

    def source(which, where, first):
        return owns[which] if first else views(which, where)

    def line_copy(which, upward, where, first=False):
        way = 0 if upward else 1
        return pltpu.make_async_remote_copy(
            src_ref=source(which, where, first),
            dst_ref=views(which, where),
            send_sem=line_send.at[which, way, where],
            recv_sem=line_recv.at[which, way, where],
            device_id=above if upward else below,
            device_id_type=MESH,
        )

    def side_copy(which, where, first=False):
        return pltpu.make_async_remote_copy(
            src_ref=source(which, where, first),
            dst_ref=views(which, where),
            send_sem=side_send.at[which, where],
            recv_sem=side_recv.at[which, where],
            device_id=pair,
            device_id_type=MESH,
        )

    def side_arrival(which, where):
        target = slot(which, where, 1 - side)
        return pltpu.make_async_remote_copy(
            src_ref=target,
            dst_ref=target,
            send_sem=side_send.at[which, where],
            recv_sem=side_recv.at[which, where],
            device_id=pair,
            device_id_type=MESH,
        )

    @pl.when(place < last)
    def _():
        for which in all_three:
            line_copy(which, True, place, True).start()

    @pl.when(place > 0)
    def _():
        for which in all_three:
            line_copy(which, False, place, True).start()

    for which in all_three:
        side_copy(which, place, True).start()
    here = [pltpu.make_async_copy(source(w, place, True), views(w, place), local_sems.at[w]) for w in all_three]
    for made in here:
        made.start()
    staged_of = lambda k: staged_ref.at[pl.ds(k * quarter, quarter)]
    fetches = [pltpu.make_async_copy(quarter_of(k), staged_of(k), local_sems.at[3 + k]) for k in range(4)]
    stores = [pltpu.make_async_copy(staged_of(k), slot_of(k), local_sems.at[7 + k]) for k in range(4)]
    for made in fetches:
        made.start()

    def rows_copy(number, source, target, device):
        return pltpu.make_async_remote_copy(
            src_ref=source,
            dst_ref=target,
            send_sem=rows_send.at[number],
            recv_sem=rows_recv.at[number],
            device_id=device,
            device_id_type=MESH,
        )

    over = rows_copy(0, quarter_of(0), slot_of(4), pair)
    across = rows_copy(1, slot_of(4), slot_of(6), far)
    near = [rows_copy(2 + k, slot_of(4 + 2 * k), slot_of(5 + 2 * k), core) for k in range(2)]
    over.start()

    for step in range(1, line):

        @pl.when(place - step >= 0)
        def _(step=step):
            where = place - step
            for which in all_three:
                line_copy(which, True, where).wait_recv()

                @pl.when(place < last)
                def _(which=which):
                    line_copy(which, True, where).start()

                side_copy(which, where).start()

        @pl.when(place + step <= last)
        def _(step=step):
            where = place + step
            for which in all_three:
                line_copy(which, False, where).wait_recv()

                @pl.when(place > 0)
                def _(which=which):
                    line_copy(which, False, where).start()

                side_copy(which, where).start()

        if step == 1:
            for fetch, store in zip(fetches, stores):
                fetch.wait()
                store.start()
            over.wait_recv()
            across.start()
            near[0].start()

    across.wait_recv()
    near[1].start()
    for made in here + stores:
        made.wait()
    for where in range(line):
        for which in all_three:
            side_arrival(which, where).wait_recv()
            side_copy(which, where).wait_send()

            @pl.when((where <= place) & (place < last))
            def _(which=which, where=where):
                line_copy(which, True, where).wait_send()

            @pl.when((where >= place) & (place > 0))
            def _(which=which, where=where):
                line_copy(which, False, where).wait_send()

    for k in range(2):
        near[k].wait_recv()
        near[k].wait_send()
    over.wait_send()
    across.wait_send()


def call_gather_weights(dp_size, grads, *owns):
    line = dp_size // 2
    hbm = pl.BlockSpec(memory_space=pl.ANY)
    return pl.pallas_call(
        functools.partial(gather_weights, line),
        in_specs=[hbm] * 4,
        out_specs=[hbm] * 4,
        out_shape=[
            *[jax.ShapeDtypeStruct((dp_size * own.shape[0], own.shape[1]), own.dtype) for own in owns],
            jax.ShapeDtypeStruct((2 * grads.shape[0], grads.shape[1]), grads.dtype),
        ],
        scratch_shapes=[
            pltpu.SemaphoreType.DMA((11,)),
            pltpu.SemaphoreType.DMA((3, line)),
            pltpu.SemaphoreType.DMA((3, line)),
            pltpu.SemaphoreType.DMA((3, 2, line)),
            pltpu.SemaphoreType.DMA((3, 2, line)),
            pltpu.SemaphoreType.DMA((4,)),
            pltpu.SemaphoreType.DMA((4,)),
            pltpu.VMEM(grads.shape, grads.dtype),
        ],
        compiler_params=pltpu.CompilerParams(
            collective_id=4, has_side_effects=True, vmem_limit_bytes=16 * 2**20
        ),
        cost_estimate=lasting(120),
        name="gather_weights",
    )(*owns, grads)


def combine_all(line, early_ref, small_ref, gate_up_ref, out_ref, *exchange):
    everyone = Everyone(line, *exchange)
    greet(everyone.partners())
    lanes = lax.broadcasted_iota(jnp.int32, early_ref.shape, 1)
    adds = lax.broadcasted_iota(jnp.int32, early_ref.shape, 0) < 8
    fold = lambda left, right: jnp.where(adds, left + right, jnp.maximum(left, right))
    value = early_ref[...]
    gate_up = jnp.sum(jnp.sum(gate_up_ref[...], 0, keepdims=True), 1, keepdims=True)
    terms = [small_ref[k : k + 1, :] for k in range(SMALL)] + [jnp.broadcast_to(gate_up, (1, HEAD))]
    for term, number in zip(terms, (0, 1, 2, 3, 6, 4)):
        value = jnp.where(adds & (lanes == 7 + number), term, value)
    everyone.near_ref[everyone.code] = value
    everyone.send_near()
    everyone.send_line(fold)
    out_ref[...] = everyone.result(fold)


def call_combine_all(dp_size, early, small, gate_up):
    line = dp_size // 2
    return pl.pallas_call(
        functools.partial(combine_all, line),
        in_specs=[WHOLE] * 3,
        out_specs=WHOLE,
        out_shape=jax.ShapeDtypeStruct(early.shape, F32),
        scratch_shapes=Everyone.scratch(line, early.shape),
        compiler_params=pltpu.CompilerParams(collective_id=6, has_side_effects=True),
        cost_estimate=lasting(10),
        name="combine_all",
    )(early, small, gate_up)


class Links:
    def __init__(self, dp_size, mp_size):
        self.dp, self.mp, self.line = dp_size, mp_size, dp_size // 2
        self.index = lax.axis_index("dp")
        self.place, self.side, self.rank = self.index // 2, self.index % 2, lax.axis_index("mp")
        self.lines = [[place * 2 + side for place in range(self.line)] for side in range(2)]

    def swap_mp(self, value, bit):
        return lax.ppermute(value, "mp", [(i, i ^ bit) for i in range(self.mp)])

    def swap_side(self, value):
        return lax.ppermute(value, "dp", [(i, i ^ 1) for i in range(self.dp)])

    def gather_line(self, own):
        return lax.all_gather(own, "dp", axis=0, tiled=True, axis_index_groups=self.lines)

    def sum_line(self, parts):
        return lax.psum_scatter(parts, "dp", scatter_dimension=0, tiled=True, axis_index_groups=self.lines)


    def to_slots(self, values):
        rows = values.shape[0] // self.mp
        return jnp.concatenate(
            [lax.dynamic_slice_in_dim(values, (self.rank ^ k) * rows, rows, 0) for k in range(self.mp)], 0
        )

    def from_slots(self, values):
        rows = values.shape[0] // self.mp
        cuts = [values[k * rows : (k + 1) * rows] for k in range(self.mp)]
        odd = (self.rank & 1) == 1
        high = (self.rank & 2) == 2
        cuts = [jnp.where(odd, cuts[k ^ 1], cuts[k]) for k in range(self.mp)]
        cuts = [jnp.where(high, cuts[k ^ 2], cuts[k]) for k in range(self.mp)]
        return jnp.concatenate(cuts, 0)

    def own_quarter(self, values):
        rows = values.shape[0] // self.mp
        return lax.dynamic_slice_in_dim(values, self.rank * rows, rows, 0)

    def gather_core(self, quarter, far):
        rows = quarter.shape[0]
        near = self.swap_mp(jnp.concatenate([quarter, far], 0), 1)
        return jnp.concatenate([quarter, near[:rows], far, near[rows:]], 0)

    def swap_core(self, slots):
        rows = slots.shape[0] // 8
        picked = lambda ks: jnp.concatenate([slots[k * rows : (k + 1) * rows] for k in ks], 0)
        return slots, self.swap_mp(picked((1, 3, 5, 7)), 1)

    def sum_core(self, slots, near):
        rows = slots.shape[0] // 8
        add = lambda ks, low: jnp.concatenate(
            [
                slots[k * rows : (k + 1) * rows].astype(F32) + near[i * rows : (i + 1) * rows].astype(F32)
                for i, k in enumerate(ks, low)
            ],
            0,
        ).astype(BF16)
        return add((0, 2), 0), add((4, 6), 2)


def after(value, *others):
    return lax.optimization_barrier((value, *others))[0]


def inverse_rms(values):
    return lax.rsqrt(jnp.mean(values * values, -1, keepdims=True) + NORM_EPS)


def body(
    dp_size,
    mp_size,
    tokens,
    cotangent,
    segment_ids,
    w_query,
    w_key,
    w_value,
    w_out,
    w_gate_up,
    w_down,
    norm_gains,
    query_moments,
    key_moments,
    value_moments,
    out_moments,
    gate_up_moments,
    down_moments,
    gains_moments,
):
    links = Links(dp_size, mp_size)
    line, side = links.line, links.side
    heads = w_query.shape[1] // HEAD
    kvs = w_key.shape[1] // HEAD
    group = heads // kvs
    width = tokens.shape[1]
    shard = w_query.shape[0]
    units = w_gate_up.shape[2]
    block = units // (line * 2)

    def interleave(query, key, value):
        parts = []
        for kv in range(kvs):
            parts.append(query[..., kv * group * HEAD : (kv + 1) * group * HEAD])
            parts.append(key[..., kv * HEAD : (kv + 1) * HEAD])
            parts.append(value[..., kv * HEAD : (kv + 1) * HEAD])
        return jnp.concatenate(parts, -1)

    by_side = w_gate_up.reshape(2, shard, line, 2, block)

    def side_units(which):
        cut = lax.dynamic_index_in_dim(by_side, which, 3, keepdims=False).astype(BF16)
        return jnp.concatenate([cut[0].reshape(shard, -1), cut[1].reshape(shard, -1)], 1)

    inputs = tokens.astype(F32)
    scale_one = inverse_rms(inputs)
    down_full = links.gather_line(w_down.astype(BF16))
    own_units = side_units(side)
    sent_units = links.swap_side(side_units(1 - side))
    rows_pair = jnp.zeros((2 * shard, own_units.shape[1]), BF16)
    rows_pair = lax.dynamic_update_slice(rows_pair, own_units, (side * shard, 0))
    rows_pair = lax.dynamic_update_slice(rows_pair, sent_units, ((1 - side) * shard, 0))
    gate_up_full = after(links.gather_line(rows_pair), down_full)
    gains_low = norm_gains.astype(BF16).astype(F32)
    gains_rows = jnp.concatenate([gains_low, jnp.zeros((6, gains_low.shape[1]), F32)], 0)
    qkv_full, out_full, gains_shards, grad_rows = call_gather_weights(
        dp_size,
        cotangent,
        after(interleave(w_query, w_key, w_value).astype(BF16), rows_pair, scale_one),
        w_out.astype(BF16),
        gains_rows,
    )
    gains_full = jnp.transpose(gains_shards.reshape(dp_size, 8, -1), (1, 0, 2)).reshape(8, width)

    quarter = tokens.shape[0] // 4

    cosine, sine = rope_tables(segment_ids.shape[1])
    normed_one = (inputs * scale_one * gains_full[0]).astype(BF16)
    qkv = jnp.dot(normed_one, qkv_full, preferred_element_type=F32)
    rank_ref = links.rank.astype(jnp.int32).reshape(1)
    mixed_slots, rotated, lse, peaks = attention_forward(rank_ref, qkv, cosine, sine, segment_ids, group, kvs)
    tokens_own = links.own_quarter(tokens)
    rows_two, middle = call_spread_forward(
        jnp.dot(mixed_slots, out_full, preferred_element_type=F32).astype(BF16), tokens_own, gains_full[1:2]
    )

    columns = line * block
    grad_hidden = dot_nt(grad_rows, down_full)
    grad_hidden, gate_up_full = lax.optimization_barrier((grad_hidden, gate_up_full))
    both = jnp.dot(rows_two, gate_up_full, preferred_element_type=F32)
    gate, up = both[:, :columns], both[:, columns:]
    sigmoid = jax.nn.sigmoid(gate)
    hidden = (gate * sigmoid * up).astype(BF16)
    grad_gate = (grad_hidden * up * sigmoid * (1.0 + gate * (1.0 - sigmoid))).astype(BF16)
    grad_up = (grad_hidden * gate * sigmoid).astype(BF16)
    output_part = jnp.dot(hidden, down_full, preferred_element_type=F32).astype(BF16)
    output_part, output_near = links.swap_core(output_part)
    grad_down_part = dot_tn(after(hidden, output_part), grad_rows).astype(BF16)
    grad_gate_part = dot_tn(after(rows_two, grad_down_part), grad_gate).astype(BF16)
    grad_both = after(jnp.concatenate([grad_gate, grad_up], 1), grad_gate_part)
    back = dot_nt(grad_both, gate_up_full).astype(BF16)
    grad_middle_slots, grad_middle, gain_two = call_spread_backward(
        after(back, output_near), middle, links.own_quarter(cotangent), gains_full[1:2]
    )
    output_mine, output_theirs = links.sum_core(output_part, after(output_near, grad_middle_slots))
    grad_down_low = links.sum_line(grad_down_part)
    grad_up_part = dot_tn(after(rows_two, output_theirs, grad_down_low), grad_up).astype(BF16)
    gate_sum = after(links.sum_line(grad_gate_part), grad_down_low)
    up_sum = after(links.sum_line(grad_up_part), gate_sum)
    grad_middle_slots = after(grad_middle_slots, grad_up_part)
    grad_mixed = dot_nt(grad_middle_slots, out_full).astype(BF16)

    grad_down = grad_down_low.astype(F32)
    down_second, down_direction = lamb_direction(w_down, down_moments[0], down_moments[1], grad_down)
    down_sum = jnp.sum(down_direction * down_direction)

    local_peak = peaks[:, :group, 0].reshape(heads)
    peak_vector = lax.dynamic_update_slice(
        jnp.full((HEADS,), MASKED, F32), local_peak, (links.rank * heads,)
    )
    owner = (links.rank == 0).astype(F32)
    lanes = lax.broadcasted_iota(jnp.int32, (16, HEAD), 1)
    lower = lax.broadcasted_iota(jnp.int32, (16, HEAD), 0) < 8
    early = jnp.broadcast_to(jnp.pad(peak_vector, (0, HEAD - HEADS), constant_values=MASKED), (16, HEAD))
    early = jnp.where(lower, 0.0, early)
    masters = (w_query, w_key, w_value, w_out, w_gate_up, w_down, norm_gains)
    for number, master in enumerate(masters):
        square = jnp.sum(master * master) * (owner if number == 6 else 1.0)
        early = jnp.where(lower & (lanes == number), square, early)
    early = jnp.where(lower & (lanes == 12), down_sum, early)

    grad_qkv = attention_backward(rank_ref, rotated, grad_mixed, lse, cosine, sine, segment_ids, group, kvs)
    grad_qkv_part = dot_tn(links.to_slots(normed_one), grad_qkv).astype(BF16)
    grad_out_part = dot_tn(mixed_slots, grad_middle_slots).astype(BF16)
    grad_normed_one = dot_nt(grad_qkv, qkv_full).astype(BF16)
    output_theirs = links.swap_side(output_theirs)
    output_pair = output_mine.astype(F32) + after(output_theirs, grad_qkv_part, grad_normed_one).astype(F32)
    output_far = links.swap_mp(output_pair[quarter:].astype(BF16), 2).astype(F32)
    input_slots, gain_terms, grad_qkv_own, grad_out = call_finish(
        dp_size,
        after(grad_normed_one, gate_sum, output_pair),
        tokens_own,
        grad_middle,
        gains_full[0:1],
        gain_two,
        grad_qkv_part,
        grad_out_part,
    )
    input_grad = links.from_slots(input_slots).astype(F32)
    output_low = (middle + output_pair[:quarter] + after(output_far, input_slots)).astype(BF16)
    output_far = links.swap_mp(output_low, 2)

    other_side = lambda value: lax.dynamic_slice_in_dim(value, (1 - side) * shard, shard, 0)
    summed = [gate_sum, up_sum]
    theirs = [links.swap_side(other_side(value)) for value in summed]
    grad_qkv_own = after(grad_qkv_own, theirs[0], other_side(up_sum))
    gain_terms = gain_terms.reshape(2, width)
    gain_width = norm_gains.shape[1]
    grad_gains = lax.dynamic_slice_in_dim(gain_terms, links.index * gain_width, gain_width, 1)

    small = (w_query, w_key, w_value, w_out, norm_gains)
    small_moments = (query_moments, key_moments, value_moments, out_moments, gains_moments)
    grad_query, grad_key, grad_value, *rest = call_small_step(
        group, kvs, jnp.full((1, HEAD), owner), grad_qkv_own, grad_out, grad_gains, small, small_moments
    )
    small_seconds, small_directions, small_sums = rest[:SMALL], rest[SMALL : 2 * SMALL], rest[2 * SMALL]
    if block % HEAD == 0:
        grad_gate_up, gate_up_second, gate_up_direction, gate_up_sums = call_gate_up_step(
            line, side.astype(jnp.int32).reshape(1), w_gate_up, gate_up_moments, summed, theirs
        )
    else:
        parts = []
        for j in range(2):
            mine = lax.dynamic_slice_in_dim(summed[j], side * shard, shard, 0)
            sides = [jnp.where(side == 0, mine, theirs[j]), jnp.where(side == 0, theirs[j], mine)]
            parts.append(jnp.stack([value.reshape(shard, line, block) for value in sides], 2))
        grad_gate_up = jnp.stack(parts, 0).reshape(w_gate_up.shape)
        grad_gate_up = grad_gate_up.astype(F32)
        gate_up_second, gate_up_direction = lamb_direction(
            w_gate_up, gate_up_moments[0], gate_up_moments[1], grad_gate_up
        )
        gate_up_sums = jnp.sum((gate_up_direction * gate_up_direction).reshape(-1, 8, 2 * HEAD), 0)
    output_far = after(output_far, gate_up_sums)
    block_output = links.from_slots(links.gather_core(output_low, output_far))
    packed = call_combine_all(dp_size, early, small_sums, gate_up_sums)
    updated = call_small_update(
        group, kvs, links.rank.astype(jnp.int32).reshape(1), packed, small, small_directions
    )
    flat_rows = lambda value: value.reshape(2 * shard, units)
    new_gate_up, copy_gate_up = (
        value.reshape(w_gate_up.shape)
        for value in call_large_update(4, packed, flat_rows(w_gate_up), flat_rows(gate_up_direction))
    )
    new_down, copy_down = call_large_update(5, packed, w_down, down_direction)
    grads = (grad_query, grad_key, grad_value, grad_out, grad_gate_up, grad_down, grad_gains)
    place_large = lambda values, gate_up, down: (*values[:4], gate_up, down, values[4])
    norms = jnp.sqrt(jnp.stack([packed[0, :7], packed[0, 7:14]]))
    return (
        block_output,
        input_grad,
        *grads,
        *place_large(small_seconds, gate_up_second, down_second),
        *place_large(updated[:SMALL], new_gate_up, new_down),
        *place_large(updated[SMALL:], copy_gate_up, copy_down),
        norms,
        packed[8, :HEADS],
    )


def solution(mesh):
    column = P("dp", "mp")
    row = P(("mp", "dp"), None)
    gate_up = P(None, "dp", "mp")
    gains = P(None, "dp")
    params = (column, column, column, row, gate_up, row, gains)
    moments = (
        P(None, "dp", "mp"),
        P(None, "dp", "mp"),
        P(None, "dp", "mp"),
        P(None, ("mp", "dp"), None),
        P(None, None, "dp", "mp"),
        P(None, ("mp", "dp"), None),
        P(None, None, "dp"),
    )
    tokens = P("dp", None)
    return jax.shard_map(
        functools.partial(body, mesh.shape["dp"], mesh.shape["mp"]),
        mesh=mesh,
        in_specs=(tokens, tokens, tokens, *params, *moments),
        out_specs=(tokens, tokens, *params, *params, *params, *params, P(), P()),
        check_vma=False,
    )
```

```python
import functools
import math

import jax
import jax.numpy as jnp
from jax import lax
from jax.experimental import pallas as pl
from jax.experimental.pallas import tpu as pltpu
from jax.sharding import PartitionSpec as P

HEADS = 16
HEAD = 128
BLOCK = 512
CLIP = 10
TILE = 256

NORM_EPS = 1e-05
ROPE_BASE = 1000000.0
RATE = 0.4
DECAY = 0.5
WEIGHT_DECAY = 0.01
STEP_EPS = 1e-06
MASKED = -1e30

F32 = jnp.float32
BF16 = jnp.bfloat16


def rope_tables(length):
    positions = jnp.arange(length, dtype=F32)
    frequency = ROPE_BASE ** (-(jnp.arange(HEAD // 2, dtype=F32) * 2.0) / HEAD)
    angles = positions[:, None] * frequency[None, :]
    cosine, sine = jnp.cos(angles), jnp.sin(angles)
    return jnp.concatenate([cosine, cosine], 1), jnp.concatenate([-sine, sine], 1)


def lasting(microseconds):
    return pl.CostEstimate(flops=0, bytes_accessed=int(microseconds * 3e6), transcendentals=0)


def turn(values, cosine, sine):
    return values * cosine + pltpu.roll(values, HEAD // 2, 1) * sine


def allowed_mask(seg_row_ref, seg_col_ref, row_start, low, high):
    query_pos = row_start + lax.broadcasted_iota(jnp.int32, (TILE, high - low), 0)
    key_pos = low + lax.broadcasted_iota(jnp.int32, (TILE, high - low), 1)
    same = seg_col_ref[row_start : row_start + TILE, :] == seg_row_ref[0, :, low:high]
    return (key_pos <= query_pos) & same


def dot_nt(left, right):
    return lax.dot_general(left, right, (((1,), (1,)), ((), ())), preferred_element_type=F32)


def dot_nn(left, right):
    return lax.dot_general(left, right, (((1,), (0,)), ((), ())), preferred_element_type=F32)


def dot_tn(left, right):
    return lax.dot_general(left, right, (((0,), (0,)), ((), ())), preferred_element_type=F32)


def slot_rows(rank_ref, start):
    return pl.ds(pl.multiple_of(((start // TILE) ^ rank_ref[0]) * TILE, TILE), TILE)


def attend_forward(group, rank_ref, qkv_ref, cos_ref, sin_ref, seg_row_ref, seg_col_ref, out_ref, rot_ref, lse_ref, peak_ref):
    length = qkv_ref.shape[0]
    scale = 1.0 / math.sqrt(HEAD)
    value_columns = slice((group + 1) * HEAD, (group + 2) * HEAD)
    for start in range(0, length, TILE):
        rows, source = slice(start, start + TILE), slot_rows(rank_ref, start)
        for part in range(group + 1):
            columns = slice(part * HEAD, (part + 1) * HEAD)
            turned = turn(qkv_ref[source, columns], cos_ref[rows, :], sin_ref[rows, :])
            rot_ref[rows, columns] = turned.astype(BF16)
        rot_ref[rows, value_columns] = qkv_ref[source, value_columns].astype(BF16)
    key_columns = slice(group * HEAD, (group + 1) * HEAD)
    peak_ref[...] = jnp.full(peak_ref.shape, MASKED, F32)
    peaks = [None] * group
    for start in range(0, length, TILE):
        low, high = max(0, start - BLOCK), start + TILE
        rows = slice(start, start + TILE)
        mask = allowed_mask(seg_row_ref, seg_col_ref, start, low, high)
        keys = rot_ref[low:high, key_columns]
        values = rot_ref[low:high, value_columns]
        for head in range(group):
            columns = slice(head * HEAD, (head + 1) * HEAD)
            scores = jnp.where(mask, dot_nt(rot_ref[rows, columns], keys) * scale, MASKED)
            top = jnp.max(scores, 1, keepdims=True)
            exponent = jnp.exp(scores - top)
            total = jnp.sum(exponent, 1, keepdims=True)
            probs = (exponent * (1.0 / total)).astype(BF16)
            out_ref[slot_rows(rank_ref, start), columns] = dot_nn(probs, values).astype(BF16)
            lse_ref[rows, columns] = jnp.broadcast_to(top + jnp.log(total), (TILE, HEAD))
            peak = jnp.max(top, 0, keepdims=True)
            peaks[head] = peak if peaks[head] is None else jnp.maximum(peaks[head], peak)
    for head in range(group):
        peak_ref[0, head : head + 1, :] = jnp.broadcast_to(peaks[head], (1, HEAD))


def attend_backward(group, rank_ref, rot_ref, grad_ref, lse_ref, cos_ref, sin_ref, seg_row_ref, seg_col_ref, out_ref, dk_ref, dv_ref):
    length = rot_ref.shape[0]
    scale = 1.0 / math.sqrt(HEAD)
    key_columns = slice(group * HEAD, (group + 1) * HEAD)
    value_columns = slice((group + 1) * HEAD, (group + 2) * HEAD)
    dk_ref[...] = jnp.zeros(dk_ref.shape, F32)
    dv_ref[...] = jnp.zeros(dv_ref.shape, F32)
    for start in range(0, length, TILE):
        low, high = max(0, start - BLOCK), start + TILE
        rows = slice(start, start + TILE)
        mask = allowed_mask(seg_row_ref, seg_col_ref, start, low, high)
        keys = rot_ref[low:high, key_columns]
        values = rot_ref[low:high, value_columns]
        for head in range(group):
            columns = slice(head * HEAD, (head + 1) * HEAD)
            queries = rot_ref[rows, columns]
            grads = grad_ref[slot_rows(rank_ref, start), columns]
            scores = dot_nt(queries, keys) * scale
            probs = jnp.exp(jnp.where(mask, scores - lse_ref[rows, columns][:, :1], MASKED))
            grad_probs = dot_nt(grads, values)
            inner = jnp.sum(probs * grad_probs, 1, keepdims=True)
            grad_scores = (probs * (grad_probs - inner)).astype(BF16)
            dv_ref[low:high, :] += dot_tn(probs.astype(BF16), grads)
            dk_ref[low:high, :] += dot_tn(grad_scores, queries)
            grad_query = dot_nn(grad_scores, keys) * scale
            turned = turn(grad_query, cos_ref[rows, :], -sin_ref[rows, :])
            out_ref[slot_rows(rank_ref, start), columns] = turned.astype(BF16)
    for start in range(0, length, TILE):
        rows = slice(start, start + TILE)
        turned = turn(dk_ref[rows, :] * scale, cos_ref[rows, :], -sin_ref[rows, :])
        out_ref[slot_rows(rank_ref, start), key_columns] = turned.astype(BF16)
        out_ref[slot_rows(rank_ref, start), value_columns] = dv_ref[rows, :].astype(BF16)


def attention_specs(length, group):
    wide = pl.BlockSpec((length, (group + 2) * HEAD), lambda kv, rank: (0, kv))
    narrow = pl.BlockSpec((length, group * HEAD), lambda kv, rank: (0, kv))
    table = pl.BlockSpec((length, HEAD), lambda kv, rank: (0, 0))
    seg_row = pl.BlockSpec((1, 1, length), lambda kv, rank: (0, 0, 0))
    seg_col = pl.BlockSpec((length, 1), lambda kv, rank: (0, 0))
    return wide, narrow, table, seg_row, seg_col


def attention_forward(rank, qkv, cosine, sine, segments, group, kv_count):
    length = segments.shape[1]
    wide, narrow, table, seg_row, seg_col = attention_specs(length, group)
    return pl.pallas_call(
        functools.partial(attend_forward, group),
        grid_spec=pltpu.PrefetchScalarGridSpec(
            num_scalar_prefetch=1,
            grid=(kv_count,),
            in_specs=[wide, table, table, seg_row, seg_col],
            out_specs=[narrow, wide, narrow, pl.BlockSpec((1, 8, HEAD), lambda kv, rank: (kv, 0, 0))],
        ),
        out_shape=[
            jax.ShapeDtypeStruct((length, kv_count * group * HEAD), BF16),
            jax.ShapeDtypeStruct((length, kv_count * (group + 2) * HEAD), BF16),
            jax.ShapeDtypeStruct((length, kv_count * group * HEAD), F32),
            jax.ShapeDtypeStruct((kv_count, 8, HEAD), F32),
        ],
        compiler_params=pltpu.CompilerParams(vmem_limit_bytes=48 * 2**20),
        cost_estimate=lasting(12),
        name="attention_forward",
    )(rank, qkv, cosine, sine, segments.reshape(1, 1, length), segments.reshape(length, 1))


def attention_backward(rank, rotated, grads, lse, cosine, sine, segments, group, kv_count):
    length = segments.shape[1]
    wide, narrow, table, seg_row, seg_col = attention_specs(length, group)
    return pl.pallas_call(
        functools.partial(attend_backward, group),
        grid_spec=pltpu.PrefetchScalarGridSpec(
            num_scalar_prefetch=1,
            grid=(kv_count,),
            in_specs=[wide, narrow, narrow, table, table, seg_row, seg_col],
            out_specs=wide,
            scratch_shapes=[pltpu.VMEM((length, HEAD), F32), pltpu.VMEM((length, HEAD), F32)],
        ),
        out_shape=jax.ShapeDtypeStruct((length, kv_count * (group + 2) * HEAD), BF16),
        compiler_params=pltpu.CompilerParams(vmem_limit_bytes=48 * 2**20),
        cost_estimate=lasting(13),
        name="attention_backward",
    )(rank, rotated, grads, lse, cosine, sine, segments.reshape(1, 1, length), segments.reshape(length, 1))


def gate_rows(both_ref, grad_ref, hidden_ref, grad_both_ref):
    columns = grad_ref.shape[1]
    gate, up, grad = both_ref[:, :columns], both_ref[:, columns:], grad_ref[...]
    sigmoid = 1.0 / (1.0 + jnp.exp(-gate))
    silu = gate * sigmoid
    hidden_ref[...] = (silu * up).astype(BF16)
    grad_both_ref[:, :columns] = (grad * up * (sigmoid * (1.0 + gate * (1.0 - sigmoid)))).astype(BF16)
    grad_both_ref[:, columns:] = (grad * silu).astype(BF16)


def call_gate_rows(both, grad):
    rows, columns = grad.shape
    tile = lambda width: pl.BlockSpec((TILE, width), lambda i: (i, 0))
    return pl.pallas_call(
        gate_rows,
        grid=(rows // TILE,),
        in_specs=[tile(2 * columns), tile(columns)],
        out_specs=[tile(columns), tile(2 * columns)],
        out_shape=[jax.ShapeDtypeStruct((rows, columns), BF16), jax.ShapeDtypeStruct((rows, 2 * columns), BF16)],
        cost_estimate=lasting(10),
        name="gate_rows",
    )(both, grad)


def lamb_direction(master, first, second, grad):
    first_moment = DECAY * first + (1.0 - DECAY) * grad
    second_moment = DECAY * second + (1.0 - DECAY) * grad * grad
    return second_moment, first_moment / (jnp.sqrt(second_moment) + STEP_EPS) + WEIGHT_DECAY * master


def gate_up_step(side_ref, master_ref, moment_ref, *refs):
    (gate_mine, up_mine, gate_theirs, up_theirs), (grad_ref, second_ref, direction_ref, sums_ref) = refs[:4], refs[4:]
    part, place, which = pl.program_id(0), pl.program_id(1), pl.program_id(2)
    mine = jnp.where(part == 0, gate_mine[...], up_mine[...])
    theirs = jnp.where(part == 0, gate_theirs[...], up_theirs[...])
    grad = jnp.where(which == side_ref[0], mine, theirs).astype(F32)
    second, direction = lamb_direction(master_ref[0], moment_ref[0, 0], moment_ref[1, 0], grad)
    grad_ref[0], second_ref[0], direction_ref[0] = grad, second, direction

    @pl.when((part == 0) & (place == 0) & (which == 0))
    def _():
        sums_ref[...] = jnp.zeros(sums_ref.shape, F32)

    sums_ref[...] += jnp.sum((direction * direction).reshape(-1, 8, direction.shape[1]), 0)


def call_gate_up_step(line, side, master, moments, summed, theirs):
    _, shard, units = master.shape
    block = units // (2 * line)
    whole = pl.BlockSpec((1, shard, block), lambda g, p, w, side: (g, 0, p * 2 + w))
    shape = jax.ShapeDtypeStruct(master.shape, F32)
    gate_place = lambda g, p: jnp.where(g == 0, p, line - 1)
    up_place = lambda g, p: jnp.where(g == 1, p, 0)
    return pl.pallas_call(
        gate_up_step,
        grid_spec=pltpu.PrefetchScalarGridSpec(
            num_scalar_prefetch=1,
            grid=(2, line, 2),
            in_specs=[
                whole,
                pl.BlockSpec((2, 1, shard, block), lambda g, p, w, side: (0, g, 0, p * 2 + w)),
                pl.BlockSpec((shard, block), lambda g, p, w, side: (side[0], gate_place(g, p))),
                pl.BlockSpec((shard, block), lambda g, p, w, side: (side[0], up_place(g, p))),
                pl.BlockSpec((shard, block), lambda g, p, w, side: (0, gate_place(g, p))),
                pl.BlockSpec((shard, block), lambda g, p, w, side: (0, up_place(g, p))),
            ],
            out_specs=[whole, whole, whole, pl.BlockSpec((8, block), lambda g, p, w, side: (0, 0))],
        ),
        out_shape=[shape, shape, shape, jax.ShapeDtypeStruct((8, block), F32)],
        cost_estimate=lasting(16),
        name="gate_up_step",
    )(side, master, moments, *summed, *theirs)


VMEM_ALL = pl.BlockSpec(memory_space=pltpu.VMEM)
SMALL = 5


def small_step(group, kvs, owner_ref, grad_qkv_ref, grad_out_ref, grad_gains_ref, *refs):
    masters, moments, refs = refs[:SMALL], refs[SMALL : 2 * SMALL], refs[2 * SMALL :]
    grads, seconds, directions, sums_ref = refs[:3], refs[3:8], refs[8:13], refs[13]
    step = (group + 2) * HEAD
    for kv in range(kvs):
        low = kv * step
        for ref, start, columns in ((grads[0], 0, group * HEAD), (grads[1], group * HEAD, HEAD), (grads[2], (group + 1) * HEAD, HEAD)):
            ref[:, kv * columns : (kv + 1) * columns] = grad_qkv_ref[:, low + start : low + start + columns]
    sums_ref[...] = jnp.zeros(sums_ref.shape, F32)
    for number in range(SMALL):
        grad = (grads[0], grads[1], grads[2], grad_out_ref, grad_gains_ref)[number][...]
        moment = moments[number]
        second, direction = lamb_direction(masters[number][...], moment[0], moment[1], grad)
        seconds[number][...] = second
        directions[number][...] = direction
        total = jnp.sum(jnp.sum(direction * direction, 0, keepdims=True), 1, keepdims=True)
        row = jnp.broadcast_to(total, (1, HEAD))
        sums_ref[number : number + 1, :] = row * owner_ref[...] if number == SMALL - 1 else row


def call_small_step(group, kvs, owner, grad_qkv, grad_out, grad_gains, masters, moments):
    like = lambda arrays: [jax.ShapeDtypeStruct(array.shape, F32) for array in arrays]
    return pl.pallas_call(
        functools.partial(small_step, group, kvs),
        in_specs=[VMEM_ALL] * (4 + 2 * SMALL),
        out_specs=[VMEM_ALL] * 14,
        out_shape=[*like(masters[:3]), *like(masters), *like(masters), jax.ShapeDtypeStruct((8, HEAD), F32)],
        compiler_params=pltpu.CompilerParams(vmem_limit_bytes=40 * 2**20),
        cost_estimate=lasting(6),
        name="small_step",
    )(owner, grad_qkv, grad_out, grad_gains, *masters, *moments)


def pick_lane(row, lane):
    lanes = lax.broadcasted_iota(jnp.int32, row.shape, 1)
    return jnp.sum(jnp.where(lanes == lane, row, 0.0), 1, keepdims=True)


def rate_of(packed_ref, number):
    squares = packed_ref[0:1, :]
    weight, update = jnp.sqrt(pick_lane(squares, number)), jnp.sqrt(pick_lane(squares, 7 + number))
    return RATE * (weight / (update + STEP_EPS))


def small_update(group, kvs, rank_ref, packed_ref, *refs):
    masters, directions, news, copies = (refs[k * SMALL : (k + 1) * SMALL] for k in range(4))
    gamma = CLIP / jnp.maximum(packed_ref[8:9, :], float(CLIP))
    heads = [pick_lane(gamma, rank_ref[0] * (group * kvs) + head) for head in range(group * kvs)]
    for place, number in enumerate((0, 1, 2, 3, 6)):
        rate = rate_of(packed_ref, number)
        if place > 1:
            stepped = masters[place][...] - rate * directions[place][...]
            news[place][...] = stepped
            copies[place][...] = stepped.astype(BF16)
            continue
        for head in range(group * kvs if place == 0 else kvs):
            scale = heads[head]
            if place == 1:
                scale = functools.reduce(jnp.minimum, heads[head * group : (head + 1) * group])
            columns = slice(head * HEAD, (head + 1) * HEAD)
            stepped = masters[place][:, columns] - rate * directions[place][:, columns]
            stepped = stepped * jnp.sqrt(scale)
            news[place][:, columns] = stepped
            copies[place][:, columns] = stepped.astype(BF16)


def call_small_update(group, kvs, rank, packed, masters, directions):
    like = lambda kind: [jax.ShapeDtypeStruct(array.shape, kind) for array in masters]
    return pl.pallas_call(
        functools.partial(small_update, group, kvs),
        in_specs=[pl.BlockSpec(memory_space=pltpu.SMEM), *[VMEM_ALL] * (1 + 2 * SMALL)],
        out_specs=[VMEM_ALL] * (2 * SMALL),
        out_shape=[*like(F32), *like(BF16)],
        compiler_params=pltpu.CompilerParams(vmem_limit_bytes=40 * 2**20),
        cost_estimate=lasting(5),
        name="small_update",
    )(rank, packed, *masters, *directions)


def large_update(number, packed_ref, master_ref, direction_ref, new_ref, copy_ref):
    stepped = master_ref[...] - rate_of(packed_ref, number) * direction_ref[...]
    new_ref[...] = stepped
    copy_ref[...] = stepped.astype(BF16)


def call_large_update(number, packed, master, direction):
    rows, columns = master.shape
    tile = min(rows, 128)
    blocks = pl.BlockSpec((tile, columns), lambda i: (i, 0))
    return pl.pallas_call(
        functools.partial(large_update, number),
        grid=(rows // tile,),
        in_specs=[pl.BlockSpec((16, HEAD), lambda i: (0, 0)), blocks, blocks],
        out_specs=[blocks, blocks],
        out_shape=[jax.ShapeDtypeStruct(master.shape, F32), jax.ShapeDtypeStruct(master.shape, BF16)],
        cost_estimate=lasting(4),
        name="large_update",
    )(packed, master, direction)


MESH = pl.DeviceIdType.MESH
WHOLE = pl.BlockSpec(memory_space=pltpu.VMEM)
CHUNKS = 8
AHEAD = 1


def greet(partners):
    barrier = pltpu.get_barrier_semaphore()
    for partner in partners:
        pl.semaphore_signal(barrier, inc=1, device_id=partner, device_id_type=MESH)
    pl.semaphore_wait(barrier, len(partners))


def sender(send_sems, recv_sems, log):
    def copy(kind, chunk, source, target, device):
        made = pltpu.make_async_remote_copy(
            src_ref=source,
            dst_ref=target,
            send_sem=send_sems.at[kind, chunk],
            recv_sem=recv_sems.at[kind, chunk],
            device_id=device,
            device_id_type=MESH,
        )
        log.append(made)
        return made

    return copy


def partners_of():
    rank, index = lax.axis_index("mp"), lax.axis_index("dp")
    return {"mp": rank ^ 1}, {"mp": rank ^ 2}, {"dp": index ^ 1}


def pick_rows(side_ref, rows_ref, _, out_ref):
    out_ref[...] = rows_ref[...]


def call_pick_rows(side, values, ready):
    rows, columns = values.shape[0] // 2, values.shape[1]
    return pl.pallas_call(
        pick_rows,
        grid_spec=pltpu.PrefetchScalarGridSpec(
            num_scalar_prefetch=1,
            grid=(1,),
            in_specs=[
                pl.BlockSpec((rows, columns), lambda i, side: (1 - side[0], 0)),
                pl.BlockSpec(memory_space=pl.ANY),
            ],
            out_specs=pl.BlockSpec((rows, columns), lambda i, side: (0, 0)),
        ),
        out_shape=jax.ShapeDtypeStruct((rows, columns), values.dtype),
        cost_estimate=lasting(2),
        name="pick_rows",
    )(side, values, ready)


class Everyone:
    def __init__(self, line, near_ref, line_ref, near_send, near_recv, line_send, line_recv):
        self.line, self.near_ref, self.line_ref = line, near_ref, line_ref
        self.near_send, self.near_recv, self.line_send, self.line_recv = near_send, near_recv, line_send, line_recv
        self.index, self.rank = lax.axis_index("dp"), lax.axis_index("mp")
        self.place, self.side = self.index // 2, self.index % 2
        self.code = self.side * 4 + self.rank

    @staticmethod
    def scratch(line, shape):
        return [
            pltpu.VMEM((8, *shape), F32),
            pltpu.VMEM((line, *shape), F32),
            pltpu.SemaphoreType.DMA((8,)),
            pltpu.SemaphoreType.DMA((8,)),
            pltpu.SemaphoreType.DMA((line,)),
            pltpu.SemaphoreType.DMA((line,)),
        ]

    def peer(self, k):
        return {"dp": self.index ^ (k // 4), "mp": self.rank ^ (k % 4)}

    def along(self, k):
        return {"dp": ((self.place + k) % self.line) * 2 + self.side}

    def partners(self):
        return [self.peer(k) for k in range(1, 8)] + [self.along(k) for k in range(1, self.line)]

    @staticmethod
    def add(left, right):
        return left + right

    def near_copy(self, k, slot):
        return pltpu.make_async_remote_copy(
            src_ref=self.near_ref.at[self.code],
            dst_ref=self.near_ref.at[slot],
            send_sem=self.near_send.at[k],
            recv_sem=self.near_recv.at[slot],
            device_id=self.peer(k),
            device_id_type=MESH,
        )

    def line_copy(self, k, slot):
        return pltpu.make_async_remote_copy(
            src_ref=self.line_ref.at[self.place],
            dst_ref=self.line_ref.at[slot],
            send_sem=self.line_send.at[k],
            recv_sem=self.line_recv.at[slot],
            device_id=self.along(k),
            device_id_type=MESH,
        )

    @staticmethod
    def total(ref, count, fold):
        value = ref[0]
        for k in range(1, count):
            value = fold(value, ref[k])
        return value

    def send_near(self):
        for k in range(1, 8):
            self.near_copy(k, self.code).start()

    def send_line(self, fold):
        for k in range(1, 8):
            self.near_copy(k, self.code ^ k).wait_recv()
        self.line_ref[self.place] = self.total(self.near_ref, 8, fold)
        for k in range(1, self.line):
            self.line_copy(k, self.place).start()

    def result(self, fold):
        for k in range(1, self.line):
            self.line_copy(k, (self.place + k) % self.line).wait_recv()
        value = self.total(self.line_ref, self.line, fold)
        for k in range(1, 8):
            self.near_copy(k, self.code).wait_send()
        for k in range(1, self.line):
            self.line_copy(k, self.place).wait_send()
        return value


def spread_forward(part_ref, tokens_ref, gain_ref, grad_ref, down_ref, rows_ref, middle_ref, hidden_ref, near_ref, out_ref, far_ref, grad_in_ref, down_in_ref, hidden_out_ref, send_sems, recv_sems, fetch_sems, store_sems):
    fetches = [
        pltpu.make_async_copy(source, target, fetch_sems.at[k])
        for k, (source, target) in enumerate(((grad_ref, grad_in_ref), (down_ref, down_in_ref)))
    ]
    for fetch in fetches:
        fetch.start()
    band = hidden_out_ref.shape[0] // CHUNKS
    stores = []

    def multiply(i):
        rows = pl.ds(i * band, band)
        hidden_out_ref[rows, :] = dot_nt(grad_in_ref[rows, :], down_in_ref[...])
        stores.append(pltpu.make_async_copy(hidden_out_ref.at[rows], hidden_ref.at[rows], store_sems.at[i]))
        stores[-1].start()

    core, far, pair = partners_of()
    quarter, _ = tokens_ref.shape
    size = quarter // CHUNKS
    at = lambda slot, i: pl.ds(slot * quarter + i * size, size)
    greet([core, far, pair])
    log = []
    copy = sender(send_sems, recv_sems, log)
    near = {}
    for i in range(CHUNKS):
        for k in range(2):
            near[k, i] = copy(k, i, part_ref.at[at(2 * k + 1, i)], near_ref.at[at(k, i)], core)
            near[k, i].start()
    sums = {}

    def send_sum(i):
        near[1, i].wait_recv()
        total = part_ref[at(2, i), :].astype(F32) + near_ref[at(1, i), :].astype(F32)
        out_ref[at(0, i), :] = total.astype(BF16)
        sums[i] = copy(2, i, out_ref.at[at(0, i)], far_ref.at[at(0, i)], far)
        sums[i].start()

    for i in range(AHEAD):
        send_sum(i)
    moves = {}
    for i in range(CHUNKS + 2):
        if i + AHEAD < CHUNKS:
            send_sum(i + AHEAD)
        if i < CHUNKS:
            near[0, i].wait_recv()
            sums[i].wait_recv()
            middle = tokens_ref[at(0, i), :].astype(F32) + (
                part_ref[at(0, i), :].astype(F32)
                + near_ref[at(0, i), :].astype(F32)
                + far_ref[at(0, i), :].astype(F32)
            )
            middle_ref[at(0, i), :] = middle
            rows_ref[at(0, i), :] = (middle * inverse_rms(middle) * gain_ref[0:1, :]).astype(BF16)
            own = rows_ref.at[at(0, i)]
            for kind, slot, device in ((3, 2, far), (4, 4, pair), (6, 1, core)):
                moves[kind, i] = copy(kind, i, own, rows_ref.at[at(slot, i)], device)
                moves[kind, i].start()
        j = i - 1
        if 0 <= j < CHUNKS:
            moves[3, j].wait_recv()
            for kind, slot, device in ((5, 6, pair), (7, 3, core)):
                moves[kind, j] = copy(kind, j, rows_ref.at[at(2, j)], rows_ref.at[at(slot, j)], device)
                moves[kind, j].start()
            moves[4, j].wait_recv()
            moves[8, j] = copy(8, j, rows_ref.at[at(4, j)], rows_ref.at[at(5, j)], core)
            moves[8, j].start()
        j = i - 2
        if 0 <= j < CHUNKS:
            moves[5, j].wait_recv()
            moves[9, j] = copy(9, j, rows_ref.at[at(6, j)], rows_ref.at[at(7, j)], core)
            moves[9, j].start()
        if i == 0:
            for fetch in fetches:
                fetch.wait()
        if i < CHUNKS:
            multiply(i)
    for i in range(CHUNKS):
        for kind in (6, 7, 8, 9):
            moves[kind, i].wait_recv()
    for made in log:
        made.wait_send()
    for store in stores:
        store.wait()


def call_spread_forward(part, tokens_own, gain, grad_rows, down):
    quarter, width = tokens_own.shape
    hidden = (grad_rows.shape[0], down.shape[0])
    hbm = pl.BlockSpec(memory_space=pl.ANY)
    return pl.pallas_call(
        spread_forward,
        in_specs=[*[WHOLE] * 3, hbm, hbm],
        out_specs=[WHOLE, WHOLE, hbm],
        out_shape=[
            jax.ShapeDtypeStruct((8 * quarter, width), BF16),
            jax.ShapeDtypeStruct((quarter, width), F32),
            jax.ShapeDtypeStruct(hidden, F32),
        ],
        scratch_shapes=[
            pltpu.VMEM((2 * quarter, width), BF16),
            pltpu.VMEM((quarter, width), BF16),
            pltpu.VMEM((quarter, width), BF16),
            pltpu.VMEM(grad_rows.shape, BF16),
            pltpu.VMEM(down.shape, BF16),
            pltpu.VMEM(hidden, F32),
            pltpu.SemaphoreType.DMA((10, CHUNKS)),
            pltpu.SemaphoreType.DMA((10, CHUNKS)),
            pltpu.SemaphoreType.DMA((2,)),
            pltpu.SemaphoreType.DMA((CHUNKS,)),
        ],
        compiler_params=pltpu.CompilerParams(
            collective_id=1, has_side_effects=True, vmem_limit_bytes=54 * 2**20
        ),
        cost_estimate=lasting(64),
        name="spread_forward",
    )(part, tokens_own, gain, grad_rows, down)


def pull_chunk(values, scale_gain, grad):
    scale = inverse_rms(values)
    turned = grad * scale_gain
    inner = jnp.mean(turned * values, -1, keepdims=True)
    return scale * turned - (scale * scale * scale) * values * inner, grad * values * scale


def spread_backward(part_ref, middle_ref, grad_ref, gain_ref, left_ref, both_ref, _, rows_ref, total_ref, gain_out_ref, up_ref, near_ref, side_out_ref, side_in_ref, far_out_ref, far_in_ref, left_in_ref, right_in_ref, up_out_ref, send_sems, recv_sems, fetch_sems, store_sems):
    units = right_in_ref.shape[1]
    fetches = [
        pltpu.make_async_copy(left_ref, left_in_ref, fetch_sems.at[0]),
        pltpu.make_async_copy(both_ref.at[:, pl.ds(units, units)], right_in_ref, fetch_sems.at[1]),
    ]
    for fetch in fetches:
        fetch.start()
    band = up_out_ref.shape[0] // CHUNKS
    stores = []

    def multiply(i):
        rows = pl.ds(i * band, band)
        up_out_ref[rows, :] = dot_tn(left_in_ref[:, rows], right_in_ref[...]).astype(BF16)
        stores.append(pltpu.make_async_copy(up_out_ref.at[rows], up_ref.at[rows], store_sems.at[i]))
        stores[-1].start()

    core, far, pair = partners_of()
    quarter, width = middle_ref.shape
    size = quarter // CHUNKS
    at = lambda slot, i: pl.ds(slot * quarter + i * size, size)
    greet([core, far, pair])
    log = []
    copy = sender(send_sems, recv_sems, log)
    near, side, sums, moves = {}, {}, {}, {}
    for i in range(CHUNKS):
        for k in (2, 3, 0, 1):
            near[k, i] = copy(k, i, part_ref.at[at(2 * k + 1, i)], near_ref.at[at(k, i)], core)
            near[k, i].start()

    def pairs(k, i):
        return part_ref[at(2 * k, i), :].astype(F32) + near_ref[at(k, i), :].astype(F32)

    def send_side(i):
        for k in (1, 0):
            near[2 + k, i].wait_recv()
            side_out_ref[at(k, i), :] = pairs(2 + k, i).astype(BF16)
            side[k, i] = copy(4 + k, i, side_out_ref.at[at(k, i)], side_in_ref.at[at(k, i)], pair)
            side[k, i].start()

    for i in range(AHEAD):
        send_side(i)
    gain_sum = jnp.zeros((1, width), F32)
    for i in range(CHUNKS + 2):
        if i + AHEAD < CHUNKS:
            send_side(i + AHEAD)
        if i < CHUNKS:
            near[1, i].wait_recv()
            side[1, i].wait_recv()
            far_out_ref[at(0, i), :] = (pairs(1, i) + side_in_ref[at(1, i), :].astype(F32)).astype(BF16)
            sums[i] = copy(6, i, far_out_ref.at[at(0, i)], far_in_ref.at[at(0, i)], far)
            sums[i].start()
        j = i - 1
        if 0 <= j < CHUNKS:
            near[0, j].wait_recv()
            side[0, j].wait_recv()
            sums[j].wait_recv()
            grad = pairs(0, j) + side_in_ref[at(0, j), :].astype(F32) + far_in_ref[at(0, j), :].astype(F32)
            back, gain_part = pull_chunk(middle_ref[at(0, j), :], gain_ref[0:1, :], grad)
            gain_sum = gain_sum + jnp.sum(gain_part, 0, keepdims=True)
            total = grad_ref[at(0, j), :].astype(F32) + back
            total_ref[at(0, j), :] = total
            rows_ref[at(0, j), :] = total.astype(BF16)
            own = rows_ref.at[at(0, j)]
            for kind, slot, device in ((7, 2, far), (8, 1, core)):
                moves[kind, j] = copy(kind, j, own, rows_ref.at[at(slot, j)], device)
                moves[kind, j].start()
        j = i - 2
        if 0 <= j < CHUNKS:
            moves[7, j].wait_recv()
            moves[9, j] = copy(9, j, rows_ref.at[at(2, j)], rows_ref.at[at(3, j)], core)
            moves[9, j].start()
        if i == 0:
            for fetch in fetches:
                fetch.wait()
        if i < CHUNKS:
            multiply(i)
    gain_out_ref[...] = jnp.broadcast_to(gain_sum, gain_out_ref.shape)
    for i in range(CHUNKS):
        for kind in (8, 9):
            moves[kind, i].wait_recv()
    for made in log:
        made.wait_send()
    for store in stores:
        store.wait()


def call_spread_backward(part, middle, grad_own, gain, left, both, ready):
    quarter, width = middle.shape
    units = both.shape[1] // 2
    hbm = pl.BlockSpec(memory_space=pl.ANY)
    return pl.pallas_call(
        spread_backward,
        in_specs=[*[WHOLE] * 4, hbm, hbm, hbm],
        out_specs=[*[WHOLE] * 3, hbm],
        out_shape=[
            jax.ShapeDtypeStruct((4 * quarter, width), BF16),
            jax.ShapeDtypeStruct((quarter, width), F32),
            jax.ShapeDtypeStruct((8, width), F32),
            jax.ShapeDtypeStruct((width, units), BF16),
        ],
        scratch_shapes=[
            pltpu.VMEM((4 * quarter, width), BF16),
            pltpu.VMEM((2 * quarter, width), BF16),
            pltpu.VMEM((2 * quarter, width), BF16),
            pltpu.VMEM((quarter, width), BF16),
            pltpu.VMEM((quarter, width), BF16),
            pltpu.VMEM(left.shape, BF16),
            pltpu.VMEM((left.shape[0], units), BF16),
            pltpu.VMEM((width, units), BF16),
            pltpu.SemaphoreType.DMA((10, CHUNKS)),
            pltpu.SemaphoreType.DMA((10, CHUNKS)),
            pltpu.SemaphoreType.DMA((2,)),
            pltpu.SemaphoreType.DMA((CHUNKS,)),
        ],
        compiler_params=pltpu.CompilerParams(
            collective_id=2, has_side_effects=True, vmem_limit_bytes=56 * 2**20
        ),
        cost_estimate=lasting(68),
        name="spread_backward",
    )(part, middle, grad_own, gain, left, both, ready)


def finish(line, part_ref, tokens_ref, total_ref, gain_ref, *refs):
    gain_two_ref, grads_refs, refs = refs[0], refs[1:3], refs[4:]
    input_ref, gain_out_ref, *owned_refs = refs[:4]
    rows_ref, near_ref, far_out_ref, far_in_ref, refs = *refs[4:8], refs[1:]
    side_in_refs, up_out_refs, up_in_refs, down_out_refs, down_in_refs = (refs[k : k + 2] for k in range(7, 17, 2))
    send_sems, recv_sems, side_send, side_recv, line_send, line_recv, *exchange = refs[17:]
    core, far, pair = partners_of()
    index = lax.axis_index("dp")
    place, side = index // 2, index % 2
    above, below = {"dp": index + 2}, {"dp": index - 2}
    quarter, width = tokens_ref.shape
    size = quarter // CHUNKS
    last = line - 1
    at = lambda slot, i: pl.ds(slot * quarter + i * size, size)

    def block(w, where, which):
        rows = owned_refs[w].shape[0]
        return pl.ds((where * 2 + which) * rows, rows)


    everyone = Everyone(line, *exchange)
    greet(everyone.partners())
    log = []
    copy = sender(send_sems, recv_sems, log)
    near, sums, moves = {}, {}, {}
    for i in range(CHUNKS):
        for k in (1, 0):
            near[k, i] = copy(k, i, part_ref.at[at(2 * k + 1, i)], near_ref.at[at(k, i)], core)
            near[k, i].start()

    def side_copy(w, where):
        return pltpu.make_async_remote_copy(
            src_ref=grads_refs[w].at[block(w, where, 1 - side)],
            dst_ref=side_in_refs[w].at[where],
            send_sem=side_send.at[w, where],
            recv_sem=side_recv.at[w, where],
            device_id=pair,
            device_id_type=MESH,
        )

    def line_copy(w, upward, step):
        out_ref, in_ref = (up_out_refs[w], up_in_refs[w]) if upward else (down_out_refs[w], down_in_refs[w])
        way = 0 if upward else 1
        return pltpu.make_async_remote_copy(
            src_ref=out_ref.at[step - 1],
            dst_ref=in_ref.at[step - 1],
            send_sem=line_send.at[w, way, step - 1],
            recv_sem=line_recv.at[w, way, step - 1],
            device_id=above if upward else below,
            device_id_type=MESH,
        )

    for step in range(last, 0, -1):

        @pl.when(place + step <= last)
        def _(step=step):
            for w in range(2):
                side_copy(w, place + step).start()

        @pl.when(place - step >= 0)
        def _(step=step):
            for w in range(2):
                side_copy(w, place - step).start()

    for w in range(2):
        side_copy(w, place).start()

    for i in range(CHUNKS):
        near[1, i].wait_recv()
        summed = part_ref[at(2, i), :].astype(F32) + near_ref[at(1, i), :].astype(F32)
        far_out_ref[at(0, i), :] = summed.astype(BF16)
        sums[i] = copy(2, i, far_out_ref.at[at(0, i)], far_in_ref.at[at(0, i)], far)
        sums[i].start()

    def term(w, where):
        return grads_refs[w][block(w, where, side), :].astype(F32) + side_in_refs[w][where].astype(F32)

    def line_step(step):
        for w in range(2):

            @pl.when(place + step <= last)
            def _(w=w):
                side_copy(w, place + step).wait_recv()
                value = term(w, place + step)
                up_out_refs[w][step - 1] = value.astype(BF16)
                if step < last:

                    @pl.when(place > 0)
                    def _():
                        line_copy(w, True, step + 1).wait_recv()
                        up_out_refs[w][step - 1] = (value + up_in_refs[w][step].astype(F32)).astype(BF16)

                line_copy(w, True, step).start()

            @pl.when(place - step >= 0)
            def _(w=w):
                side_copy(w, place - step).wait_recv()
                value = term(w, place - step)
                down_out_refs[w][step - 1] = value.astype(BF16)
                if step < last:

                    @pl.when(place < last)
                    def _():
                        line_copy(w, False, step + 1).wait_recv()
                        down_out_refs[w][step - 1] = (value + down_in_refs[w][step].astype(F32)).astype(BF16)

                line_copy(w, False, step).start()

    def settle(slot, i):
        start = pl.multiple_of((lax.axis_index("mp") ^ slot) * quarter + i * size, size)
        input_ref[pl.ds(start, size), :] = rows_ref[at(slot, i), :].astype(F32)

    gain_sum = jnp.zeros((1, width), F32)
    steps = list(range(last, 0, -1))
    for i in range(CHUNKS + 1):
        if i < CHUNKS:
            near[0, i].wait_recv()
            sums[i].wait_recv()
            grad = (
                part_ref[at(0, i), :].astype(F32)
                + near_ref[at(0, i), :].astype(F32)
                + far_in_ref[at(0, i), :].astype(F32)
            )
            back, gain_part = pull_chunk(tokens_ref[at(0, i), :].astype(F32), gain_ref[0:1, :], grad)
            gain_sum = gain_sum + jnp.sum(gain_part, 0, keepdims=True)
            rows_ref[at(0, i), :] = (total_ref[at(0, i), :] + back).astype(BF16)
            settle(0, i)
            own = rows_ref.at[at(0, i)]
            for kind, slot, device in ((3, 2, far), (4, 1, core)):
                moves[kind, i] = copy(kind, i, own, rows_ref.at[at(slot, i)], device)
                moves[kind, i].start()
        if steps:
            line_step(steps.pop(0))
        j = i - 1
        if 0 <= j < CHUNKS:
            moves[3, j].wait_recv()
            settle(2, j)
            moves[5, j] = copy(5, j, rows_ref.at[at(2, j)], rows_ref.at[at(3, j)], core)
            moves[5, j].start()
    while steps:
        line_step(steps.pop(0))
    columns = gain_out_ref.shape[1]
    for r in range(4):
        cut = slice(r * columns, (r + 1) * columns)
        everyone.near_ref[everyone.code, r : r + 1, :] = gain_sum[:, cut]
        everyone.near_ref[everyone.code, r + 4 : r + 5, :] = gain_two_ref[0:1, cut]
    everyone.send_near()
    everyone.send_line(everyone.add)
    for w in range(2):
        side_copy(w, place).wait_recv()
        owned_refs[w][...] = term(w, place)

        @pl.when(place > 0)
        def _(w=w):
            line_copy(w, True, 1).wait_recv()
            owned_refs[w][...] += up_in_refs[w][0].astype(F32)

        @pl.when(place < last)
        def _(w=w):
            line_copy(w, False, 1).wait_recv()
            owned_refs[w][...] += down_in_refs[w][0].astype(F32)

    gain_out_ref[...] = everyone.result(everyone.add)
    for i in range(CHUNKS):
        for kind, slot in ((4, 1), (5, 3)):
            moves[kind, i].wait_recv()
            settle(slot, i)
    for made in log:
        made.wait_send()
    for w in range(2):
        for where in range(line):
            side_copy(w, where).wait_send()
        for step in range(last, 0, -1):

            @pl.when(place + step <= last)
            def _(w=w, step=step):
                line_copy(w, True, step).wait_send()

            @pl.when(place - step >= 0)
            def _(w=w, step=step):
                line_copy(w, False, step).wait_send()


def call_finish(dp_size, part, tokens_own, total, gain, gain_two, ready, *grads):
    quarter, width = tokens_own.shape
    line = dp_size // 2
    owned = [(grad.shape[0] // dp_size, grad.shape[1]) for grad in grads]
    stacks = lambda count: [pltpu.VMEM((count, *shape), BF16) for shape in owned]
    return pl.pallas_call(
        functools.partial(finish, line),
        in_specs=[*[WHOLE] * 7, pl.BlockSpec(memory_space=pl.ANY)],
        out_specs=[WHOLE] * 4,
        out_shape=[
            jax.ShapeDtypeStruct((4 * quarter, width), F32),
            jax.ShapeDtypeStruct((8, width // 4), F32),
            *[jax.ShapeDtypeStruct(shape, F32) for shape in owned],
        ],
        scratch_shapes=[
            pltpu.VMEM((4 * quarter, width), BF16),
            pltpu.VMEM((2 * quarter, width), BF16),
            pltpu.VMEM((quarter, width), BF16),
            pltpu.VMEM((quarter, width), BF16),
            *stacks(line),
            *stacks(line - 1),
            *stacks(line - 1),
            *stacks(line - 1),
            *stacks(line - 1),
            pltpu.SemaphoreType.DMA((6, CHUNKS)),
            pltpu.SemaphoreType.DMA((6, CHUNKS)),
            pltpu.SemaphoreType.DMA((2, line)),
            pltpu.SemaphoreType.DMA((2, line)),
            pltpu.SemaphoreType.DMA((2, 2, line)),
            pltpu.SemaphoreType.DMA((2, 2, line)),
            *Everyone.scratch(line, (8, width // 4)),
        ],
        compiler_params=pltpu.CompilerParams(
            collective_id=3, has_side_effects=True, vmem_limit_bytes=56 * 2**20
        ),
        cost_estimate=lasting(85),
        name="finish",
    )(part, tokens_own, total, gain, gain_two, *grads, ready)


def gather_weights(line, own_ref, out_ref, gains_ref, grad_ref, full_ref, out_full_ref, gains_full_ref, rows_ref, local_sems, side_send, side_recv, line_send, line_recv, rows_send, rows_recv, staged_ref):
    index = lax.axis_index("dp")
    place, side = index // 2, index % 2
    pair, above, below = {"dp": index ^ 1}, {"dp": index + 2}, {"dp": index - 2}
    rank = lax.axis_index("mp")
    core, far = {"mp": rank ^ 1}, {"mp": rank ^ 2}
    quarter = grad_ref.shape[0] // 4
    slot_of = lambda k: rows_ref.at[pl.ds(k * quarter, quarter)]
    quarter_of = lambda k: grad_ref.at[pl.ds((rank ^ k) * quarter, quarter)]
    last = line - 1
    owns, fulls = (own_ref, out_ref, gains_ref), (full_ref, out_full_ref, gains_full_ref)
    all_three = range(3)

    barrier = pltpu.get_barrier_semaphore()
    pl.semaphore_signal(barrier, inc=1, device_id=pair, device_id_type=MESH)
    pl.semaphore_signal(barrier, inc=1, device_id=core, device_id_type=MESH)
    pl.semaphore_signal(barrier, inc=1, device_id=far, device_id_type=MESH)

    @pl.when(place < last)
    def _():
        pl.semaphore_signal(barrier, inc=1, device_id=above, device_id_type=MESH)

    @pl.when(place > 0)
    def _():
        pl.semaphore_signal(barrier, inc=1, device_id=below, device_id_type=MESH)

    pl.semaphore_wait(barrier, 3 + (place < last).astype(jnp.int32) + (place > 0).astype(jnp.int32))

    def slot(which, where, side):
        rows = owns[which].shape[0]
        return fulls[which].at[pl.ds((where * 2 + side) * rows, rows)]

    def views(which, where):
        return slot(which, where, side)

    def source(which, where, first):
        return owns[which] if first else views(which, where)

    def line_copy(which, upward, where, first=False):
        way = 0 if upward else 1
        return pltpu.make_async_remote_copy(
            src_ref=source(which, where, first),
            dst_ref=views(which, where),
            send_sem=line_send.at[which, way, where],
            recv_sem=line_recv.at[which, way, where],
            device_id=above if upward else below,
            device_id_type=MESH,
        )

    def side_copy(which, where, first=False):
        return pltpu.make_async_remote_copy(
            src_ref=source(which, where, first),
            dst_ref=views(which, where),
            send_sem=side_send.at[which, where],
            recv_sem=side_recv.at[which, where],
            device_id=pair,
            device_id_type=MESH,
        )

    def side_arrival(which, where):
        target = slot(which, where, 1 - side)
        return pltpu.make_async_remote_copy(
            src_ref=target,
            dst_ref=target,
            send_sem=side_send.at[which, where],
            recv_sem=side_recv.at[which, where],
            device_id=pair,
            device_id_type=MESH,
        )

    @pl.when(place < last)
    def _():
        for which in all_three:
            line_copy(which, True, place, True).start()

    @pl.when(place > 0)
    def _():
        for which in all_three:
            line_copy(which, False, place, True).start()

    for which in all_three:
        side_copy(which, place, True).start()
    here = [pltpu.make_async_copy(source(w, place, True), views(w, place), local_sems.at[w]) for w in all_three]
    for made in here:
        made.start()
    staged_of = lambda k: staged_ref.at[pl.ds(k * quarter, quarter)]
    fetches = [pltpu.make_async_copy(quarter_of(k), staged_of(k), local_sems.at[3 + k]) for k in range(4)]
    stores = [pltpu.make_async_copy(staged_of(k), slot_of(k), local_sems.at[7 + k]) for k in range(4)]
    for made in fetches:
        made.start()

    def rows_copy(number, source, target, device):
        return pltpu.make_async_remote_copy(
            src_ref=source,
            dst_ref=target,
            send_sem=rows_send.at[number],
            recv_sem=rows_recv.at[number],
            device_id=device,
            device_id_type=MESH,
        )

    over = rows_copy(0, quarter_of(0), slot_of(4), pair)
    across = rows_copy(1, slot_of(4), slot_of(6), far)
    near = [rows_copy(2 + k, slot_of(4 + 2 * k), slot_of(5 + 2 * k), core) for k in range(2)]
    over.start()

    for step in range(1, line):

        @pl.when(place - step >= 0)
        def _(step=step):
            where = place - step
            for which in all_three:
                line_copy(which, True, where).wait_recv()

                @pl.when(place < last)
                def _(which=which):
                    line_copy(which, True, where).start()

                side_copy(which, where).start()

        @pl.when(place + step <= last)
        def _(step=step):
            where = place + step
            for which in all_three:
                line_copy(which, False, where).wait_recv()

                @pl.when(place > 0)
                def _(which=which):
                    line_copy(which, False, where).start()

                side_copy(which, where).start()

        if step == 1:
            for fetch, store in zip(fetches, stores):
                fetch.wait()
                store.start()
            over.wait_recv()
            across.start()
            near[0].start()

    across.wait_recv()
    near[1].start()
    for made in here + stores:
        made.wait()
    for where in range(line):
        for which in all_three:
            side_arrival(which, where).wait_recv()
            side_copy(which, where).wait_send()

            @pl.when((where <= place) & (place < last))
            def _(which=which, where=where):
                line_copy(which, True, where).wait_send()

            @pl.when((where >= place) & (place > 0))
            def _(which=which, where=where):
                line_copy(which, False, where).wait_send()

    for k in range(2):
        near[k].wait_recv()
        near[k].wait_send()
    over.wait_send()
    across.wait_send()


def call_gather_weights(dp_size, grads, *owns):
    line = dp_size // 2
    hbm = pl.BlockSpec(memory_space=pl.ANY)
    return pl.pallas_call(
        functools.partial(gather_weights, line),
        in_specs=[hbm] * 4,
        out_specs=[hbm] * 4,
        out_shape=[
            *[jax.ShapeDtypeStruct((dp_size * own.shape[0], own.shape[1]), own.dtype) for own in owns],
            jax.ShapeDtypeStruct((2 * grads.shape[0], grads.shape[1]), grads.dtype),
        ],
        scratch_shapes=[
            pltpu.SemaphoreType.DMA((11,)),
            pltpu.SemaphoreType.DMA((3, line)),
            pltpu.SemaphoreType.DMA((3, line)),
            pltpu.SemaphoreType.DMA((3, 2, line)),
            pltpu.SemaphoreType.DMA((3, 2, line)),
            pltpu.SemaphoreType.DMA((4,)),
            pltpu.SemaphoreType.DMA((4,)),
            pltpu.VMEM(grads.shape, grads.dtype),
        ],
        compiler_params=pltpu.CompilerParams(
            collective_id=4, has_side_effects=True, vmem_limit_bytes=16 * 2**20
        ),
        cost_estimate=lasting(120),
        name="gather_weights",
    )(*owns, grads)


def combine_all(line, early_ref, small_ref, gate_up_ref, out_ref, *exchange):
    everyone = Everyone(line, *exchange)
    greet(everyone.partners())
    lanes = lax.broadcasted_iota(jnp.int32, early_ref.shape, 1)
    adds = lax.broadcasted_iota(jnp.int32, early_ref.shape, 0) < 8
    fold = lambda left, right: jnp.where(adds, left + right, jnp.maximum(left, right))
    value = early_ref[...]
    gate_up = jnp.sum(jnp.sum(gate_up_ref[...], 0, keepdims=True), 1, keepdims=True)
    terms = [small_ref[k : k + 1, :] for k in range(SMALL)] + [jnp.broadcast_to(gate_up, (1, HEAD))]
    for term, number in zip(terms, (0, 1, 2, 3, 6, 4)):
        value = jnp.where(adds & (lanes == 7 + number), term, value)
    everyone.near_ref[everyone.code] = value
    everyone.send_near()
    everyone.send_line(fold)
    out_ref[...] = everyone.result(fold)


def call_combine_all(dp_size, early, small, gate_up):
    line = dp_size // 2
    return pl.pallas_call(
        functools.partial(combine_all, line),
        in_specs=[WHOLE] * 3,
        out_specs=WHOLE,
        out_shape=jax.ShapeDtypeStruct(early.shape, F32),
        scratch_shapes=Everyone.scratch(line, early.shape),
        compiler_params=pltpu.CompilerParams(collective_id=6, has_side_effects=True),
        cost_estimate=lasting(10),
        name="combine_all",
    )(early, small, gate_up)


class Links:
    def __init__(self, dp_size, mp_size):
        self.dp, self.mp, self.line = dp_size, mp_size, dp_size // 2
        self.index = lax.axis_index("dp")
        self.place, self.side, self.rank = self.index // 2, self.index % 2, lax.axis_index("mp")
        self.lines = [[place * 2 + side for place in range(self.line)] for side in range(2)]

    def swap_mp(self, value, bit):
        return lax.ppermute(value, "mp", [(i, i ^ bit) for i in range(self.mp)])

    def swap_side(self, value):
        return lax.ppermute(value, "dp", [(i, i ^ 1) for i in range(self.dp)])

    def gather_line(self, own):
        return lax.all_gather(own, "dp", axis=0, tiled=True, axis_index_groups=self.lines)

    def sum_line(self, parts):
        return lax.psum_scatter(parts, "dp", scatter_dimension=0, tiled=True, axis_index_groups=self.lines)


    def to_slots(self, values):
        rows = values.shape[0] // self.mp
        return jnp.concatenate(
            [lax.dynamic_slice_in_dim(values, (self.rank ^ k) * rows, rows, 0) for k in range(self.mp)], 0
        )

    def from_slots(self, values):
        rows = values.shape[0] // self.mp
        cuts = [values[k * rows : (k + 1) * rows] for k in range(self.mp)]
        odd = (self.rank & 1) == 1
        high = (self.rank & 2) == 2
        cuts = [jnp.where(odd, cuts[k ^ 1], cuts[k]) for k in range(self.mp)]
        cuts = [jnp.where(high, cuts[k ^ 2], cuts[k]) for k in range(self.mp)]
        return jnp.concatenate(cuts, 0)

    def gather_core(self, quarter, far):
        rows = quarter.shape[0]
        near = self.swap_mp(jnp.concatenate([quarter, far], 0), 1)
        return jnp.concatenate([quarter, near[:rows], far, near[rows:]], 0)

    def swap_core(self, slots):
        rows = slots.shape[0] // 8
        picked = lambda ks: jnp.concatenate([slots[k * rows : (k + 1) * rows] for k in ks], 0)
        return slots, self.swap_mp(picked((1, 3, 5, 7)), 1)

    def sum_core(self, slots, near):
        rows = slots.shape[0] // 8
        add = lambda ks, low: jnp.concatenate(
            [
                slots[k * rows : (k + 1) * rows].astype(F32) + near[i * rows : (i + 1) * rows].astype(F32)
                for i, k in enumerate(ks, low)
            ],
            0,
        ).astype(BF16)
        return add((0, 2), 0), add((4,), 2), add((6,), 3)


def after(value, *others):
    return lax.optimization_barrier((value, *others))[0]


def inverse_rms(values):
    return lax.rsqrt(jnp.mean(values * values, -1, keepdims=True) + NORM_EPS)


def body(
    dp_size,
    mp_size,
    tokens,
    cotangent,
    segment_ids,
    w_query,
    w_key,
    w_value,
    w_out,
    w_gate_up,
    w_down,
    norm_gains,
    query_moments,
    key_moments,
    value_moments,
    out_moments,
    gate_up_moments,
    down_moments,
    gains_moments,
):
    links = Links(dp_size, mp_size)
    line, side = links.line, links.side
    heads = w_query.shape[1] // HEAD
    kvs = w_key.shape[1] // HEAD
    group = heads // kvs
    width = tokens.shape[1]
    shard = w_query.shape[0]
    units = w_gate_up.shape[2]
    block = units // (line * 2)

    def interleave(query, key, value):
        parts = []
        for kv in range(kvs):
            parts.append(query[..., kv * group * HEAD : (kv + 1) * group * HEAD])
            parts.append(key[..., kv * HEAD : (kv + 1) * HEAD])
            parts.append(value[..., kv * HEAD : (kv + 1) * HEAD])
        return jnp.concatenate(parts, -1)

    by_side = w_gate_up.reshape(2, shard, line, 2, block)

    def side_units(which):
        cut = lax.dynamic_index_in_dim(by_side, which, 3, keepdims=False).astype(BF16)
        return jnp.concatenate([cut[0].reshape(shard, -1), cut[1].reshape(shard, -1)], 1)

    token_slots = links.to_slots(tokens)
    inputs = token_slots.astype(F32)
    scale_one = inverse_rms(inputs)
    down_full = links.gather_line(w_down.astype(BF16))
    own_units = side_units(side)
    sent_units = links.swap_side(side_units(1 - side))
    rows_pair = jnp.zeros((2 * shard, own_units.shape[1]), BF16)
    rows_pair = lax.dynamic_update_slice(rows_pair, own_units, (side * shard, 0))
    rows_pair = lax.dynamic_update_slice(rows_pair, sent_units, ((1 - side) * shard, 0))
    gate_up_full = after(links.gather_line(rows_pair), down_full)
    gains_low = norm_gains.astype(BF16).astype(F32)
    gains_rows = jnp.concatenate([gains_low, jnp.zeros((6, gains_low.shape[1]), F32)], 0)
    qkv_full, out_full, gains_shards, grad_rows = call_gather_weights(
        dp_size,
        cotangent,
        after(interleave(w_query, w_key, w_value).astype(BF16), rows_pair, scale_one, token_slots),
        w_out.astype(BF16),
        gains_rows,
    )
    gains_full = jnp.transpose(gains_shards.reshape(dp_size, 8, -1), (1, 0, 2)).reshape(8, width)

    quarter = tokens.shape[0] // 4

    cosine, sine = rope_tables(segment_ids.shape[1])
    normed_one = (inputs * scale_one * gains_full[0]).astype(BF16)
    qkv = jnp.dot(normed_one, qkv_full, preferred_element_type=F32)
    rank_ref = links.rank.astype(jnp.int32).reshape(1)
    mixed_slots, rotated, lse, peaks = attention_forward(rank_ref, qkv, cosine, sine, segment_ids, group, kvs)
    tokens_own = token_slots[:quarter]
    rows_two, middle, grad_hidden = call_spread_forward(
        jnp.dot(mixed_slots, out_full, preferred_element_type=F32).astype(BF16),
        tokens_own,
        gains_full[1:2],
        grad_rows,
        down_full,
    )

    columns = line * block
    both = jnp.dot(rows_two, gate_up_full, preferred_element_type=F32)
    hidden, grad_both = call_gate_rows(both, grad_hidden)
    grad_down_part = dot_tn(hidden, grad_rows).astype(BF16)
    output_part = jnp.dot(after(hidden, grad_down_part), down_full, preferred_element_type=F32).astype(BF16)
    output_part, output_near = links.swap_core(output_part)
    output_mine, output_other, output_theirs = links.sum_core(output_part, after(output_near, grad_down_part))
    output_second = links.swap_side(output_theirs)
    grad_gate_part = dot_tn(rows_two, grad_both[:, :columns]).astype(BF16)
    output_first = links.swap_side(output_other)
    back = dot_nt(after(grad_both, grad_gate_part), gate_up_full).astype(BF16)
    grad_middle_slots, grad_middle, gain_two, grad_up_part = call_spread_backward(
        back, middle, grad_rows[:quarter], gains_full[1:2], rows_two, grad_both, output_second
    )
    output_second = output_mine[quarter:].astype(F32) + after(output_second, back).astype(F32)
    output_far = links.swap_mp(after(output_second.astype(BF16), grad_middle_slots), 2)
    grad_down_low = links.sum_line(grad_down_part)
    gate_sum = after(links.sum_line(grad_gate_part), grad_down_low)
    up_sum = after(links.sum_line(grad_up_part), gate_sum)
    grad_mixed = dot_nt(grad_middle_slots, out_full).astype(BF16)

    grad_down = grad_down_low.astype(F32)
    down_second, down_direction = lamb_direction(w_down, down_moments[0], down_moments[1], grad_down)
    down_sum = jnp.sum(down_direction * down_direction)

    local_peak = peaks[:, :group, 0].reshape(heads)
    peak_vector = lax.dynamic_update_slice(
        jnp.full((HEADS,), MASKED, F32), local_peak, (links.rank * heads,)
    )
    owner = (links.rank == 0).astype(F32)
    lanes = lax.broadcasted_iota(jnp.int32, (16, HEAD), 1)
    lower = lax.broadcasted_iota(jnp.int32, (16, HEAD), 0) < 8
    early = jnp.broadcast_to(jnp.pad(peak_vector, (0, HEAD - HEADS), constant_values=MASKED), (16, HEAD))
    early = jnp.where(lower, 0.0, early)
    masters = (w_query, w_key, w_value, w_out, w_gate_up, w_down, norm_gains)
    for number, master in enumerate(masters):
        square = jnp.sum(master * master) * (owner if number == 6 else 1.0)
        early = jnp.where(lower & (lanes == number), square, early)
    early = jnp.where(lower & (lanes == 12), down_sum, early)

    grad_qkv = attention_backward(rank_ref, rotated, grad_mixed, lse, cosine, sine, segment_ids, group, kvs)
    grad_qkv_part = dot_tn(normed_one, grad_qkv).astype(BF16)
    grad_out_part = dot_tn(mixed_slots, grad_middle_slots).astype(BF16)
    grad_normed_one = dot_nt(grad_qkv, qkv_full).astype(BF16)
    input_grad, gain_terms, grad_qkv_own, grad_out = call_finish(
        dp_size,
        after(grad_normed_one, gate_sum),
        tokens_own,
        grad_middle,
        gains_full[0:1],
        gain_two,
        output_first,
        grad_qkv_part,
        grad_out_part,
    )
    output_far = after(output_far, input_grad).astype(F32)
    output_low = (middle + output_mine[:quarter].astype(F32) + output_first.astype(F32) + output_far).astype(BF16)
    output_far = links.swap_mp(output_low, 2)

    summed = [gate_sum, up_sum]
    side_ref = side.astype(jnp.int32).reshape(1)
    theirs = [
        links.swap_side(call_pick_rows(side_ref, value, ready))
        for value, ready in ((gate_sum, grad_qkv), (up_sum, gain_terms))
    ]
    gain_terms = gain_terms.reshape(2, width)
    gain_width = norm_gains.shape[1]
    grad_gains = lax.dynamic_slice_in_dim(gain_terms, links.index * gain_width, gain_width, 1)

    small = (w_query, w_key, w_value, w_out, norm_gains)
    small_moments = (query_moments, key_moments, value_moments, out_moments, gains_moments)
    grad_query, grad_key, grad_value, *rest = call_small_step(
        group, kvs, jnp.full((1, HEAD), owner), grad_qkv_own, grad_out, grad_gains, small, small_moments
    )
    theirs = [after(value, grad_query, down_direction, early, output_low) for value in theirs]
    small_seconds, small_directions, small_sums = rest[:SMALL], rest[SMALL : 2 * SMALL], rest[2 * SMALL]
    if block % HEAD == 0:
        grad_gate_up, gate_up_second, gate_up_direction, gate_up_sums = call_gate_up_step(
            line, side.astype(jnp.int32).reshape(1), w_gate_up, gate_up_moments, summed, theirs
        )
    else:
        parts = []
        for j in range(2):
            mine = lax.dynamic_slice_in_dim(summed[j], side * shard, shard, 0)
            sides = [jnp.where(side == 0, mine, theirs[j]), jnp.where(side == 0, theirs[j], mine)]
            parts.append(jnp.stack([value.reshape(shard, line, block) for value in sides], 2))
        grad_gate_up = jnp.stack(parts, 0).reshape(w_gate_up.shape)
        grad_gate_up = grad_gate_up.astype(F32)
        gate_up_second, gate_up_direction = lamb_direction(
            w_gate_up, gate_up_moments[0], gate_up_moments[1], grad_gate_up
        )
        gate_up_sums = jnp.sum((gate_up_direction * gate_up_direction).reshape(-1, 8, 2 * HEAD), 0)
    output_far = after(output_far, gate_up_sums)
    block_output = links.from_slots(links.gather_core(output_low, output_far))
    packed = call_combine_all(dp_size, early, small_sums, gate_up_sums)
    updated = call_small_update(
        group, kvs, links.rank.astype(jnp.int32).reshape(1), packed, small, small_directions
    )
    flat_rows = lambda value: value.reshape(2 * shard, units)
    new_gate_up, copy_gate_up = (
        value.reshape(w_gate_up.shape)
        for value in call_large_update(4, packed, flat_rows(w_gate_up), flat_rows(gate_up_direction))
    )
    new_down, copy_down = call_large_update(5, packed, w_down, down_direction)
    grads = (grad_query, grad_key, grad_value, grad_out, grad_gate_up, grad_down, grad_gains)
    place_large = lambda values, gate_up, down: (*values[:4], gate_up, down, values[4])
    norms = jnp.sqrt(jnp.stack([packed[0, :7], packed[0, 7:14]]))
    return (
        block_output,
        input_grad,
        *grads,
        *place_large(small_seconds, gate_up_second, down_second),
        *place_large(updated[:SMALL], new_gate_up, new_down),
        *place_large(updated[SMALL:], copy_gate_up, copy_down),
        norms,
        packed[8, :HEADS],
    )


def solution(mesh):
    column = P("dp", "mp")
    row = P(("mp", "dp"), None)
    gate_up = P(None, "dp", "mp")
    gains = P(None, "dp")
    params = (column, column, column, row, gate_up, row, gains)
    moments = (
        P(None, "dp", "mp"),
        P(None, "dp", "mp"),
        P(None, "dp", "mp"),
        P(None, ("mp", "dp"), None),
        P(None, None, "dp", "mp"),
        P(None, ("mp", "dp"), None),
        P(None, None, "dp"),
    )
    tokens = P("dp", None)
    return jax.shard_map(
        functools.partial(body, mesh.shape["dp"], mesh.shape["mp"]),
        mesh=mesh,
        in_specs=(tokens, tokens, tokens, *params, *moments),
        out_specs=(tokens, tokens, *params, *params, *params, *params, P(), P()),
        check_vma=False,
    )
```

```python
import functools
import math

import jax
import jax.numpy as jnp
from jax import lax
from jax.experimental import pallas as pl
from jax.experimental.pallas import tpu as pltpu
from jax.sharding import PartitionSpec as P

HEADS = 16
HEAD = 128
BLOCK = 512
CLIP = 10
TILE = 256

NORM_EPS = 1e-05
ROPE_BASE = 1000000.0
RATE = 0.4
DECAY = 0.5
WEIGHT_DECAY = 0.01
STEP_EPS = 1e-06
MASKED = -1e30

F32 = jnp.float32
BF16 = jnp.bfloat16


def rope_tables(length):
    positions = jnp.arange(length, dtype=F32)
    frequency = ROPE_BASE ** (-(jnp.arange(HEAD // 2, dtype=F32) * 2.0) / HEAD)
    angles = positions[:, None] * frequency[None, :]
    cosine, sine = jnp.cos(angles), jnp.sin(angles)
    return jnp.concatenate([cosine, cosine], 1), jnp.concatenate([-sine, sine], 1)


def lasting(microseconds):
    return pl.CostEstimate(flops=0, bytes_accessed=int(microseconds * 3e6), transcendentals=0)


def turn(values, cosine, sine):
    return values * cosine + pltpu.roll(values, HEAD // 2, 1) * sine


def allowed_mask(seg_row_ref, seg_col_ref, row_start, low, high):
    query_pos = row_start + lax.broadcasted_iota(jnp.int32, (TILE, high - low), 0)
    key_pos = low + lax.broadcasted_iota(jnp.int32, (TILE, high - low), 1)
    same = seg_col_ref[row_start : row_start + TILE, :] == seg_row_ref[0, :, low:high]
    return (key_pos <= query_pos) & same


def dot_nt(left, right):
    return lax.dot_general(left, right, (((1,), (1,)), ((), ())), preferred_element_type=F32)


def dot_nn(left, right):
    return lax.dot_general(left, right, (((1,), (0,)), ((), ())), preferred_element_type=F32)


def dot_tn(left, right):
    return lax.dot_general(left, right, (((0,), (0,)), ((), ())), preferred_element_type=F32)


def slot_rows(rank_ref, start):
    return pl.ds(pl.multiple_of(((start // TILE) ^ rank_ref[0]) * TILE, TILE), TILE)


def attend_forward(group, rank_ref, qkv_ref, cos_ref, sin_ref, seg_row_ref, seg_col_ref, out_ref, rot_ref, lse_ref, peak_ref):
    length = qkv_ref.shape[0]
    scale = 1.0 / math.sqrt(HEAD)
    value_columns = slice((group + 1) * HEAD, (group + 2) * HEAD)
    for start in range(0, length, TILE):
        rows, source = slice(start, start + TILE), slot_rows(rank_ref, start)
        for part in range(group + 1):
            columns = slice(part * HEAD, (part + 1) * HEAD)
            turned = turn(qkv_ref[source, columns], cos_ref[rows, :], sin_ref[rows, :])
            rot_ref[rows, columns] = turned.astype(BF16)
        rot_ref[rows, value_columns] = qkv_ref[source, value_columns].astype(BF16)
    key_columns = slice(group * HEAD, (group + 1) * HEAD)
    peak_ref[...] = jnp.full(peak_ref.shape, MASKED, F32)
    peaks = [None] * group
    for start in range(0, length, TILE):
        low, high = max(0, start - BLOCK), start + TILE
        rows = slice(start, start + TILE)
        mask = allowed_mask(seg_row_ref, seg_col_ref, start, low, high)
        keys = rot_ref[low:high, key_columns]
        values = rot_ref[low:high, value_columns]
        for head in range(group):
            columns = slice(head * HEAD, (head + 1) * HEAD)
            scores = jnp.where(mask, dot_nt(rot_ref[rows, columns], keys) * scale, MASKED)
            top = jnp.max(scores, 1, keepdims=True)
            exponent = jnp.exp(scores - top)
            total = jnp.sum(exponent, 1, keepdims=True)
            probs = (exponent * (1.0 / total)).astype(BF16)
            out_ref[slot_rows(rank_ref, start), columns] = dot_nn(probs, values).astype(BF16)
            lse_ref[rows, columns] = jnp.broadcast_to(top + jnp.log(total), (TILE, HEAD))
            peak = jnp.max(top, 0, keepdims=True)
            peaks[head] = peak if peaks[head] is None else jnp.maximum(peaks[head], peak)
    for head in range(group):
        peak_ref[0, head : head + 1, :] = jnp.broadcast_to(peaks[head], (1, HEAD))


def attend_backward(group, rank_ref, rot_ref, grad_ref, lse_ref, cos_ref, sin_ref, seg_row_ref, seg_col_ref, out_ref, dk_ref, dv_ref):
    length = rot_ref.shape[0]
    scale = 1.0 / math.sqrt(HEAD)
    key_columns = slice(group * HEAD, (group + 1) * HEAD)
    value_columns = slice((group + 1) * HEAD, (group + 2) * HEAD)
    dk_ref[...] = jnp.zeros(dk_ref.shape, F32)
    dv_ref[...] = jnp.zeros(dv_ref.shape, F32)
    for start in range(0, length, TILE):
        low, high = max(0, start - BLOCK), start + TILE
        rows = slice(start, start + TILE)
        mask = allowed_mask(seg_row_ref, seg_col_ref, start, low, high)
        keys = rot_ref[low:high, key_columns]
        values = rot_ref[low:high, value_columns]
        for head in range(group):
            columns = slice(head * HEAD, (head + 1) * HEAD)
            queries = rot_ref[rows, columns]
            grads = grad_ref[slot_rows(rank_ref, start), columns]
            scores = dot_nt(queries, keys) * scale
            probs = jnp.exp(jnp.where(mask, scores - lse_ref[rows, columns][:, :1], MASKED))
            grad_probs = dot_nt(grads, values)
            inner = jnp.sum(probs * grad_probs, 1, keepdims=True)
            grad_scores = (probs * (grad_probs - inner)).astype(BF16)
            dv_ref[low:high, :] += dot_tn(probs.astype(BF16), grads)
            dk_ref[low:high, :] += dot_tn(grad_scores, queries)
            grad_query = dot_nn(grad_scores, keys) * scale
            turned = turn(grad_query, cos_ref[rows, :], -sin_ref[rows, :])
            out_ref[slot_rows(rank_ref, start), columns] = turned.astype(BF16)
    for start in range(0, length, TILE):
        rows = slice(start, start + TILE)
        turned = turn(dk_ref[rows, :] * scale, cos_ref[rows, :], -sin_ref[rows, :])
        out_ref[slot_rows(rank_ref, start), key_columns] = turned.astype(BF16)
        out_ref[slot_rows(rank_ref, start), value_columns] = dv_ref[rows, :].astype(BF16)


def attention_specs(length, group):
    wide = pl.BlockSpec((length, (group + 2) * HEAD), lambda kv, rank: (0, kv))
    narrow = pl.BlockSpec((length, group * HEAD), lambda kv, rank: (0, kv))
    table = pl.BlockSpec((length, HEAD), lambda kv, rank: (0, 0))
    seg_row = pl.BlockSpec((1, 1, length), lambda kv, rank: (0, 0, 0))
    seg_col = pl.BlockSpec((length, 1), lambda kv, rank: (0, 0))
    return wide, narrow, table, seg_row, seg_col


def attention_forward(rank, qkv, cosine, sine, segments, group, kv_count):
    length = segments.shape[1]
    wide, narrow, table, seg_row, seg_col = attention_specs(length, group)
    return pl.pallas_call(
        functools.partial(attend_forward, group),
        grid_spec=pltpu.PrefetchScalarGridSpec(
            num_scalar_prefetch=1,
            grid=(kv_count,),
            in_specs=[wide, table, table, seg_row, seg_col],
            out_specs=[narrow, wide, narrow, pl.BlockSpec((1, 8, HEAD), lambda kv, rank: (kv, 0, 0))],
        ),
        out_shape=[
            jax.ShapeDtypeStruct((length, kv_count * group * HEAD), BF16),
            jax.ShapeDtypeStruct((length, kv_count * (group + 2) * HEAD), BF16),
            jax.ShapeDtypeStruct((length, kv_count * group * HEAD), F32),
            jax.ShapeDtypeStruct((kv_count, 8, HEAD), F32),
        ],
        compiler_params=pltpu.CompilerParams(vmem_limit_bytes=48 * 2**20),
        cost_estimate=lasting(12),
        name="attention_forward",
    )(rank, qkv, cosine, sine, segments.reshape(1, 1, length), segments.reshape(length, 1))


def attention_backward(rank, rotated, grads, lse, cosine, sine, segments, group, kv_count):
    length = segments.shape[1]
    wide, narrow, table, seg_row, seg_col = attention_specs(length, group)
    return pl.pallas_call(
        functools.partial(attend_backward, group),
        grid_spec=pltpu.PrefetchScalarGridSpec(
            num_scalar_prefetch=1,
            grid=(kv_count,),
            in_specs=[wide, narrow, narrow, table, table, seg_row, seg_col],
            out_specs=wide,
            scratch_shapes=[pltpu.VMEM((length, HEAD), F32), pltpu.VMEM((length, HEAD), F32)],
        ),
        out_shape=jax.ShapeDtypeStruct((length, kv_count * (group + 2) * HEAD), BF16),
        compiler_params=pltpu.CompilerParams(vmem_limit_bytes=48 * 2**20),
        cost_estimate=lasting(13),
        name="attention_backward",
    )(rank, rotated, grads, lse, cosine, sine, segments.reshape(1, 1, length), segments.reshape(length, 1))


def gate_rows(both_ref, grad_ref, hidden_ref, grad_both_ref):
    columns = grad_ref.shape[1]
    gate, up, grad = both_ref[:, :columns], both_ref[:, columns:], grad_ref[...]
    sigmoid = 1.0 / (1.0 + jnp.exp(-gate))
    silu = gate * sigmoid
    hidden_ref[...] = (silu * up).astype(BF16)
    grad_both_ref[:, :columns] = (grad * up * (sigmoid * (1.0 + gate * (1.0 - sigmoid)))).astype(BF16)
    grad_both_ref[:, columns:] = (grad * silu).astype(BF16)


def call_gate_rows(both, grad):
    rows, columns = grad.shape
    tile = lambda width: pl.BlockSpec((TILE, width), lambda i: (i, 0))
    return pl.pallas_call(
        gate_rows,
        grid=(rows // TILE,),
        in_specs=[tile(2 * columns), tile(columns)],
        out_specs=[tile(columns), tile(2 * columns)],
        out_shape=[jax.ShapeDtypeStruct((rows, columns), BF16), jax.ShapeDtypeStruct((rows, 2 * columns), BF16)],
        cost_estimate=lasting(10),
        name="gate_rows",
    )(both, grad)


def lamb_direction(master, first, second, grad):
    first_moment = DECAY * first + (1.0 - DECAY) * grad
    second_moment = DECAY * second + (1.0 - DECAY) * grad * grad
    return second_moment, first_moment / (jnp.sqrt(second_moment) + STEP_EPS) + WEIGHT_DECAY * master


def gate_up_step(side_ref, master_ref, moment_ref, *refs):
    (gate_mine, up_mine, gate_theirs, up_theirs), (grad_ref, second_ref, direction_ref, sums_ref) = refs[:4], refs[4:]
    part, place, which = pl.program_id(0), pl.program_id(1), pl.program_id(2)
    mine = jnp.where(part == 0, gate_mine[...], up_mine[...])
    theirs = jnp.where(part == 0, gate_theirs[...], up_theirs[...])
    grad = jnp.where(which == side_ref[0], mine, theirs).astype(F32)
    second, direction = lamb_direction(master_ref[0], moment_ref[0, 0], moment_ref[1, 0], grad)
    grad_ref[0], second_ref[0], direction_ref[0] = grad, second, direction

    @pl.when((part == 0) & (place == 0) & (which == 0))
    def _():
        sums_ref[...] = jnp.zeros(sums_ref.shape, F32)

    sums_ref[...] += jnp.sum((direction * direction).reshape(-1, 8, direction.shape[1]), 0)


def call_gate_up_step(line, side, master, moments, summed, theirs):
    _, shard, units = master.shape
    block = units // (2 * line)
    whole = pl.BlockSpec((1, shard, block), lambda g, p, w, side: (g, 0, p * 2 + w))
    shape = jax.ShapeDtypeStruct(master.shape, F32)
    gate_place = lambda g, p: jnp.where(g == 0, p, line - 1)
    up_place = lambda g, p: jnp.where(g == 1, p, 0)
    return pl.pallas_call(
        gate_up_step,
        grid_spec=pltpu.PrefetchScalarGridSpec(
            num_scalar_prefetch=1,
            grid=(2, line, 2),
            in_specs=[
                whole,
                pl.BlockSpec((2, 1, shard, block), lambda g, p, w, side: (0, g, 0, p * 2 + w)),
                pl.BlockSpec((shard, block), lambda g, p, w, side: (side[0], gate_place(g, p))),
                pl.BlockSpec((shard, block), lambda g, p, w, side: (side[0], up_place(g, p))),
                pl.BlockSpec((shard, block), lambda g, p, w, side: (0, gate_place(g, p))),
                pl.BlockSpec((shard, block), lambda g, p, w, side: (0, up_place(g, p))),
            ],
            out_specs=[whole, whole, whole, pl.BlockSpec((8, block), lambda g, p, w, side: (0, 0))],
        ),
        out_shape=[shape, shape, shape, jax.ShapeDtypeStruct((8, block), F32)],
        cost_estimate=lasting(16),
        name="gate_up_step",
    )(side, master, moments, *summed, *theirs)


VMEM_ALL = pl.BlockSpec(memory_space=pltpu.VMEM)
SMALL = 5


def small_step(group, kvs, owner_ref, grad_qkv_ref, grad_out_ref, grad_gains_ref, *refs):
    masters, moments, refs = refs[:SMALL], refs[SMALL : 2 * SMALL], refs[2 * SMALL :]
    grads, seconds, directions, sums_ref = refs[:3], refs[3:8], refs[8:13], refs[13]
    step = (group + 2) * HEAD
    for kv in range(kvs):
        low = kv * step
        for ref, start, columns in ((grads[0], 0, group * HEAD), (grads[1], group * HEAD, HEAD), (grads[2], (group + 1) * HEAD, HEAD)):
            ref[:, kv * columns : (kv + 1) * columns] = grad_qkv_ref[:, low + start : low + start + columns]
    sums_ref[...] = jnp.zeros(sums_ref.shape, F32)
    for number in range(SMALL):
        grad = (grads[0], grads[1], grads[2], grad_out_ref, grad_gains_ref)[number][...]
        moment = moments[number]
        second, direction = lamb_direction(masters[number][...], moment[0], moment[1], grad)
        seconds[number][...] = second
        directions[number][...] = direction
        total = jnp.sum(jnp.sum(direction * direction, 0, keepdims=True), 1, keepdims=True)
        row = jnp.broadcast_to(total, (1, HEAD))
        sums_ref[number : number + 1, :] = row * owner_ref[...] if number == SMALL - 1 else row


def call_small_step(group, kvs, owner, grad_qkv, grad_out, grad_gains, masters, moments):
    like = lambda arrays: [jax.ShapeDtypeStruct(array.shape, F32) for array in arrays]
    return pl.pallas_call(
        functools.partial(small_step, group, kvs),
        in_specs=[VMEM_ALL] * (4 + 2 * SMALL),
        out_specs=[VMEM_ALL] * 14,
        out_shape=[*like(masters[:3]), *like(masters), *like(masters), jax.ShapeDtypeStruct((8, HEAD), F32)],
        compiler_params=pltpu.CompilerParams(vmem_limit_bytes=40 * 2**20),
        cost_estimate=lasting(6),
        name="small_step",
    )(owner, grad_qkv, grad_out, grad_gains, *masters, *moments)


def pick_lane(row, lane):
    lanes = lax.broadcasted_iota(jnp.int32, row.shape, 1)
    return jnp.sum(jnp.where(lanes == lane, row, 0.0), 1, keepdims=True)


def rate_of(packed_ref, number):
    squares = packed_ref[0:1, :]
    weight, update = jnp.sqrt(pick_lane(squares, number)), jnp.sqrt(pick_lane(squares, 7 + number))
    return RATE * (weight / (update + STEP_EPS))


def small_update(group, kvs, rank_ref, packed_ref, *refs):
    masters, directions, news, copies = (refs[k * SMALL : (k + 1) * SMALL] for k in range(4))
    gamma = CLIP / jnp.maximum(packed_ref[8:9, :], float(CLIP))
    heads = [pick_lane(gamma, rank_ref[0] * (group * kvs) + head) for head in range(group * kvs)]
    for place, number in enumerate((0, 1, 2, 3, 6)):
        rate = rate_of(packed_ref, number)
        if place > 1:
            stepped = masters[place][...] - rate * directions[place][...]
            news[place][...] = stepped
            copies[place][...] = stepped.astype(BF16)
            continue
        for head in range(group * kvs if place == 0 else kvs):
            scale = heads[head]
            if place == 1:
                scale = functools.reduce(jnp.minimum, heads[head * group : (head + 1) * group])
            columns = slice(head * HEAD, (head + 1) * HEAD)
            stepped = masters[place][:, columns] - rate * directions[place][:, columns]
            stepped = stepped * jnp.sqrt(scale)
            news[place][:, columns] = stepped
            copies[place][:, columns] = stepped.astype(BF16)


def call_small_update(group, kvs, rank, packed, masters, directions):
    like = lambda kind: [jax.ShapeDtypeStruct(array.shape, kind) for array in masters]
    return pl.pallas_call(
        functools.partial(small_update, group, kvs),
        in_specs=[pl.BlockSpec(memory_space=pltpu.SMEM), *[VMEM_ALL] * (1 + 2 * SMALL)],
        out_specs=[VMEM_ALL] * (2 * SMALL),
        out_shape=[*like(F32), *like(BF16)],
        compiler_params=pltpu.CompilerParams(vmem_limit_bytes=40 * 2**20),
        cost_estimate=lasting(5),
        name="small_update",
    )(rank, packed, *masters, *directions)


def large_update(number, packed_ref, master_ref, direction_ref, new_ref, copy_ref):
    stepped = master_ref[...] - rate_of(packed_ref, number) * direction_ref[...]
    new_ref[...] = stepped
    copy_ref[...] = stepped.astype(BF16)


def call_large_update(number, packed, master, direction):
    rows, columns = master.shape
    tile = min(rows, 128)
    blocks = pl.BlockSpec((tile, columns), lambda i: (i, 0))
    return pl.pallas_call(
        functools.partial(large_update, number),
        grid=(rows // tile,),
        in_specs=[pl.BlockSpec((16, HEAD), lambda i: (0, 0)), blocks, blocks],
        out_specs=[blocks, blocks],
        out_shape=[jax.ShapeDtypeStruct(master.shape, F32), jax.ShapeDtypeStruct(master.shape, BF16)],
        cost_estimate=lasting(4),
        name="large_update",
    )(packed, master, direction)


MESH = pl.DeviceIdType.MESH
WHOLE = pl.BlockSpec(memory_space=pltpu.VMEM)
CHUNKS = 8
AHEAD = 1


def greet(partners):
    barrier = pltpu.get_barrier_semaphore()
    for partner in partners:
        pl.semaphore_signal(barrier, inc=1, device_id=partner, device_id_type=MESH)
    pl.semaphore_wait(barrier, len(partners))


def sender(send_sems, recv_sems, log):
    def copy(kind, chunk, source, target, device):
        made = pltpu.make_async_remote_copy(
            src_ref=source,
            dst_ref=target,
            send_sem=send_sems.at[kind, chunk],
            recv_sem=recv_sems.at[kind, chunk],
            device_id=device,
            device_id_type=MESH,
        )
        log.append(made)
        return made

    return copy


def partners_of():
    rank, index = lax.axis_index("mp"), lax.axis_index("dp")
    return {"mp": rank ^ 1}, {"mp": rank ^ 2}, {"dp": index ^ 1}


def pick_rows(side_ref, rows_ref, _, out_ref):
    out_ref[...] = rows_ref[...]


def call_pick_rows(side, values, ready):
    rows, columns = values.shape[0] // 2, values.shape[1]
    return pl.pallas_call(
        pick_rows,
        grid_spec=pltpu.PrefetchScalarGridSpec(
            num_scalar_prefetch=1,
            grid=(1,),
            in_specs=[
                pl.BlockSpec((rows, columns), lambda i, side: (1 - side[0], 0)),
                pl.BlockSpec(memory_space=pl.ANY),
            ],
            out_specs=pl.BlockSpec((rows, columns), lambda i, side: (0, 0)),
        ),
        out_shape=jax.ShapeDtypeStruct((rows, columns), values.dtype),
        cost_estimate=lasting(2),
        name="pick_rows",
    )(side, values, ready)


class Everyone:
    def __init__(self, line, near_ref, line_ref, near_send, near_recv, line_send, line_recv):
        self.line, self.near_ref, self.line_ref = line, near_ref, line_ref
        self.near_send, self.near_recv, self.line_send, self.line_recv = near_send, near_recv, line_send, line_recv
        self.index, self.rank = lax.axis_index("dp"), lax.axis_index("mp")
        self.place, self.side = self.index // 2, self.index % 2
        self.code = self.side * 4 + self.rank

    @staticmethod
    def scratch(line, shape):
        return [
            pltpu.VMEM((8, *shape), F32),
            pltpu.VMEM((line, *shape), F32),
            pltpu.SemaphoreType.DMA((8,)),
            pltpu.SemaphoreType.DMA((8,)),
            pltpu.SemaphoreType.DMA((line,)),
            pltpu.SemaphoreType.DMA((line,)),
        ]

    def peer(self, k):
        return {"dp": self.index ^ (k // 4), "mp": self.rank ^ (k % 4)}

    def along(self, k):
        return {"dp": ((self.place + k) % self.line) * 2 + self.side}

    def partners(self):
        return [self.peer(k) for k in range(1, 8)] + [self.along(k) for k in range(1, self.line)]

    @staticmethod
    def add(left, right):
        return left + right

    def near_copy(self, k, slot):
        return pltpu.make_async_remote_copy(
            src_ref=self.near_ref.at[self.code],
            dst_ref=self.near_ref.at[slot],
            send_sem=self.near_send.at[k],
            recv_sem=self.near_recv.at[slot],
            device_id=self.peer(k),
            device_id_type=MESH,
        )

    def line_copy(self, k, slot):
        return pltpu.make_async_remote_copy(
            src_ref=self.line_ref.at[self.place],
            dst_ref=self.line_ref.at[slot],
            send_sem=self.line_send.at[k],
            recv_sem=self.line_recv.at[slot],
            device_id=self.along(k),
            device_id_type=MESH,
        )

    @staticmethod
    def total(ref, count, fold):
        value = ref[0]
        for k in range(1, count):
            value = fold(value, ref[k])
        return value

    def send_near(self):
        for k in range(1, 8):
            self.near_copy(k, self.code).start()

    def send_line(self, fold):
        for k in range(1, 8):
            self.near_copy(k, self.code ^ k).wait_recv()
        self.line_ref[self.place] = self.total(self.near_ref, 8, fold)
        for k in range(1, self.line):
            self.line_copy(k, self.place).start()

    def result(self, fold):
        for k in range(1, self.line):
            self.line_copy(k, (self.place + k) % self.line).wait_recv()
        value = self.total(self.line_ref, self.line, fold)
        for k in range(1, 8):
            self.near_copy(k, self.code).wait_send()
        for k in range(1, self.line):
            self.line_copy(k, self.place).wait_send()
        return value


def spread_forward(part_ref, tokens_ref, gain_ref, grad_ref, down_ref, rows_ref, middle_ref, hidden_ref, near_ref, out_ref, far_ref, grad_in_ref, down_in_ref, hidden_out_ref, send_sems, recv_sems, fetch_sems, store_sems):
    fetches = [
        pltpu.make_async_copy(source, target, fetch_sems.at[k])
        for k, (source, target) in enumerate(((grad_ref, grad_in_ref), (down_ref, down_in_ref)))
    ]
    for fetch in fetches:
        fetch.start()
    band = hidden_out_ref.shape[0] // CHUNKS
    stores = []

    def multiply(i):
        rows = pl.ds(i * band, band)
        hidden_out_ref[rows, :] = dot_nt(grad_in_ref[rows, :], down_in_ref[...])
        stores.append(pltpu.make_async_copy(hidden_out_ref.at[rows], hidden_ref.at[rows], store_sems.at[i]))
        stores[-1].start()

    core, far, pair = partners_of()
    quarter, _ = tokens_ref.shape
    size = quarter // CHUNKS
    at = lambda slot, i: pl.ds(slot * quarter + i * size, size)
    greet([core, far, pair])
    log = []
    copy = sender(send_sems, recv_sems, log)
    near = {}
    for i in range(CHUNKS):
        for k in range(2):
            near[k, i] = copy(k, i, part_ref.at[at(2 * k + 1, i)], near_ref.at[at(k, i)], core)
            near[k, i].start()
    sums = {}

    def send_sum(i):
        near[1, i].wait_recv()
        total = part_ref[at(2, i), :].astype(F32) + near_ref[at(1, i), :].astype(F32)
        out_ref[at(0, i), :] = total.astype(BF16)
        sums[i] = copy(2, i, out_ref.at[at(0, i)], far_ref.at[at(0, i)], far)
        sums[i].start()

    for i in range(AHEAD):
        send_sum(i)
    moves = {}
    for i in range(CHUNKS + 2):
        if i + AHEAD < CHUNKS:
            send_sum(i + AHEAD)
        if i < CHUNKS:
            near[0, i].wait_recv()
            sums[i].wait_recv()
            middle = tokens_ref[at(0, i), :].astype(F32) + (
                part_ref[at(0, i), :].astype(F32)
                + near_ref[at(0, i), :].astype(F32)
                + far_ref[at(0, i), :].astype(F32)
            )
            middle_ref[at(0, i), :] = middle
            rows_ref[at(0, i), :] = (middle * inverse_rms(middle) * gain_ref[0:1, :]).astype(BF16)
            own = rows_ref.at[at(0, i)]
            for kind, slot, device in ((3, 2, far), (4, 4, pair), (6, 1, core)):
                moves[kind, i] = copy(kind, i, own, rows_ref.at[at(slot, i)], device)
                moves[kind, i].start()
        j = i - 1
        if 0 <= j < CHUNKS:
            moves[3, j].wait_recv()
            for kind, slot, device in ((5, 6, pair), (7, 3, core)):
                moves[kind, j] = copy(kind, j, rows_ref.at[at(2, j)], rows_ref.at[at(slot, j)], device)
                moves[kind, j].start()
            moves[4, j].wait_recv()
            moves[8, j] = copy(8, j, rows_ref.at[at(4, j)], rows_ref.at[at(5, j)], core)
            moves[8, j].start()
        j = i - 2
        if 0 <= j < CHUNKS:
            moves[5, j].wait_recv()
            moves[9, j] = copy(9, j, rows_ref.at[at(6, j)], rows_ref.at[at(7, j)], core)
            moves[9, j].start()
        if i == 0:
            for fetch in fetches:
                fetch.wait()
        if i < CHUNKS:
            multiply(i)
    for i in range(CHUNKS):
        for kind in (6, 7, 8, 9):
            moves[kind, i].wait_recv()
    for made in log:
        made.wait_send()
    for store in stores:
        store.wait()


def call_spread_forward(part, tokens_own, gain, grad_rows, down):
    quarter, width = tokens_own.shape
    hidden = (grad_rows.shape[0], down.shape[0])
    hbm = pl.BlockSpec(memory_space=pl.ANY)
    return pl.pallas_call(
        spread_forward,
        in_specs=[*[WHOLE] * 3, hbm, hbm],
        out_specs=[WHOLE, WHOLE, hbm],
        out_shape=[
            jax.ShapeDtypeStruct((8 * quarter, width), BF16),
            jax.ShapeDtypeStruct((quarter, width), F32),
            jax.ShapeDtypeStruct(hidden, F32),
        ],
        scratch_shapes=[
            pltpu.VMEM((2 * quarter, width), BF16),
            pltpu.VMEM((quarter, width), BF16),
            pltpu.VMEM((quarter, width), BF16),
            pltpu.VMEM(grad_rows.shape, BF16),
            pltpu.VMEM(down.shape, BF16),
            pltpu.VMEM(hidden, F32),
            pltpu.SemaphoreType.DMA((10, CHUNKS)),
            pltpu.SemaphoreType.DMA((10, CHUNKS)),
            pltpu.SemaphoreType.DMA((2,)),
            pltpu.SemaphoreType.DMA((CHUNKS,)),
        ],
        compiler_params=pltpu.CompilerParams(
            collective_id=1, has_side_effects=True, vmem_limit_bytes=54 * 2**20
        ),
        cost_estimate=lasting(64),
        name="spread_forward",
    )(part, tokens_own, gain, grad_rows, down)


def pull_chunk(values, scale_gain, grad):
    scale = inverse_rms(values)
    turned = grad * scale_gain
    inner = jnp.mean(turned * values, -1, keepdims=True)
    return scale * turned - (scale * scale * scale) * values * inner, grad * values * scale


def spread_backward(part_ref, middle_ref, grad_ref, gain_ref, left_ref, both_ref, _, rows_ref, total_ref, gain_out_ref, up_ref, near_ref, side_out_ref, side_in_ref, far_out_ref, far_in_ref, left_in_ref, right_in_ref, up_out_ref, send_sems, recv_sems, fetch_sems, store_sems):
    units = right_in_ref.shape[1]
    fetches = [
        pltpu.make_async_copy(left_ref, left_in_ref, fetch_sems.at[0]),
        pltpu.make_async_copy(both_ref.at[:, pl.ds(units, units)], right_in_ref, fetch_sems.at[1]),
    ]
    for fetch in fetches:
        fetch.start()
    band = up_out_ref.shape[0] // CHUNKS
    stores = []

    def multiply(i):
        rows = pl.ds(i * band, band)
        up_out_ref[rows, :] = dot_tn(left_in_ref[:, rows], right_in_ref[...]).astype(BF16)
        stores.append(pltpu.make_async_copy(up_out_ref.at[rows], up_ref.at[rows], store_sems.at[i]))
        stores[-1].start()

    core, far, pair = partners_of()
    quarter, width = middle_ref.shape
    size = quarter // CHUNKS
    at = lambda slot, i: pl.ds(slot * quarter + i * size, size)
    greet([core, far, pair])
    log = []
    copy = sender(send_sems, recv_sems, log)
    near, side, sums, moves = {}, {}, {}, {}
    for i in range(CHUNKS):
        for k in (2, 3, 0, 1):
            near[k, i] = copy(k, i, part_ref.at[at(2 * k + 1, i)], near_ref.at[at(k, i)], core)
            near[k, i].start()

    def pairs(k, i):
        return part_ref[at(2 * k, i), :].astype(F32) + near_ref[at(k, i), :].astype(F32)

    def send_side(i):
        for k in (1, 0):
            near[2 + k, i].wait_recv()
            side_out_ref[at(k, i), :] = pairs(2 + k, i).astype(BF16)
            side[k, i] = copy(4 + k, i, side_out_ref.at[at(k, i)], side_in_ref.at[at(k, i)], pair)
            side[k, i].start()

    for i in range(AHEAD):
        send_side(i)
    gain_sum = jnp.zeros((1, width), F32)
    for i in range(CHUNKS + 2):
        if i + AHEAD < CHUNKS:
            send_side(i + AHEAD)
        if i < CHUNKS:
            near[1, i].wait_recv()
            side[1, i].wait_recv()
            far_out_ref[at(0, i), :] = (pairs(1, i) + side_in_ref[at(1, i), :].astype(F32)).astype(BF16)
            sums[i] = copy(6, i, far_out_ref.at[at(0, i)], far_in_ref.at[at(0, i)], far)
            sums[i].start()
        j = i - 1
        if 0 <= j < CHUNKS:
            near[0, j].wait_recv()
            side[0, j].wait_recv()
            sums[j].wait_recv()
            grad = pairs(0, j) + side_in_ref[at(0, j), :].astype(F32) + far_in_ref[at(0, j), :].astype(F32)
            back, gain_part = pull_chunk(middle_ref[at(0, j), :], gain_ref[0:1, :], grad)
            gain_sum = gain_sum + jnp.sum(gain_part, 0, keepdims=True)
            total = grad_ref[at(0, j), :].astype(F32) + back
            total_ref[at(0, j), :] = total
            rows_ref[at(0, j), :] = total.astype(BF16)
            own = rows_ref.at[at(0, j)]
            for kind, slot, device in ((7, 2, far), (8, 1, core)):
                moves[kind, j] = copy(kind, j, own, rows_ref.at[at(slot, j)], device)
                moves[kind, j].start()
        j = i - 2
        if 0 <= j < CHUNKS:
            moves[7, j].wait_recv()
            moves[9, j] = copy(9, j, rows_ref.at[at(2, j)], rows_ref.at[at(3, j)], core)
            moves[9, j].start()
        if i == 0:
            for fetch in fetches:
                fetch.wait()
        if i < CHUNKS:
            multiply(i)
    gain_out_ref[...] = jnp.broadcast_to(gain_sum, gain_out_ref.shape)
    for i in range(CHUNKS):
        for kind in (8, 9):
            moves[kind, i].wait_recv()
    for made in log:
        made.wait_send()
    for store in stores:
        store.wait()


def call_spread_backward(part, middle, grad_own, gain, left, both, ready):
    quarter, width = middle.shape
    units = both.shape[1] // 2
    hbm = pl.BlockSpec(memory_space=pl.ANY)
    return pl.pallas_call(
        spread_backward,
        in_specs=[*[WHOLE] * 4, hbm, hbm, hbm],
        out_specs=[*[WHOLE] * 3, hbm],
        out_shape=[
            jax.ShapeDtypeStruct((4 * quarter, width), BF16),
            jax.ShapeDtypeStruct((quarter, width), F32),
            jax.ShapeDtypeStruct((8, width), F32),
            jax.ShapeDtypeStruct((width, units), BF16),
        ],
        scratch_shapes=[
            pltpu.VMEM((4 * quarter, width), BF16),
            pltpu.VMEM((2 * quarter, width), BF16),
            pltpu.VMEM((2 * quarter, width), BF16),
            pltpu.VMEM((quarter, width), BF16),
            pltpu.VMEM((quarter, width), BF16),
            pltpu.VMEM(left.shape, BF16),
            pltpu.VMEM((left.shape[0], units), BF16),
            pltpu.VMEM((width, units), BF16),
            pltpu.SemaphoreType.DMA((10, CHUNKS)),
            pltpu.SemaphoreType.DMA((10, CHUNKS)),
            pltpu.SemaphoreType.DMA((2,)),
            pltpu.SemaphoreType.DMA((CHUNKS,)),
        ],
        compiler_params=pltpu.CompilerParams(
            collective_id=2, has_side_effects=True, vmem_limit_bytes=56 * 2**20
        ),
        cost_estimate=lasting(68),
        name="spread_backward",
    )(part, middle, grad_own, gain, left, both, ready)


def finish(line, part_ref, tokens_ref, total_ref, gain_ref, *refs):
    gain_two_ref, grads_refs, refs = refs[0], refs[1:3], refs[7:]
    input_ref, gain_out_ref, *owned_refs = refs[:4]
    rows_ref, near_ref, far_out_ref, far_in_ref, refs = *refs[4:8], refs[1:]
    side_in_refs, up_out_refs, up_in_refs, down_out_refs, down_in_refs = (refs[k : k + 2] for k in range(7, 17, 2))
    send_sems, recv_sems, side_send, side_recv, line_send, line_recv, *exchange = refs[17:]
    core, far, pair = partners_of()
    index = lax.axis_index("dp")
    place, side = index // 2, index % 2
    above, below = {"dp": index + 2}, {"dp": index - 2}
    quarter, width = tokens_ref.shape
    size = quarter // CHUNKS
    last = line - 1
    at = lambda slot, i: pl.ds(slot * quarter + i * size, size)

    def block(w, where, which):
        rows = owned_refs[w].shape[0]
        return pl.ds((where * 2 + which) * rows, rows)


    everyone = Everyone(line, *exchange)
    greet(everyone.partners())
    log = []
    copy = sender(send_sems, recv_sems, log)
    near, sums, moves = {}, {}, {}
    for i in range(CHUNKS):
        for k in (1, 0):
            near[k, i] = copy(k, i, part_ref.at[at(2 * k + 1, i)], near_ref.at[at(k, i)], core)
            near[k, i].start()

    def side_copy(w, where):
        return pltpu.make_async_remote_copy(
            src_ref=grads_refs[w].at[block(w, where, 1 - side)],
            dst_ref=side_in_refs[w].at[where],
            send_sem=side_send.at[w, where],
            recv_sem=side_recv.at[w, where],
            device_id=pair,
            device_id_type=MESH,
        )

    def line_copy(w, upward, step):
        out_ref, in_ref = (up_out_refs[w], up_in_refs[w]) if upward else (down_out_refs[w], down_in_refs[w])
        way = 0 if upward else 1
        return pltpu.make_async_remote_copy(
            src_ref=out_ref.at[step - 1],
            dst_ref=in_ref.at[step - 1],
            send_sem=line_send.at[w, way, step - 1],
            recv_sem=line_recv.at[w, way, step - 1],
            device_id=above if upward else below,
            device_id_type=MESH,
        )

    for step in range(last, 0, -1):

        @pl.when(place + step <= last)
        def _(step=step):
            for w in range(2):
                side_copy(w, place + step).start()

        @pl.when(place - step >= 0)
        def _(step=step):
            for w in range(2):
                side_copy(w, place - step).start()

    for w in range(2):
        side_copy(w, place).start()

    for i in range(CHUNKS):
        near[1, i].wait_recv()
        summed = part_ref[at(2, i), :].astype(F32) + near_ref[at(1, i), :].astype(F32)
        far_out_ref[at(0, i), :] = summed.astype(BF16)
        sums[i] = copy(2, i, far_out_ref.at[at(0, i)], far_in_ref.at[at(0, i)], far)
        sums[i].start()

    def term(w, where):
        return grads_refs[w][block(w, where, side), :].astype(F32) + side_in_refs[w][where].astype(F32)

    def line_step(step):
        for w in range(2):

            @pl.when(place + step <= last)
            def _(w=w):
                side_copy(w, place + step).wait_recv()
                value = term(w, place + step)
                up_out_refs[w][step - 1] = value.astype(BF16)
                if step < last:

                    @pl.when(place > 0)
                    def _():
                        line_copy(w, True, step + 1).wait_recv()
                        up_out_refs[w][step - 1] = (value + up_in_refs[w][step].astype(F32)).astype(BF16)

                line_copy(w, True, step).start()

            @pl.when(place - step >= 0)
            def _(w=w):
                side_copy(w, place - step).wait_recv()
                value = term(w, place - step)
                down_out_refs[w][step - 1] = value.astype(BF16)
                if step < last:

                    @pl.when(place < last)
                    def _():
                        line_copy(w, False, step + 1).wait_recv()
                        down_out_refs[w][step - 1] = (value + down_in_refs[w][step].astype(F32)).astype(BF16)

                line_copy(w, False, step).start()

    def settle(slot, i):
        start = pl.multiple_of((lax.axis_index("mp") ^ slot) * quarter + i * size, size)
        input_ref[pl.ds(start, size), :] = rows_ref[at(slot, i), :].astype(F32)

    gain_sum = jnp.zeros((1, width), F32)
    steps = list(range(last, 0, -1))
    for i in range(CHUNKS + 1):
        if i < CHUNKS:
            near[0, i].wait_recv()
            sums[i].wait_recv()
            grad = (
                part_ref[at(0, i), :].astype(F32)
                + near_ref[at(0, i), :].astype(F32)
                + far_in_ref[at(0, i), :].astype(F32)
            )
            back, gain_part = pull_chunk(tokens_ref[at(0, i), :].astype(F32), gain_ref[0:1, :], grad)
            gain_sum = gain_sum + jnp.sum(gain_part, 0, keepdims=True)
            rows_ref[at(0, i), :] = (total_ref[at(0, i), :] + back).astype(BF16)
            settle(0, i)
            own = rows_ref.at[at(0, i)]
            for kind, slot, device in ((3, 2, far), (4, 1, core)):
                moves[kind, i] = copy(kind, i, own, rows_ref.at[at(slot, i)], device)
                moves[kind, i].start()
        if steps:
            line_step(steps.pop(0))
        j = i - 1
        if 0 <= j < CHUNKS:
            moves[3, j].wait_recv()
            settle(2, j)
            moves[5, j] = copy(5, j, rows_ref.at[at(2, j)], rows_ref.at[at(3, j)], core)
            moves[5, j].start()
    while steps:
        line_step(steps.pop(0))
    columns = gain_out_ref.shape[1]
    for r in range(4):
        cut = slice(r * columns, (r + 1) * columns)
        everyone.near_ref[everyone.code, r : r + 1, :] = gain_sum[:, cut]
        everyone.near_ref[everyone.code, r + 4 : r + 5, :] = gain_two_ref[0:1, cut]
    everyone.send_near()
    everyone.send_line(everyone.add)
    for w in range(2):
        side_copy(w, place).wait_recv()
        owned_refs[w][...] = term(w, place)

        @pl.when(place > 0)
        def _(w=w):
            line_copy(w, True, 1).wait_recv()
            owned_refs[w][...] += up_in_refs[w][0].astype(F32)

        @pl.when(place < last)
        def _(w=w):
            line_copy(w, False, 1).wait_recv()
            owned_refs[w][...] += down_in_refs[w][0].astype(F32)

    gain_out_ref[...] = everyone.result(everyone.add)
    for i in range(CHUNKS):
        for kind, slot in ((4, 1), (5, 3)):
            moves[kind, i].wait_recv()
            settle(slot, i)
    for made in log:
        made.wait_send()
    for w in range(2):
        for where in range(line):
            side_copy(w, where).wait_send()
        for step in range(last, 0, -1):

            @pl.when(place + step <= last)
            def _(w=w, step=step):
                line_copy(w, True, step).wait_send()

            @pl.when(place - step >= 0)
            def _(w=w, step=step):
                line_copy(w, False, step).wait_send()


def call_finish(dp_size, part, tokens_own, total, gain, gain_two, ready, *grads):
    quarter, width = tokens_own.shape
    line = dp_size // 2
    owned = [(grad.shape[0] // dp_size, grad.shape[1]) for grad in grads]
    stacks = lambda count: [pltpu.VMEM((count, *shape), BF16) for shape in owned]
    return pl.pallas_call(
        functools.partial(finish, line),
        in_specs=[*[WHOLE] * 7, *[pl.BlockSpec(memory_space=pl.ANY)] * 4],
        out_specs=[WHOLE] * 4,
        out_shape=[
            jax.ShapeDtypeStruct((4 * quarter, width), F32),
            jax.ShapeDtypeStruct((8, width // 4), F32),
            *[jax.ShapeDtypeStruct(shape, F32) for shape in owned],
        ],
        scratch_shapes=[
            pltpu.VMEM((4 * quarter, width), BF16),
            pltpu.VMEM((2 * quarter, width), BF16),
            pltpu.VMEM((quarter, width), BF16),
            pltpu.VMEM((quarter, width), BF16),
            *stacks(line),
            *stacks(line - 1),
            *stacks(line - 1),
            *stacks(line - 1),
            *stacks(line - 1),
            pltpu.SemaphoreType.DMA((6, CHUNKS)),
            pltpu.SemaphoreType.DMA((6, CHUNKS)),
            pltpu.SemaphoreType.DMA((2, line)),
            pltpu.SemaphoreType.DMA((2, line)),
            pltpu.SemaphoreType.DMA((2, 2, line)),
            pltpu.SemaphoreType.DMA((2, 2, line)),
            *Everyone.scratch(line, (8, width // 4)),
        ],
        compiler_params=pltpu.CompilerParams(
            collective_id=3, has_side_effects=True, vmem_limit_bytes=56 * 2**20
        ),
        cost_estimate=lasting(85),
        name="finish",
    )(part, tokens_own, total, gain, gain_two, *grads, *ready)


def gather_weights(line, own_ref, out_ref, gains_ref, grad_ref, full_ref, out_full_ref, gains_full_ref, rows_ref, local_sems, side_send, side_recv, line_send, line_recv, rows_send, rows_recv, staged_ref):
    index = lax.axis_index("dp")
    place, side = index // 2, index % 2
    pair, above, below = {"dp": index ^ 1}, {"dp": index + 2}, {"dp": index - 2}
    rank = lax.axis_index("mp")
    core, far = {"mp": rank ^ 1}, {"mp": rank ^ 2}
    quarter = grad_ref.shape[0] // 4
    slot_of = lambda k: rows_ref.at[pl.ds(k * quarter, quarter)]
    quarter_of = lambda k: grad_ref.at[pl.ds((rank ^ k) * quarter, quarter)]
    last = line - 1
    owns, fulls = (own_ref, out_ref, gains_ref), (full_ref, out_full_ref, gains_full_ref)
    all_three = range(3)

    barrier = pltpu.get_barrier_semaphore()
    pl.semaphore_signal(barrier, inc=1, device_id=pair, device_id_type=MESH)
    pl.semaphore_signal(barrier, inc=1, device_id=core, device_id_type=MESH)
    pl.semaphore_signal(barrier, inc=1, device_id=far, device_id_type=MESH)

    @pl.when(place < last)
    def _():
        pl.semaphore_signal(barrier, inc=1, device_id=above, device_id_type=MESH)

    @pl.when(place > 0)
    def _():
        pl.semaphore_signal(barrier, inc=1, device_id=below, device_id_type=MESH)

    pl.semaphore_wait(barrier, 3 + (place < last).astype(jnp.int32) + (place > 0).astype(jnp.int32))

    def slot(which, where, side):
        rows = owns[which].shape[0]
        return fulls[which].at[pl.ds((where * 2 + side) * rows, rows)]

    def views(which, where):
        return slot(which, where, side)

    def source(which, where, first):
        return owns[which] if first else views(which, where)

    def line_copy(which, upward, where, first=False):
        way = 0 if upward else 1
        return pltpu.make_async_remote_copy(
            src_ref=source(which, where, first),
            dst_ref=views(which, where),
            send_sem=line_send.at[which, way, where],
            recv_sem=line_recv.at[which, way, where],
            device_id=above if upward else below,
            device_id_type=MESH,
        )

    def side_copy(which, where, first=False):
        return pltpu.make_async_remote_copy(
            src_ref=source(which, where, first),
            dst_ref=views(which, where),
            send_sem=side_send.at[which, where],
            recv_sem=side_recv.at[which, where],
            device_id=pair,
            device_id_type=MESH,
        )

    def side_arrival(which, where):
        target = slot(which, where, 1 - side)
        return pltpu.make_async_remote_copy(
            src_ref=target,
            dst_ref=target,
            send_sem=side_send.at[which, where],
            recv_sem=side_recv.at[which, where],
            device_id=pair,
            device_id_type=MESH,
        )

    @pl.when(place < last)
    def _():
        for which in all_three:
            line_copy(which, True, place, True).start()

    @pl.when(place > 0)
    def _():
        for which in all_three:
            line_copy(which, False, place, True).start()

    for which in all_three:
        side_copy(which, place, True).start()
    here = [pltpu.make_async_copy(source(w, place, True), views(w, place), local_sems.at[w]) for w in all_three]
    for made in here:
        made.start()
    staged_of = lambda k: staged_ref.at[pl.ds(k * quarter, quarter)]
    fetches = [pltpu.make_async_copy(quarter_of(k), staged_of(k), local_sems.at[3 + k]) for k in range(4)]
    stores = [pltpu.make_async_copy(staged_of(k), slot_of(k), local_sems.at[7 + k]) for k in range(4)]
    for made in fetches:
        made.start()

    def rows_copy(number, source, target, device):
        return pltpu.make_async_remote_copy(
            src_ref=source,
            dst_ref=target,
            send_sem=rows_send.at[number],
            recv_sem=rows_recv.at[number],
            device_id=device,
            device_id_type=MESH,
        )

    over = rows_copy(0, quarter_of(0), slot_of(4), pair)
    across = rows_copy(1, slot_of(4), slot_of(6), far)
    near = [rows_copy(2 + k, slot_of(4 + 2 * k), slot_of(5 + 2 * k), core) for k in range(2)]
    over.start()

    for step in range(1, line):

        @pl.when(place - step >= 0)
        def _(step=step):
            where = place - step
            for which in all_three:
                line_copy(which, True, where).wait_recv()

                @pl.when(place < last)
                def _(which=which):
                    line_copy(which, True, where).start()

                side_copy(which, where).start()

        @pl.when(place + step <= last)
        def _(step=step):
            where = place + step
            for which in all_three:
                line_copy(which, False, where).wait_recv()

                @pl.when(place > 0)
                def _(which=which):
                    line_copy(which, False, where).start()

                side_copy(which, where).start()

        if step == 1:
            for fetch, store in zip(fetches, stores):
                fetch.wait()
                store.start()
            over.wait_recv()
            across.start()
            near[0].start()

    across.wait_recv()
    near[1].start()
    for made in here + stores:
        made.wait()
    for where in range(line):
        for which in all_three:
            side_arrival(which, where).wait_recv()
            side_copy(which, where).wait_send()

            @pl.when((where <= place) & (place < last))
            def _(which=which, where=where):
                line_copy(which, True, where).wait_send()

            @pl.when((where >= place) & (place > 0))
            def _(which=which, where=where):
                line_copy(which, False, where).wait_send()

    for k in range(2):
        near[k].wait_recv()
        near[k].wait_send()
    over.wait_send()
    across.wait_send()


def call_gather_weights(dp_size, grads, *owns):
    line = dp_size // 2
    hbm = pl.BlockSpec(memory_space=pl.ANY)
    return pl.pallas_call(
        functools.partial(gather_weights, line),
        in_specs=[hbm] * 4,
        out_specs=[hbm] * 4,
        out_shape=[
            *[jax.ShapeDtypeStruct((dp_size * own.shape[0], own.shape[1]), own.dtype) for own in owns],
            jax.ShapeDtypeStruct((2 * grads.shape[0], grads.shape[1]), grads.dtype),
        ],
        scratch_shapes=[
            pltpu.SemaphoreType.DMA((11,)),
            pltpu.SemaphoreType.DMA((3, line)),
            pltpu.SemaphoreType.DMA((3, line)),
            pltpu.SemaphoreType.DMA((3, 2, line)),
            pltpu.SemaphoreType.DMA((3, 2, line)),
            pltpu.SemaphoreType.DMA((4,)),
            pltpu.SemaphoreType.DMA((4,)),
            pltpu.VMEM(grads.shape, grads.dtype),
        ],
        compiler_params=pltpu.CompilerParams(
            collective_id=4, has_side_effects=True, vmem_limit_bytes=16 * 2**20
        ),
        cost_estimate=lasting(120),
        name="gather_weights",
    )(*owns, grads)


def combine_all(line, early_ref, small_ref, gate_up_ref, out_ref, *exchange):
    everyone = Everyone(line, *exchange)
    greet(everyone.partners())
    lanes = lax.broadcasted_iota(jnp.int32, early_ref.shape, 1)
    adds = lax.broadcasted_iota(jnp.int32, early_ref.shape, 0) < 8
    fold = lambda left, right: jnp.where(adds, left + right, jnp.maximum(left, right))
    value = early_ref[...]
    gate_up = jnp.sum(jnp.sum(gate_up_ref[...], 0, keepdims=True), 1, keepdims=True)
    terms = [small_ref[k : k + 1, :] for k in range(SMALL)] + [jnp.broadcast_to(gate_up, (1, HEAD))]
    for term, number in zip(terms, (0, 1, 2, 3, 6, 4)):
        value = jnp.where(adds & (lanes == 7 + number), term, value)
    everyone.near_ref[everyone.code] = value
    everyone.send_near()
    everyone.send_line(fold)
    out_ref[...] = everyone.result(fold)


def call_combine_all(dp_size, early, small, gate_up):
    line = dp_size // 2
    return pl.pallas_call(
        functools.partial(combine_all, line),
        in_specs=[WHOLE] * 3,
        out_specs=WHOLE,
        out_shape=jax.ShapeDtypeStruct(early.shape, F32),
        scratch_shapes=Everyone.scratch(line, early.shape),
        compiler_params=pltpu.CompilerParams(collective_id=6, has_side_effects=True),
        cost_estimate=lasting(10),
        name="combine_all",
    )(early, small, gate_up)


class Links:
    def __init__(self, dp_size, mp_size):
        self.dp, self.mp, self.line = dp_size, mp_size, dp_size // 2
        self.index = lax.axis_index("dp")
        self.place, self.side, self.rank = self.index // 2, self.index % 2, lax.axis_index("mp")
        self.lines = [[place * 2 + side for place in range(self.line)] for side in range(2)]

    def swap_mp(self, value, bit):
        return lax.ppermute(value, "mp", [(i, i ^ bit) for i in range(self.mp)])

    def swap_side(self, value):
        return lax.ppermute(value, "dp", [(i, i ^ 1) for i in range(self.dp)])

    def gather_line(self, own):
        return lax.all_gather(own, "dp", axis=0, tiled=True, axis_index_groups=self.lines)

    def sum_line(self, parts):
        return lax.psum_scatter(parts, "dp", scatter_dimension=0, tiled=True, axis_index_groups=self.lines)


    def to_slots(self, values):
        rows = values.shape[0] // self.mp
        return jnp.concatenate(
            [lax.dynamic_slice_in_dim(values, (self.rank ^ k) * rows, rows, 0) for k in range(self.mp)], 0
        )

    def from_slots(self, values):
        rows = values.shape[0] // self.mp
        cuts = [values[k * rows : (k + 1) * rows] for k in range(self.mp)]
        odd = (self.rank & 1) == 1
        high = (self.rank & 2) == 2
        cuts = [jnp.where(odd, cuts[k ^ 1], cuts[k]) for k in range(self.mp)]
        cuts = [jnp.where(high, cuts[k ^ 2], cuts[k]) for k in range(self.mp)]
        return jnp.concatenate(cuts, 0)

    def gather_core(self, quarter, far):
        rows = quarter.shape[0]
        near = self.swap_mp(jnp.concatenate([quarter, far], 0), 1)
        return jnp.concatenate([quarter, near[:rows], far, near[rows:]], 0)

    def swap_core(self, slots):
        rows = slots.shape[0] // 8
        picked = lambda ks: jnp.concatenate([slots[k * rows : (k + 1) * rows] for k in ks], 0)
        return slots, self.swap_mp(picked((1, 3, 5, 7)), 1)

    def sum_core(self, slots, near):
        rows = slots.shape[0] // 8
        add = lambda ks, low: jnp.concatenate(
            [
                slots[k * rows : (k + 1) * rows].astype(F32) + near[i * rows : (i + 1) * rows].astype(F32)
                for i, k in enumerate(ks, low)
            ],
            0,
        ).astype(BF16)
        return add((0, 2), 0), add((4,), 2), add((6,), 3)


def after(value, *others):
    return lax.optimization_barrier((value, *others))[0]


def inverse_rms(values):
    return lax.rsqrt(jnp.mean(values * values, -1, keepdims=True) + NORM_EPS)


def body(
    dp_size,
    mp_size,
    tokens,
    cotangent,
    segment_ids,
    w_query,
    w_key,
    w_value,
    w_out,
    w_gate_up,
    w_down,
    norm_gains,
    query_moments,
    key_moments,
    value_moments,
    out_moments,
    gate_up_moments,
    down_moments,
    gains_moments,
):
    links = Links(dp_size, mp_size)
    line, side = links.line, links.side
    heads = w_query.shape[1] // HEAD
    kvs = w_key.shape[1] // HEAD
    group = heads // kvs
    width = tokens.shape[1]
    shard = w_query.shape[0]
    units = w_gate_up.shape[2]
    block = units // (line * 2)

    def interleave(query, key, value):
        parts = []
        for kv in range(kvs):
            parts.append(query[..., kv * group * HEAD : (kv + 1) * group * HEAD])
            parts.append(key[..., kv * HEAD : (kv + 1) * HEAD])
            parts.append(value[..., kv * HEAD : (kv + 1) * HEAD])
        return jnp.concatenate(parts, -1)

    by_side = w_gate_up.reshape(2, shard, line, 2, block)

    def side_units(which):
        cut = lax.dynamic_index_in_dim(by_side, which, 3, keepdims=False).astype(BF16)
        return jnp.concatenate([cut[0].reshape(shard, -1), cut[1].reshape(shard, -1)], 1)

    token_slots = links.to_slots(tokens)
    inputs = token_slots.astype(F32)
    scale_one = inverse_rms(inputs)
    down_full = links.gather_line(w_down.astype(BF16))
    own_units = side_units(side)
    sent_units = links.swap_side(side_units(1 - side))
    rows_pair = jnp.zeros((2 * shard, own_units.shape[1]), BF16)
    rows_pair = lax.dynamic_update_slice(rows_pair, own_units, (side * shard, 0))
    rows_pair = lax.dynamic_update_slice(rows_pair, sent_units, ((1 - side) * shard, 0))
    gate_up_full = after(links.gather_line(rows_pair), down_full)
    gains_low = norm_gains.astype(BF16).astype(F32)
    gains_rows = jnp.concatenate([gains_low, jnp.zeros((6, gains_low.shape[1]), F32)], 0)
    qkv_full, out_full, gains_shards, grad_rows = call_gather_weights(
        dp_size,
        cotangent,
        after(interleave(w_query, w_key, w_value).astype(BF16), rows_pair, scale_one, token_slots),
        w_out.astype(BF16),
        gains_rows,
    )
    gains_full = jnp.transpose(gains_shards.reshape(dp_size, 8, -1), (1, 0, 2)).reshape(8, width)

    quarter = tokens.shape[0] // 4

    cosine, sine = rope_tables(segment_ids.shape[1])
    normed_one = (inputs * scale_one * gains_full[0]).astype(BF16)
    qkv = jnp.dot(normed_one, qkv_full, preferred_element_type=F32)
    rank_ref = links.rank.astype(jnp.int32).reshape(1)
    mixed_slots, rotated, lse, peaks = attention_forward(rank_ref, qkv, cosine, sine, segment_ids, group, kvs)
    tokens_own = token_slots[:quarter]
    rows_two, middle, grad_hidden = call_spread_forward(
        jnp.dot(mixed_slots, out_full, preferred_element_type=F32).astype(BF16),
        tokens_own,
        gains_full[1:2],
        grad_rows,
        down_full,
    )

    columns = line * block
    both = jnp.dot(rows_two, gate_up_full, preferred_element_type=F32)
    hidden, grad_both = call_gate_rows(both, grad_hidden)
    grad_down_part = dot_tn(hidden, grad_rows).astype(BF16)
    output_part = jnp.dot(after(hidden, grad_down_part), down_full, preferred_element_type=F32).astype(BF16)
    output_part, output_near = links.swap_core(output_part)
    output_mine, output_other, output_theirs = links.sum_core(output_part, after(output_near, grad_down_part))
    output_second = links.swap_side(output_theirs)
    grad_gate_part = dot_tn(rows_two, grad_both[:, :columns]).astype(BF16)
    output_first = links.swap_side(output_other)
    back = dot_nt(after(grad_both, grad_gate_part), gate_up_full).astype(BF16)
    grad_middle_slots, grad_middle, gain_two, grad_up_part = call_spread_backward(
        back, middle, grad_rows[:quarter], gains_full[1:2], rows_two, grad_both, output_second
    )
    output_second = output_mine[quarter:].astype(F32) + after(output_second, back).astype(F32)
    output_far = links.swap_mp(after(output_second.astype(BF16), grad_middle_slots), 2)
    grad_down_low = links.sum_line(grad_down_part)
    gate_sum = after(links.sum_line(grad_gate_part), grad_down_low)
    up_sum = after(links.sum_line(grad_up_part), gate_sum)
    grad_mixed = dot_nt(grad_middle_slots, out_full).astype(BF16)

    grad_down = grad_down_low.astype(F32)
    down_second, down_direction = lamb_direction(w_down, down_moments[0], down_moments[1], grad_down)
    down_sum = jnp.sum(down_direction * down_direction)

    local_peak = peaks[:, :group, 0].reshape(heads)
    peak_vector = lax.dynamic_update_slice(
        jnp.full((HEADS,), MASKED, F32), local_peak, (links.rank * heads,)
    )
    owner = (links.rank == 0).astype(F32)
    lanes = lax.broadcasted_iota(jnp.int32, (16, HEAD), 1)
    lower = lax.broadcasted_iota(jnp.int32, (16, HEAD), 0) < 8
    early = jnp.broadcast_to(jnp.pad(peak_vector, (0, HEAD - HEADS), constant_values=MASKED), (16, HEAD))
    early = jnp.where(lower, 0.0, early)
    masters = (w_query, w_key, w_value, w_out, w_gate_up, w_down, norm_gains)
    for number, master in enumerate(masters):
        square = jnp.sum(master * master) * (owner if number == 6 else 1.0)
        early = jnp.where(lower & (lanes == number), square, early)
    early = jnp.where(lower & (lanes == 12), down_sum, early)

    grad_qkv = attention_backward(rank_ref, rotated, grad_mixed, lse, cosine, sine, segment_ids, group, kvs)
    grad_qkv_part = dot_tn(normed_one, grad_qkv).astype(BF16)
    grad_out_part = dot_tn(mixed_slots, grad_middle_slots).astype(BF16)
    grad_normed_one = dot_nt(grad_qkv, qkv_full).astype(BF16)
    side_ref = side.astype(jnp.int32).reshape(1)
    gate_theirs = links.swap_side(call_pick_rows(side_ref, gate_sum, grad_qkv))
    input_grad, gain_terms, grad_qkv_own, grad_out = call_finish(
        dp_size,
        after(grad_normed_one, gate_sum),
        tokens_own,
        grad_middle,
        gains_full[0:1],
        gain_two,
        (output_first, down_direction, early, gate_theirs),
        grad_qkv_part,
        grad_out_part,
    )
    output_far = after(output_far, input_grad).astype(F32)
    output_low = (middle + output_mine[:quarter].astype(F32) + output_first.astype(F32) + output_far).astype(BF16)
    output_far = links.swap_mp(output_low, 2)

    summed = [gate_sum, up_sum]
    theirs = [gate_theirs, links.swap_side(call_pick_rows(side_ref, up_sum, gain_terms))]
    gain_terms = gain_terms.reshape(2, width)
    gain_width = norm_gains.shape[1]
    grad_gains = lax.dynamic_slice_in_dim(gain_terms, links.index * gain_width, gain_width, 1)

    small = (w_query, w_key, w_value, w_out, norm_gains)
    small_moments = (query_moments, key_moments, value_moments, out_moments, gains_moments)
    grad_query, grad_key, grad_value, *rest = call_small_step(
        group, kvs, jnp.full((1, HEAD), owner), grad_qkv_own, grad_out, grad_gains, small, small_moments
    )
    theirs = [after(value, grad_query, down_direction, early, output_low) for value in theirs]
    small_seconds, small_directions, small_sums = rest[:SMALL], rest[SMALL : 2 * SMALL], rest[2 * SMALL]
    if block % HEAD == 0:
        grad_gate_up, gate_up_second, gate_up_direction, gate_up_sums = call_gate_up_step(
            line, side.astype(jnp.int32).reshape(1), w_gate_up, gate_up_moments, summed, theirs
        )
    else:
        parts = []
        for j in range(2):
            mine = lax.dynamic_slice_in_dim(summed[j], side * shard, shard, 0)
            sides = [jnp.where(side == 0, mine, theirs[j]), jnp.where(side == 0, theirs[j], mine)]
            parts.append(jnp.stack([value.reshape(shard, line, block) for value in sides], 2))
        grad_gate_up = jnp.stack(parts, 0).reshape(w_gate_up.shape)
        grad_gate_up = grad_gate_up.astype(F32)
        gate_up_second, gate_up_direction = lamb_direction(
            w_gate_up, gate_up_moments[0], gate_up_moments[1], grad_gate_up
        )
        gate_up_sums = jnp.sum((gate_up_direction * gate_up_direction).reshape(-1, 8, 2 * HEAD), 0)
    output_far = after(output_far, gate_up_sums)
    block_output = links.from_slots(links.gather_core(output_low, output_far))
    packed = call_combine_all(dp_size, early, small_sums, gate_up_sums)
    updated = call_small_update(
        group, kvs, links.rank.astype(jnp.int32).reshape(1), packed, small, small_directions
    )
    flat_rows = lambda value: value.reshape(2 * shard, units)
    new_gate_up, copy_gate_up = (
        value.reshape(w_gate_up.shape)
        for value in call_large_update(4, packed, flat_rows(w_gate_up), flat_rows(gate_up_direction))
    )
    new_down, copy_down = call_large_update(5, packed, w_down, down_direction)
    grads = (grad_query, grad_key, grad_value, grad_out, grad_gate_up, grad_down, grad_gains)
    place_large = lambda values, gate_up, down: (*values[:4], gate_up, down, values[4])
    norms = jnp.sqrt(jnp.stack([packed[0, :7], packed[0, 7:14]]))
    return (
        block_output,
        input_grad,
        *grads,
        *place_large(small_seconds, gate_up_second, down_second),
        *place_large(updated[:SMALL], new_gate_up, new_down),
        *place_large(updated[SMALL:], copy_gate_up, copy_down),
        norms,
        packed[8, :HEADS],
    )


def solution(mesh):
    column = P("dp", "mp")
    row = P(("mp", "dp"), None)
    gate_up = P(None, "dp", "mp")
    gains = P(None, "dp")
    params = (column, column, column, row, gate_up, row, gains)
    moments = (
        P(None, "dp", "mp"),
        P(None, "dp", "mp"),
        P(None, "dp", "mp"),
        P(None, ("mp", "dp"), None),
        P(None, None, "dp", "mp"),
        P(None, ("mp", "dp"), None),
        P(None, None, "dp"),
    )
    tokens = P("dp", None)
    return jax.shard_map(
        functools.partial(body, mesh.shape["dp"], mesh.shape["mp"]),
        mesh=mesh,
        in_specs=(tokens, tokens, tokens, *params, *moments),
        out_specs=(tokens, tokens, *params, *params, *params, *params, P(), P()),
        check_vma=False,
    )
```

```python
import functools
import math

import jax
import jax.numpy as jnp
from jax import lax
from jax.experimental import pallas as pl
from jax.experimental.pallas import tpu as pltpu
from jax.sharding import PartitionSpec as P

HEADS = 16
HEAD = 128
BLOCK = 512
CLIP = 10
TILE = 256

NORM_EPS = 1e-05
ROPE_BASE = 1000000.0
RATE = 0.4
DECAY = 0.5
WEIGHT_DECAY = 0.01
STEP_EPS = 1e-06
MASKED = -1e30

F32 = jnp.float32
BF16 = jnp.bfloat16


def rope_tables(length):
    positions = jnp.arange(length, dtype=F32)
    frequency = ROPE_BASE ** (-(jnp.arange(HEAD // 2, dtype=F32) * 2.0) / HEAD)
    angles = positions[:, None] * frequency[None, :]
    cosine, sine = jnp.cos(angles), jnp.sin(angles)
    return jnp.concatenate([cosine, cosine], 1), jnp.concatenate([-sine, sine], 1)


def lasting(microseconds):
    return pl.CostEstimate(flops=0, bytes_accessed=int(microseconds * 3e6), transcendentals=0)


def turn(values, cosine, sine):
    return values * cosine + pltpu.roll(values, HEAD // 2, 1) * sine


def allowed_mask(seg_row_ref, seg_col_ref, row_start, low, high):
    query_pos = row_start + lax.broadcasted_iota(jnp.int32, (TILE, high - low), 0)
    key_pos = low + lax.broadcasted_iota(jnp.int32, (TILE, high - low), 1)
    same = seg_col_ref[row_start : row_start + TILE, :] == seg_row_ref[0, :, low:high]
    return (key_pos <= query_pos) & same


def dot_nt(left, right):
    return lax.dot_general(left, right, (((1,), (1,)), ((), ())), preferred_element_type=F32)


def dot_nn(left, right):
    return lax.dot_general(left, right, (((1,), (0,)), ((), ())), preferred_element_type=F32)


def dot_tn(left, right):
    return lax.dot_general(left, right, (((0,), (0,)), ((), ())), preferred_element_type=F32)


def slot_rows(rank_ref, start):
    return pl.ds(pl.multiple_of(((start // TILE) ^ rank_ref[0]) * TILE, TILE), TILE)


def attend_forward(group, rank_ref, qkv_ref, cos_ref, sin_ref, seg_row_ref, seg_col_ref, out_ref, rot_ref, lse_ref, peak_ref):
    length = qkv_ref.shape[0]
    scale = 1.0 / math.sqrt(HEAD)
    value_columns = slice((group + 1) * HEAD, (group + 2) * HEAD)
    for start in range(0, length, TILE):
        rows, source = slice(start, start + TILE), slot_rows(rank_ref, start)
        for part in range(group + 1):
            columns = slice(part * HEAD, (part + 1) * HEAD)
            turned = turn(qkv_ref[source, columns], cos_ref[rows, :], sin_ref[rows, :])
            rot_ref[rows, columns] = turned.astype(BF16)
        rot_ref[rows, value_columns] = qkv_ref[source, value_columns].astype(BF16)
    key_columns = slice(group * HEAD, (group + 1) * HEAD)
    peak_ref[...] = jnp.full(peak_ref.shape, MASKED, F32)
    peaks = [None] * group
    for start in range(0, length, TILE):
        low, high = max(0, start - BLOCK), start + TILE
        rows = slice(start, start + TILE)
        mask = allowed_mask(seg_row_ref, seg_col_ref, start, low, high)
        keys = rot_ref[low:high, key_columns]
        values = rot_ref[low:high, value_columns]
        for head in range(group):
            columns = slice(head * HEAD, (head + 1) * HEAD)
            scores = jnp.where(mask, dot_nt(rot_ref[rows, columns], keys) * scale, MASKED)
            top = jnp.max(scores, 1, keepdims=True)
            exponent = jnp.exp(scores - top)
            total = jnp.sum(exponent, 1, keepdims=True)
            probs = (exponent * (1.0 / total)).astype(BF16)
            out_ref[slot_rows(rank_ref, start), columns] = dot_nn(probs, values).astype(BF16)
            lse_ref[rows, columns] = jnp.broadcast_to(top + jnp.log(total), (TILE, HEAD))
            peak = jnp.max(top, 0, keepdims=True)
            peaks[head] = peak if peaks[head] is None else jnp.maximum(peaks[head], peak)
    for head in range(group):
        peak_ref[0, head : head + 1, :] = jnp.broadcast_to(peaks[head], (1, HEAD))


def attend_backward(group, rank_ref, rot_ref, grad_ref, lse_ref, cos_ref, sin_ref, seg_row_ref, seg_col_ref, out_ref, dk_ref, dv_ref):
    length = rot_ref.shape[0]
    scale = 1.0 / math.sqrt(HEAD)
    key_columns = slice(group * HEAD, (group + 1) * HEAD)
    value_columns = slice((group + 1) * HEAD, (group + 2) * HEAD)
    dk_ref[...] = jnp.zeros(dk_ref.shape, F32)
    dv_ref[...] = jnp.zeros(dv_ref.shape, F32)
    for start in range(0, length, TILE):
        low, high = max(0, start - BLOCK), start + TILE
        rows = slice(start, start + TILE)
        mask = allowed_mask(seg_row_ref, seg_col_ref, start, low, high)
        keys = rot_ref[low:high, key_columns]
        values = rot_ref[low:high, value_columns]
        for head in range(group):
            columns = slice(head * HEAD, (head + 1) * HEAD)
            queries = rot_ref[rows, columns]
            grads = grad_ref[slot_rows(rank_ref, start), columns]
            scores = dot_nt(queries, keys) * scale
            probs = jnp.exp(jnp.where(mask, scores - lse_ref[rows, columns][:, :1], MASKED))
            grad_probs = dot_nt(grads, values)
            inner = jnp.sum(probs * grad_probs, 1, keepdims=True)
            grad_scores = (probs * (grad_probs - inner)).astype(BF16)
            dv_ref[low:high, :] += dot_tn(probs.astype(BF16), grads)
            dk_ref[low:high, :] += dot_tn(grad_scores, queries)
            grad_query = dot_nn(grad_scores, keys) * scale
            turned = turn(grad_query, cos_ref[rows, :], -sin_ref[rows, :])
            out_ref[slot_rows(rank_ref, start), columns] = turned.astype(BF16)
    for start in range(0, length, TILE):
        rows = slice(start, start + TILE)
        turned = turn(dk_ref[rows, :] * scale, cos_ref[rows, :], -sin_ref[rows, :])
        out_ref[slot_rows(rank_ref, start), key_columns] = turned.astype(BF16)
        out_ref[slot_rows(rank_ref, start), value_columns] = dv_ref[rows, :].astype(BF16)


def attention_specs(length, group):
    wide = pl.BlockSpec((length, (group + 2) * HEAD), lambda kv, rank: (0, kv))
    narrow = pl.BlockSpec((length, group * HEAD), lambda kv, rank: (0, kv))
    table = pl.BlockSpec((length, HEAD), lambda kv, rank: (0, 0))
    seg_row = pl.BlockSpec((1, 1, length), lambda kv, rank: (0, 0, 0))
    seg_col = pl.BlockSpec((length, 1), lambda kv, rank: (0, 0))
    return wide, narrow, table, seg_row, seg_col


def attention_forward(rank, qkv, cosine, sine, segments, group, kv_count):
    length = segments.shape[1]
    wide, narrow, table, seg_row, seg_col = attention_specs(length, group)
    return pl.pallas_call(
        functools.partial(attend_forward, group),
        grid_spec=pltpu.PrefetchScalarGridSpec(
            num_scalar_prefetch=1,
            grid=(kv_count,),
            in_specs=[wide, table, table, seg_row, seg_col],
            out_specs=[narrow, wide, narrow, pl.BlockSpec((1, 8, HEAD), lambda kv, rank: (kv, 0, 0))],
        ),
        out_shape=[
            jax.ShapeDtypeStruct((length, kv_count * group * HEAD), BF16),
            jax.ShapeDtypeStruct((length, kv_count * (group + 2) * HEAD), BF16),
            jax.ShapeDtypeStruct((length, kv_count * group * HEAD), F32),
            jax.ShapeDtypeStruct((kv_count, 8, HEAD), F32),
        ],
        compiler_params=pltpu.CompilerParams(vmem_limit_bytes=48 * 2**20),
        cost_estimate=lasting(12),
        name="attention_forward",
    )(rank, qkv, cosine, sine, segments.reshape(1, 1, length), segments.reshape(length, 1))


def attention_backward(rank, rotated, grads, lse, cosine, sine, segments, group, kv_count):
    length = segments.shape[1]
    wide, narrow, table, seg_row, seg_col = attention_specs(length, group)
    return pl.pallas_call(
        functools.partial(attend_backward, group),
        grid_spec=pltpu.PrefetchScalarGridSpec(
            num_scalar_prefetch=1,
            grid=(kv_count,),
            in_specs=[wide, narrow, narrow, table, table, seg_row, seg_col],
            out_specs=wide,
            scratch_shapes=[pltpu.VMEM((length, HEAD), F32), pltpu.VMEM((length, HEAD), F32)],
        ),
        out_shape=jax.ShapeDtypeStruct((length, kv_count * (group + 2) * HEAD), BF16),
        compiler_params=pltpu.CompilerParams(vmem_limit_bytes=48 * 2**20),
        cost_estimate=lasting(13),
        name="attention_backward",
    )(rank, rotated, grads, lse, cosine, sine, segments.reshape(1, 1, length), segments.reshape(length, 1))


def gate_rows(both_ref, grad_ref, hidden_ref, grad_both_ref):
    columns = grad_ref.shape[1]
    gate, up, grad = both_ref[:, :columns], both_ref[:, columns:], grad_ref[...]
    sigmoid = 1.0 / (1.0 + jnp.exp(-gate))
    silu = gate * sigmoid
    hidden_ref[...] = (silu * up).astype(BF16)
    grad_both_ref[:, :columns] = (grad * up * (sigmoid * (1.0 + gate * (1.0 - sigmoid)))).astype(BF16)
    grad_both_ref[:, columns:] = (grad * silu).astype(BF16)


def call_gate_rows(both, grad):
    rows, columns = grad.shape
    tile = lambda width: pl.BlockSpec((TILE, width), lambda i: (i, 0))
    return pl.pallas_call(
        gate_rows,
        grid=(rows // TILE,),
        in_specs=[tile(2 * columns), tile(columns)],
        out_specs=[tile(columns), tile(2 * columns)],
        out_shape=[jax.ShapeDtypeStruct((rows, columns), BF16), jax.ShapeDtypeStruct((rows, 2 * columns), BF16)],
        cost_estimate=lasting(10),
        name="gate_rows",
    )(both, grad)


def lamb_direction(master, first, second, grad):
    first_moment = DECAY * first + (1.0 - DECAY) * grad
    second_moment = DECAY * second + (1.0 - DECAY) * grad * grad
    return second_moment, first_moment / (jnp.sqrt(second_moment) + STEP_EPS) + WEIGHT_DECAY * master


def gate_up_step(side_ref, master_ref, moment_ref, *refs):
    (gate_mine, up_mine, gate_theirs, up_theirs), (grad_ref, second_ref, direction_ref, sums_ref) = refs[:4], refs[4:]
    part, place = pl.program_id(0), pl.program_id(1)
    mine = jnp.where(part == 0, gate_mine[...], up_mine[...])
    theirs = jnp.where(part == 0, gate_theirs[...], up_theirs[...])
    first = side_ref[0] == 0
    grad = jnp.concatenate([jnp.where(first, mine, theirs), jnp.where(first, theirs, mine)], 1).astype(F32)
    second, direction = lamb_direction(master_ref[0], moment_ref[0, 0], moment_ref[1, 0], grad)
    grad_ref[0], second_ref[0], direction_ref[0] = grad, second, direction

    @pl.when((part == 0) & (place == 0))
    def _():
        sums_ref[...] = jnp.zeros(sums_ref.shape, F32)

    sums_ref[...] += jnp.sum((direction * direction).reshape(-1, 8, direction.shape[1]), 0)


def call_gate_up_step(line, side, master, moments, summed, theirs):
    _, shard, units = master.shape
    block = units // (2 * line)
    whole = pl.BlockSpec((1, shard, 2 * block), lambda g, p, side: (g, 0, p))
    shape = jax.ShapeDtypeStruct(master.shape, F32)
    gate_place = lambda g, p: jnp.where(g == 0, p, line - 1)
    up_place = lambda g, p: jnp.where(g == 1, p, 0)
    return pl.pallas_call(
        gate_up_step,
        grid_spec=pltpu.PrefetchScalarGridSpec(
            num_scalar_prefetch=1,
            grid=(2, line),
            in_specs=[
                whole,
                pl.BlockSpec((2, 1, shard, 2 * block), lambda g, p, side: (0, g, 0, p)),
                pl.BlockSpec((shard, block), lambda g, p, side: (side[0], gate_place(g, p))),
                pl.BlockSpec((shard, block), lambda g, p, side: (side[0], up_place(g, p))),
                pl.BlockSpec((shard, block), lambda g, p, side: (0, gate_place(g, p))),
                pl.BlockSpec((shard, block), lambda g, p, side: (0, up_place(g, p))),
            ],
            out_specs=[whole, whole, whole, pl.BlockSpec((8, 2 * block), lambda g, p, side: (0, 0))],
        ),
        out_shape=[shape, shape, shape, jax.ShapeDtypeStruct((8, 2 * block), F32)],
        cost_estimate=lasting(16),
        name="gate_up_step",
    )(side, master, moments, *summed, *theirs)


VMEM_ALL = pl.BlockSpec(memory_space=pltpu.VMEM)
SMALL = 5


def small_step(group, kvs, owner_ref, grad_qkv_ref, grad_out_ref, grad_gains_ref, *refs):
    masters, moments, refs = refs[:SMALL], refs[SMALL : 2 * SMALL], refs[2 * SMALL :]
    grads, seconds, directions, sums_ref = refs[:3], refs[3:8], refs[8:13], refs[13]
    step = (group + 2) * HEAD
    for kv in range(kvs):
        low = kv * step
        for ref, start, columns in ((grads[0], 0, group * HEAD), (grads[1], group * HEAD, HEAD), (grads[2], (group + 1) * HEAD, HEAD)):
            ref[:, kv * columns : (kv + 1) * columns] = grad_qkv_ref[:, low + start : low + start + columns]
    sums_ref[...] = jnp.zeros(sums_ref.shape, F32)
    for number in range(SMALL):
        grad = (grads[0], grads[1], grads[2], grad_out_ref, grad_gains_ref)[number][...]
        moment = moments[number]
        second, direction = lamb_direction(masters[number][...], moment[0], moment[1], grad)
        seconds[number][...] = second
        directions[number][...] = direction
        total = jnp.sum(jnp.sum(direction * direction, 0, keepdims=True), 1, keepdims=True)
        row = jnp.broadcast_to(total, (1, HEAD))
        sums_ref[number : number + 1, :] = row * owner_ref[...] if number == SMALL - 1 else row


def call_small_step(group, kvs, owner, grad_qkv, grad_out, grad_gains, masters, moments):
    like = lambda arrays: [jax.ShapeDtypeStruct(array.shape, F32) for array in arrays]
    return pl.pallas_call(
        functools.partial(small_step, group, kvs),
        in_specs=[VMEM_ALL] * (4 + 2 * SMALL),
        out_specs=[VMEM_ALL] * 14,
        out_shape=[*like(masters[:3]), *like(masters), *like(masters), jax.ShapeDtypeStruct((8, HEAD), F32)],
        compiler_params=pltpu.CompilerParams(vmem_limit_bytes=40 * 2**20),
        cost_estimate=lasting(6),
        name="small_step",
    )(owner, grad_qkv, grad_out, grad_gains, *masters, *moments)


def pick_lane(row, lane):
    lanes = lax.broadcasted_iota(jnp.int32, row.shape, 1)
    return jnp.sum(jnp.where(lanes == lane, row, 0.0), 1, keepdims=True)


def rate_of(packed_ref, number):
    squares = packed_ref[0:1, :]
    weight, update = jnp.sqrt(pick_lane(squares, number)), jnp.sqrt(pick_lane(squares, 7 + number))
    return RATE * (weight / (update + STEP_EPS))


def small_update(group, kvs, rank_ref, packed_ref, *refs):
    masters, directions, news, copies = (refs[k * SMALL : (k + 1) * SMALL] for k in range(4))
    gamma = CLIP / jnp.maximum(packed_ref[8:9, :], float(CLIP))
    heads = [pick_lane(gamma, rank_ref[0] * (group * kvs) + head) for head in range(group * kvs)]
    for place, number in enumerate((0, 1, 2, 3, 6)):
        rate = rate_of(packed_ref, number)
        if place > 1:
            stepped = masters[place][...] - rate * directions[place][...]
            news[place][...] = stepped
            copies[place][...] = stepped.astype(BF16)
            continue
        for head in range(group * kvs if place == 0 else kvs):
            scale = heads[head]
            if place == 1:
                scale = functools.reduce(jnp.minimum, heads[head * group : (head + 1) * group])
            columns = slice(head * HEAD, (head + 1) * HEAD)
            stepped = masters[place][:, columns] - rate * directions[place][:, columns]
            stepped = stepped * jnp.sqrt(scale)
            news[place][:, columns] = stepped
            copies[place][:, columns] = stepped.astype(BF16)


def call_small_update(group, kvs, rank, packed, masters, directions):
    like = lambda kind: [jax.ShapeDtypeStruct(array.shape, kind) for array in masters]
    return pl.pallas_call(
        functools.partial(small_update, group, kvs),
        in_specs=[pl.BlockSpec(memory_space=pltpu.SMEM), *[VMEM_ALL] * (1 + 2 * SMALL)],
        out_specs=[VMEM_ALL] * (2 * SMALL),
        out_shape=[*like(F32), *like(BF16)],
        compiler_params=pltpu.CompilerParams(vmem_limit_bytes=40 * 2**20),
        cost_estimate=lasting(5),
        name="small_update",
    )(rank, packed, *masters, *directions)


def large_update(number, packed_ref, master_ref, direction_ref, new_ref, copy_ref):
    stepped = master_ref[...] - rate_of(packed_ref, number) * direction_ref[...]
    new_ref[...] = stepped
    copy_ref[...] = stepped.astype(BF16)


def call_large_update(number, packed, master, direction):
    rows, columns = master.shape
    tile = min(rows, 128)
    blocks = pl.BlockSpec((tile, columns), lambda i: (i, 0))
    return pl.pallas_call(
        functools.partial(large_update, number),
        grid=(rows // tile,),
        in_specs=[pl.BlockSpec((16, HEAD), lambda i: (0, 0)), blocks, blocks],
        out_specs=[blocks, blocks],
        out_shape=[jax.ShapeDtypeStruct(master.shape, F32), jax.ShapeDtypeStruct(master.shape, BF16)],
        cost_estimate=lasting(4),
        name="large_update",
    )(packed, master, direction)


MESH = pl.DeviceIdType.MESH
WHOLE = pl.BlockSpec(memory_space=pltpu.VMEM)
CHUNKS = 8
AHEAD = 1


def greet(partners):
    barrier = pltpu.get_barrier_semaphore()
    for partner in partners:
        pl.semaphore_signal(barrier, inc=1, device_id=partner, device_id_type=MESH)
    pl.semaphore_wait(barrier, len(partners))


def sender(send_sems, recv_sems, log):
    def copy(kind, chunk, source, target, device):
        made = pltpu.make_async_remote_copy(
            src_ref=source,
            dst_ref=target,
            send_sem=send_sems.at[kind, chunk],
            recv_sem=recv_sems.at[kind, chunk],
            device_id=device,
            device_id_type=MESH,
        )
        log.append(made)
        return made

    return copy


def partners_of():
    rank, index = lax.axis_index("mp"), lax.axis_index("dp")
    return {"mp": rank ^ 1}, {"mp": rank ^ 2}, {"dp": index ^ 1}


def pick_rows(side_ref, rows_ref, _, out_ref):
    out_ref[...] = rows_ref[...]


def call_pick_rows(side, values, ready):
    rows, columns = values.shape[0] // 2, values.shape[1]
    return pl.pallas_call(
        pick_rows,
        grid_spec=pltpu.PrefetchScalarGridSpec(
            num_scalar_prefetch=1,
            grid=(1,),
            in_specs=[
                pl.BlockSpec((rows, columns), lambda i, side: (1 - side[0], 0)),
                pl.BlockSpec(memory_space=pl.ANY),
            ],
            out_specs=pl.BlockSpec((rows, columns), lambda i, side: (0, 0)),
        ),
        out_shape=jax.ShapeDtypeStruct((rows, columns), values.dtype),
        cost_estimate=lasting(2),
        name="pick_rows",
    )(side, values, ready)


class Everyone:
    def __init__(self, line, near_ref, line_ref, near_send, near_recv, line_send, line_recv):
        self.line, self.near_ref, self.line_ref = line, near_ref, line_ref
        self.near_send, self.near_recv, self.line_send, self.line_recv = near_send, near_recv, line_send, line_recv
        self.index, self.rank = lax.axis_index("dp"), lax.axis_index("mp")
        self.place, self.side = self.index // 2, self.index % 2
        self.code = self.side * 4 + self.rank

    @staticmethod
    def scratch(line, shape):
        return [
            pltpu.VMEM((8, *shape), F32),
            pltpu.VMEM((line, *shape), F32),
            pltpu.SemaphoreType.DMA((8,)),
            pltpu.SemaphoreType.DMA((8,)),
            pltpu.SemaphoreType.DMA((line,)),
            pltpu.SemaphoreType.DMA((line,)),
        ]

    def peer(self, k):
        return {"dp": self.index ^ (k // 4), "mp": self.rank ^ (k % 4)}

    def along(self, k):
        return {"dp": ((self.place + k) % self.line) * 2 + self.side}

    def partners(self):
        return [self.peer(k) for k in range(1, 8)] + [self.along(k) for k in range(1, self.line)]

    @staticmethod
    def add(left, right):
        return left + right

    def near_copy(self, k, slot):
        return pltpu.make_async_remote_copy(
            src_ref=self.near_ref.at[self.code],
            dst_ref=self.near_ref.at[slot],
            send_sem=self.near_send.at[k],
            recv_sem=self.near_recv.at[slot],
            device_id=self.peer(k),
            device_id_type=MESH,
        )

    def line_copy(self, k, slot):
        return pltpu.make_async_remote_copy(
            src_ref=self.line_ref.at[self.place],
            dst_ref=self.line_ref.at[slot],
            send_sem=self.line_send.at[k],
            recv_sem=self.line_recv.at[slot],
            device_id=self.along(k),
            device_id_type=MESH,
        )

    @staticmethod
    def total(ref, count, fold):
        value = ref[0]
        for k in range(1, count):
            value = fold(value, ref[k])
        return value

    def send_near(self):
        for k in range(1, 8):
            self.near_copy(k, self.code).start()

    def send_line(self, fold):
        for k in range(1, 8):
            self.near_copy(k, self.code ^ k).wait_recv()
        self.line_ref[self.place] = self.total(self.near_ref, 8, fold)
        for k in range(1, self.line):
            self.line_copy(k, self.place).start()

    def result(self, fold):
        for k in range(1, self.line):
            self.line_copy(k, (self.place + k) % self.line).wait_recv()
        value = self.total(self.line_ref, self.line, fold)
        for k in range(1, 8):
            self.near_copy(k, self.code).wait_send()
        for k in range(1, self.line):
            self.line_copy(k, self.place).wait_send()
        return value


def spread_forward(part_ref, tokens_ref, gain_ref, grad_ref, down_ref, rows_ref, middle_ref, hidden_ref, near_ref, out_ref, far_ref, grad_in_ref, down_in_ref, hidden_out_ref, send_sems, recv_sems, fetch_sems, store_sems):
    fetches = [
        pltpu.make_async_copy(source, target, fetch_sems.at[k])
        for k, (source, target) in enumerate(((grad_ref, grad_in_ref), (down_ref, down_in_ref)))
    ]
    for fetch in fetches:
        fetch.start()
    band = hidden_out_ref.shape[0] // CHUNKS
    stores = []

    def multiply(i):
        rows = pl.ds(i * band, band)
        hidden_out_ref[rows, :] = dot_nt(grad_in_ref[rows, :], down_in_ref[...])
        stores.append(pltpu.make_async_copy(hidden_out_ref.at[rows], hidden_ref.at[rows], store_sems.at[i]))
        stores[-1].start()

    core, far, pair = partners_of()
    quarter, _ = tokens_ref.shape
    size = quarter // CHUNKS
    at = lambda slot, i: pl.ds(slot * quarter + i * size, size)
    greet([core, far, pair])
    log = []
    copy = sender(send_sems, recv_sems, log)
    near = {}
    for i in range(CHUNKS):
        for k in range(2):
            near[k, i] = copy(k, i, part_ref.at[at(2 * k + 1, i)], near_ref.at[at(k, i)], core)
            near[k, i].start()
    sums = {}

    def send_sum(i):
        near[1, i].wait_recv()
        total = part_ref[at(2, i), :].astype(F32) + near_ref[at(1, i), :].astype(F32)
        out_ref[at(0, i), :] = total.astype(BF16)
        sums[i] = copy(2, i, out_ref.at[at(0, i)], far_ref.at[at(0, i)], far)
        sums[i].start()

    for i in range(AHEAD):
        send_sum(i)
    moves = {}
    for i in range(CHUNKS + 2):
        if i + AHEAD < CHUNKS:
            send_sum(i + AHEAD)
        if i < CHUNKS:
            near[0, i].wait_recv()
            sums[i].wait_recv()
            middle = tokens_ref[at(0, i), :].astype(F32) + (
                part_ref[at(0, i), :].astype(F32)
                + near_ref[at(0, i), :].astype(F32)
                + far_ref[at(0, i), :].astype(F32)
            )
            middle_ref[at(0, i), :] = middle
            rows_ref[at(0, i), :] = (middle * inverse_rms(middle) * gain_ref[0:1, :]).astype(BF16)
            own = rows_ref.at[at(0, i)]
            for kind, slot, device in ((3, 2, far), (4, 4, pair), (6, 1, core)):
                moves[kind, i] = copy(kind, i, own, rows_ref.at[at(slot, i)], device)
                moves[kind, i].start()
        j = i - 1
        if 0 <= j < CHUNKS:
            moves[3, j].wait_recv()
            for kind, slot, device in ((5, 6, pair), (7, 3, core)):
                moves[kind, j] = copy(kind, j, rows_ref.at[at(2, j)], rows_ref.at[at(slot, j)], device)
                moves[kind, j].start()
            moves[4, j].wait_recv()
            moves[8, j] = copy(8, j, rows_ref.at[at(4, j)], rows_ref.at[at(5, j)], core)
            moves[8, j].start()
        j = i - 2
        if 0 <= j < CHUNKS:
            moves[5, j].wait_recv()
            moves[9, j] = copy(9, j, rows_ref.at[at(6, j)], rows_ref.at[at(7, j)], core)
            moves[9, j].start()
        if i == 0:
            for fetch in fetches:
                fetch.wait()
        if i < CHUNKS:
            multiply(i)
    for i in range(CHUNKS):
        for kind in (6, 7, 8, 9):
            moves[kind, i].wait_recv()
    for made in log:
        made.wait_send()
    for store in stores:
        store.wait()


def call_spread_forward(part, tokens_own, gain, grad_rows, down):
    quarter, width = tokens_own.shape
    hidden = (grad_rows.shape[0], down.shape[0])
    hbm = pl.BlockSpec(memory_space=pl.ANY)
    return pl.pallas_call(
        spread_forward,
        in_specs=[*[WHOLE] * 3, hbm, hbm],
        out_specs=[WHOLE, WHOLE, hbm],
        out_shape=[
            jax.ShapeDtypeStruct((8 * quarter, width), BF16),
            jax.ShapeDtypeStruct((quarter, width), F32),
            jax.ShapeDtypeStruct(hidden, F32),
        ],
        scratch_shapes=[
            pltpu.VMEM((2 * quarter, width), BF16),
            pltpu.VMEM((quarter, width), BF16),
            pltpu.VMEM((quarter, width), BF16),
            pltpu.VMEM(grad_rows.shape, BF16),
            pltpu.VMEM(down.shape, BF16),
            pltpu.VMEM(hidden, F32),
            pltpu.SemaphoreType.DMA((10, CHUNKS)),
            pltpu.SemaphoreType.DMA((10, CHUNKS)),
            pltpu.SemaphoreType.DMA((2,)),
            pltpu.SemaphoreType.DMA((CHUNKS,)),
        ],
        compiler_params=pltpu.CompilerParams(
            collective_id=1, has_side_effects=True, vmem_limit_bytes=54 * 2**20
        ),
        cost_estimate=lasting(64),
        name="spread_forward",
    )(part, tokens_own, gain, grad_rows, down)


def pull_chunk(values, scale_gain, grad):
    scale = inverse_rms(values)
    turned = grad * scale_gain
    inner = jnp.mean(turned * values, -1, keepdims=True)
    return scale * turned - (scale * scale * scale) * values * inner, grad * values * scale


def spread_backward(part_ref, middle_ref, grad_ref, gain_ref, left_ref, both_ref, _, rows_ref, total_ref, gain_out_ref, up_ref, near_ref, side_out_ref, side_in_ref, far_out_ref, far_in_ref, left_in_ref, right_in_ref, up_out_ref, send_sems, recv_sems, fetch_sems, store_sems):
    units = right_in_ref.shape[1]
    fetches = [
        pltpu.make_async_copy(left_ref, left_in_ref, fetch_sems.at[0]),
        pltpu.make_async_copy(both_ref.at[:, pl.ds(units, units)], right_in_ref, fetch_sems.at[1]),
    ]
    for fetch in fetches:
        fetch.start()
    band = up_out_ref.shape[0] // CHUNKS
    stores = []

    def multiply(i):
        rows = pl.ds(i * band, band)
        up_out_ref[rows, :] = dot_tn(left_in_ref[:, rows], right_in_ref[...]).astype(BF16)
        stores.append(pltpu.make_async_copy(up_out_ref.at[rows], up_ref.at[rows], store_sems.at[i]))
        stores[-1].start()

    core, far, pair = partners_of()
    quarter, width = middle_ref.shape
    size = quarter // CHUNKS
    at = lambda slot, i: pl.ds(slot * quarter + i * size, size)
    greet([core, far, pair])
    log = []
    copy = sender(send_sems, recv_sems, log)
    near, side, sums, moves = {}, {}, {}, {}
    for i in range(CHUNKS):
        for k in (2, 3, 0, 1):
            near[k, i] = copy(k, i, part_ref.at[at(2 * k + 1, i)], near_ref.at[at(k, i)], core)
            near[k, i].start()

    def pairs(k, i):
        return part_ref[at(2 * k, i), :].astype(F32) + near_ref[at(k, i), :].astype(F32)

    def send_side(i):
        for k in (1, 0):
            near[2 + k, i].wait_recv()
            side_out_ref[at(k, i), :] = pairs(2 + k, i).astype(BF16)
            side[k, i] = copy(4 + k, i, side_out_ref.at[at(k, i)], side_in_ref.at[at(k, i)], pair)
            side[k, i].start()

    for i in range(AHEAD):
        send_side(i)
    gain_sum = jnp.zeros((1, width), F32)
    for i in range(CHUNKS + 2):
        if i + AHEAD < CHUNKS:
            send_side(i + AHEAD)
        if i < CHUNKS:
            near[1, i].wait_recv()
            side[1, i].wait_recv()
            far_out_ref[at(0, i), :] = (pairs(1, i) + side_in_ref[at(1, i), :].astype(F32)).astype(BF16)
            sums[i] = copy(6, i, far_out_ref.at[at(0, i)], far_in_ref.at[at(0, i)], far)
            sums[i].start()
        j = i - 1
        if 0 <= j < CHUNKS:
            near[0, j].wait_recv()
            side[0, j].wait_recv()
            sums[j].wait_recv()
            grad = pairs(0, j) + side_in_ref[at(0, j), :].astype(F32) + far_in_ref[at(0, j), :].astype(F32)
            back, gain_part = pull_chunk(middle_ref[at(0, j), :], gain_ref[0:1, :], grad)
            gain_sum = gain_sum + jnp.sum(gain_part, 0, keepdims=True)
            total = grad_ref[at(0, j), :].astype(F32) + back
            total_ref[at(0, j), :] = total
            rows_ref[at(0, j), :] = total.astype(BF16)
            own = rows_ref.at[at(0, j)]
            for kind, slot, device in ((7, 2, far), (8, 1, core)):
                moves[kind, j] = copy(kind, j, own, rows_ref.at[at(slot, j)], device)
                moves[kind, j].start()
        j = i - 2
        if 0 <= j < CHUNKS:
            moves[7, j].wait_recv()
            moves[9, j] = copy(9, j, rows_ref.at[at(2, j)], rows_ref.at[at(3, j)], core)
            moves[9, j].start()
        if i == 0:
            for fetch in fetches:
                fetch.wait()
        if i < CHUNKS:
            multiply(i)
    gain_out_ref[...] = jnp.broadcast_to(gain_sum, gain_out_ref.shape)
    for i in range(CHUNKS):
        for kind in (8, 9):
            moves[kind, i].wait_recv()
    for made in log:
        made.wait_send()
    for store in stores:
        store.wait()


def call_spread_backward(part, middle, grad_own, gain, left, both, ready):
    quarter, width = middle.shape
    units = both.shape[1] // 2
    hbm = pl.BlockSpec(memory_space=pl.ANY)
    return pl.pallas_call(
        spread_backward,
        in_specs=[*[WHOLE] * 4, hbm, hbm, hbm],
        out_specs=[*[WHOLE] * 3, hbm],
        out_shape=[
            jax.ShapeDtypeStruct((4 * quarter, width), BF16),
            jax.ShapeDtypeStruct((quarter, width), F32),
            jax.ShapeDtypeStruct((8, width), F32),
            jax.ShapeDtypeStruct((width, units), BF16),
        ],
        scratch_shapes=[
            pltpu.VMEM((4 * quarter, width), BF16),
            pltpu.VMEM((2 * quarter, width), BF16),
            pltpu.VMEM((2 * quarter, width), BF16),
            pltpu.VMEM((quarter, width), BF16),
            pltpu.VMEM((quarter, width), BF16),
            pltpu.VMEM(left.shape, BF16),
            pltpu.VMEM((left.shape[0], units), BF16),
            pltpu.VMEM((width, units), BF16),
            pltpu.SemaphoreType.DMA((10, CHUNKS)),
            pltpu.SemaphoreType.DMA((10, CHUNKS)),
            pltpu.SemaphoreType.DMA((2,)),
            pltpu.SemaphoreType.DMA((CHUNKS,)),
        ],
        compiler_params=pltpu.CompilerParams(
            collective_id=2, has_side_effects=True, vmem_limit_bytes=56 * 2**20
        ),
        cost_estimate=lasting(68),
        name="spread_backward",
    )(part, middle, grad_own, gain, left, both, ready)


def finish(line, part_ref, tokens_ref, total_ref, gain_ref, *refs):
    gain_two_ref, grads_refs, refs = refs[0], refs[1:3], refs[7:]
    input_ref, gain_out_ref, *owned_refs = refs[:4]
    rows_ref, near_ref, far_out_ref, far_in_ref, refs = *refs[4:8], refs[1:]
    side_in_refs, up_out_refs, up_in_refs, down_out_refs, down_in_refs = (refs[k : k + 2] for k in range(7, 17, 2))
    send_sems, recv_sems, side_send, side_recv, line_send, line_recv, *exchange = refs[17:]
    core, far, pair = partners_of()
    index = lax.axis_index("dp")
    place, side = index // 2, index % 2
    above, below = {"dp": index + 2}, {"dp": index - 2}
    quarter, width = tokens_ref.shape
    size = quarter // CHUNKS
    last = line - 1
    at = lambda slot, i: pl.ds(slot * quarter + i * size, size)

    def block(w, where, which):
        rows = owned_refs[w].shape[0]
        return pl.ds((where * 2 + which) * rows, rows)


    everyone = Everyone(line, *exchange)
    greet(everyone.partners())
    log = []
    copy = sender(send_sems, recv_sems, log)
    near, sums, moves = {}, {}, {}
    for i in range(CHUNKS):
        for k in (1, 0):
            near[k, i] = copy(k, i, part_ref.at[at(2 * k + 1, i)], near_ref.at[at(k, i)], core)
            near[k, i].start()

    def side_copy(w, where):
        return pltpu.make_async_remote_copy(
            src_ref=grads_refs[w].at[block(w, where, 1 - side)],
            dst_ref=side_in_refs[w].at[where],
            send_sem=side_send.at[w, where],
            recv_sem=side_recv.at[w, where],
            device_id=pair,
            device_id_type=MESH,
        )

    def line_copy(w, upward, step):
        out_ref, in_ref = (up_out_refs[w], up_in_refs[w]) if upward else (down_out_refs[w], down_in_refs[w])
        way = 0 if upward else 1
        return pltpu.make_async_remote_copy(
            src_ref=out_ref.at[step - 1],
            dst_ref=in_ref.at[step - 1],
            send_sem=line_send.at[w, way, step - 1],
            recv_sem=line_recv.at[w, way, step - 1],
            device_id=above if upward else below,
            device_id_type=MESH,
        )

    for step in range(last, 0, -1):

        @pl.when(place + step <= last)
        def _(step=step):
            for w in range(2):
                side_copy(w, place + step).start()

        @pl.when(place - step >= 0)
        def _(step=step):
            for w in range(2):
                side_copy(w, place - step).start()

    for w in range(2):
        side_copy(w, place).start()

    for i in range(CHUNKS):
        near[1, i].wait_recv()
        summed = part_ref[at(2, i), :].astype(F32) + near_ref[at(1, i), :].astype(F32)
        far_out_ref[at(0, i), :] = summed.astype(BF16)
        sums[i] = copy(2, i, far_out_ref.at[at(0, i)], far_in_ref.at[at(0, i)], far)
        sums[i].start()

    def term(w, where):
        return grads_refs[w][block(w, where, side), :].astype(F32) + side_in_refs[w][where].astype(F32)

    def line_step(step):
        for w in range(2):

            @pl.when(place + step <= last)
            def _(w=w):
                side_copy(w, place + step).wait_recv()
                value = term(w, place + step)
                up_out_refs[w][step - 1] = value.astype(BF16)
                if step < last:

                    @pl.when(place > 0)
                    def _():
                        line_copy(w, True, step + 1).wait_recv()
                        up_out_refs[w][step - 1] = (value + up_in_refs[w][step].astype(F32)).astype(BF16)

                line_copy(w, True, step).start()

            @pl.when(place - step >= 0)
            def _(w=w):
                side_copy(w, place - step).wait_recv()
                value = term(w, place - step)
                down_out_refs[w][step - 1] = value.astype(BF16)
                if step < last:

                    @pl.when(place < last)
                    def _():
                        line_copy(w, False, step + 1).wait_recv()
                        down_out_refs[w][step - 1] = (value + down_in_refs[w][step].astype(F32)).astype(BF16)

                line_copy(w, False, step).start()

    def settle(slot, i):
        start = pl.multiple_of((lax.axis_index("mp") ^ slot) * quarter + i * size, size)
        input_ref[pl.ds(start, size), :] = rows_ref[at(slot, i), :].astype(F32)

    gain_sum = jnp.zeros((1, width), F32)
    steps = list(range(last, 0, -1))
    for i in range(CHUNKS + 1):
        if i < CHUNKS:
            near[0, i].wait_recv()
            sums[i].wait_recv()
            grad = (
                part_ref[at(0, i), :].astype(F32)
                + near_ref[at(0, i), :].astype(F32)
                + far_in_ref[at(0, i), :].astype(F32)
            )
            back, gain_part = pull_chunk(tokens_ref[at(0, i), :].astype(F32), gain_ref[0:1, :], grad)
            gain_sum = gain_sum + jnp.sum(gain_part, 0, keepdims=True)
            rows_ref[at(0, i), :] = (total_ref[at(0, i), :] + back).astype(BF16)
            settle(0, i)
            own = rows_ref.at[at(0, i)]
            for kind, slot, device in ((3, 2, far), (4, 1, core)):
                moves[kind, i] = copy(kind, i, own, rows_ref.at[at(slot, i)], device)
                moves[kind, i].start()
        if steps:
            line_step(steps.pop(0))
        j = i - 1
        if 0 <= j < CHUNKS:
            moves[3, j].wait_recv()
            settle(2, j)
            moves[5, j] = copy(5, j, rows_ref.at[at(2, j)], rows_ref.at[at(3, j)], core)
            moves[5, j].start()
    while steps:
        line_step(steps.pop(0))
    columns = gain_out_ref.shape[1]
    for r in range(4):
        cut = slice(r * columns, (r + 1) * columns)
        everyone.near_ref[everyone.code, r : r + 1, :] = gain_sum[:, cut]
        everyone.near_ref[everyone.code, r + 4 : r + 5, :] = gain_two_ref[0:1, cut]
    everyone.send_near()
    everyone.send_line(everyone.add)
    for w in range(2):
        side_copy(w, place).wait_recv()
        owned_refs[w][...] = term(w, place)

        @pl.when(place > 0)
        def _(w=w):
            line_copy(w, True, 1).wait_recv()
            owned_refs[w][...] += up_in_refs[w][0].astype(F32)

        @pl.when(place < last)
        def _(w=w):
            line_copy(w, False, 1).wait_recv()
            owned_refs[w][...] += down_in_refs[w][0].astype(F32)

    gain_out_ref[...] = everyone.result(everyone.add)
    for i in range(CHUNKS):
        for kind, slot in ((4, 1), (5, 3)):
            moves[kind, i].wait_recv()
            settle(slot, i)
    for made in log:
        made.wait_send()
    for w in range(2):
        for where in range(line):
            side_copy(w, where).wait_send()
        for step in range(last, 0, -1):

            @pl.when(place + step <= last)
            def _(w=w, step=step):
                line_copy(w, True, step).wait_send()

            @pl.when(place - step >= 0)
            def _(w=w, step=step):
                line_copy(w, False, step).wait_send()


def call_finish(dp_size, part, tokens_own, total, gain, gain_two, ready, *grads):
    quarter, width = tokens_own.shape
    line = dp_size // 2
    owned = [(grad.shape[0] // dp_size, grad.shape[1]) for grad in grads]
    stacks = lambda count: [pltpu.VMEM((count, *shape), BF16) for shape in owned]
    return pl.pallas_call(
        functools.partial(finish, line),
        in_specs=[*[WHOLE] * 7, *[pl.BlockSpec(memory_space=pl.ANY)] * 4],
        out_specs=[WHOLE] * 4,
        out_shape=[
            jax.ShapeDtypeStruct((4 * quarter, width), F32),
            jax.ShapeDtypeStruct((8, width // 4), F32),
            *[jax.ShapeDtypeStruct(shape, F32) for shape in owned],
        ],
        scratch_shapes=[
            pltpu.VMEM((4 * quarter, width), BF16),
            pltpu.VMEM((2 * quarter, width), BF16),
            pltpu.VMEM((quarter, width), BF16),
            pltpu.VMEM((quarter, width), BF16),
            *stacks(line),
            *stacks(line - 1),
            *stacks(line - 1),
            *stacks(line - 1),
            *stacks(line - 1),
            pltpu.SemaphoreType.DMA((6, CHUNKS)),
            pltpu.SemaphoreType.DMA((6, CHUNKS)),
            pltpu.SemaphoreType.DMA((2, line)),
            pltpu.SemaphoreType.DMA((2, line)),
            pltpu.SemaphoreType.DMA((2, 2, line)),
            pltpu.SemaphoreType.DMA((2, 2, line)),
            *Everyone.scratch(line, (8, width // 4)),
        ],
        compiler_params=pltpu.CompilerParams(
            collective_id=3, has_side_effects=True, vmem_limit_bytes=56 * 2**20
        ),
        cost_estimate=lasting(85),
        name="finish",
    )(part, tokens_own, total, gain, gain_two, *grads, *ready)


def gather_weights(line, own_ref, out_ref, gains_ref, grad_ref, full_ref, out_full_ref, gains_full_ref, rows_ref, local_sems, side_send, side_recv, line_send, line_recv, rows_send, rows_recv, staged_ref):
    index = lax.axis_index("dp")
    place, side = index // 2, index % 2
    pair, above, below = {"dp": index ^ 1}, {"dp": index + 2}, {"dp": index - 2}
    rank = lax.axis_index("mp")
    core, far = {"mp": rank ^ 1}, {"mp": rank ^ 2}
    quarter = grad_ref.shape[0] // 4
    slot_of = lambda k: rows_ref.at[pl.ds(k * quarter, quarter)]
    quarter_of = lambda k: grad_ref.at[pl.ds((rank ^ k) * quarter, quarter)]
    last = line - 1
    owns, fulls = (own_ref, out_ref, gains_ref), (full_ref, out_full_ref, gains_full_ref)
    all_three = range(3)

    barrier = pltpu.get_barrier_semaphore()
    pl.semaphore_signal(barrier, inc=1, device_id=pair, device_id_type=MESH)
    pl.semaphore_signal(barrier, inc=1, device_id=core, device_id_type=MESH)
    pl.semaphore_signal(barrier, inc=1, device_id=far, device_id_type=MESH)

    @pl.when(place < last)
    def _():
        pl.semaphore_signal(barrier, inc=1, device_id=above, device_id_type=MESH)

    @pl.when(place > 0)
    def _():
        pl.semaphore_signal(barrier, inc=1, device_id=below, device_id_type=MESH)

    pl.semaphore_wait(barrier, 3 + (place < last).astype(jnp.int32) + (place > 0).astype(jnp.int32))

    def slot(which, where, side):
        rows = owns[which].shape[0]
        return fulls[which].at[pl.ds((where * 2 + side) * rows, rows)]

    def views(which, where):
        return slot(which, where, side)

    def source(which, where, first):
        return owns[which] if first else views(which, where)

    def line_copy(which, upward, where, first=False):
        way = 0 if upward else 1
        return pltpu.make_async_remote_copy(
            src_ref=source(which, where, first),
            dst_ref=views(which, where),
            send_sem=line_send.at[which, way, where],
            recv_sem=line_recv.at[which, way, where],
            device_id=above if upward else below,
            device_id_type=MESH,
        )

    def side_copy(which, where, first=False):
        return pltpu.make_async_remote_copy(
            src_ref=source(which, where, first),
            dst_ref=views(which, where),
            send_sem=side_send.at[which, where],
            recv_sem=side_recv.at[which, where],
            device_id=pair,
            device_id_type=MESH,
        )

    def side_arrival(which, where):
        target = slot(which, where, 1 - side)
        return pltpu.make_async_remote_copy(
            src_ref=target,
            dst_ref=target,
            send_sem=side_send.at[which, where],
            recv_sem=side_recv.at[which, where],
            device_id=pair,
            device_id_type=MESH,
        )

    @pl.when(place < last)
    def _():
        for which in all_three:
            line_copy(which, True, place, True).start()

    @pl.when(place > 0)
    def _():
        for which in all_three:
            line_copy(which, False, place, True).start()

    for which in all_three:
        side_copy(which, place, True).start()
    here = [pltpu.make_async_copy(source(w, place, True), views(w, place), local_sems.at[w]) for w in all_three]
    for made in here:
        made.start()
    staged_of = lambda k: staged_ref.at[pl.ds(k * quarter, quarter)]
    fetches = [pltpu.make_async_copy(quarter_of(k), staged_of(k), local_sems.at[3 + k]) for k in range(4)]
    stores = [pltpu.make_async_copy(staged_of(k), slot_of(k), local_sems.at[7 + k]) for k in range(4)]
    for made in fetches:
        made.start()

    def rows_copy(number, source, target, device):
        return pltpu.make_async_remote_copy(
            src_ref=source,
            dst_ref=target,
            send_sem=rows_send.at[number],
            recv_sem=rows_recv.at[number],
            device_id=device,
            device_id_type=MESH,
        )

    over = rows_copy(0, quarter_of(0), slot_of(4), pair)
    across = rows_copy(1, slot_of(4), slot_of(6), far)
    near = [rows_copy(2 + k, slot_of(4 + 2 * k), slot_of(5 + 2 * k), core) for k in range(2)]
    over.start()

    for step in range(1, line):

        @pl.when(place - step >= 0)
        def _(step=step):
            where = place - step
            for which in all_three:
                line_copy(which, True, where).wait_recv()

                @pl.when(place < last)
                def _(which=which):
                    line_copy(which, True, where).start()

                side_copy(which, where).start()

        @pl.when(place + step <= last)
        def _(step=step):
            where = place + step
            for which in all_three:
                line_copy(which, False, where).wait_recv()

                @pl.when(place > 0)
                def _(which=which):
                    line_copy(which, False, where).start()

                side_copy(which, where).start()

        if step == 1:
            for fetch, store in zip(fetches, stores):
                fetch.wait()
                store.start()
            over.wait_recv()
            across.start()
            near[0].start()

    across.wait_recv()
    near[1].start()
    for made in here + stores:
        made.wait()
    for where in range(line):
        for which in all_three:
            side_arrival(which, where).wait_recv()
            side_copy(which, where).wait_send()

            @pl.when((where <= place) & (place < last))
            def _(which=which, where=where):
                line_copy(which, True, where).wait_send()

            @pl.when((where >= place) & (place > 0))
            def _(which=which, where=where):
                line_copy(which, False, where).wait_send()

    for k in range(2):
        near[k].wait_recv()
        near[k].wait_send()
    over.wait_send()
    across.wait_send()


def call_gather_weights(dp_size, grads, *owns):
    line = dp_size // 2
    hbm = pl.BlockSpec(memory_space=pl.ANY)
    return pl.pallas_call(
        functools.partial(gather_weights, line),
        in_specs=[hbm] * 4,
        out_specs=[hbm] * 4,
        out_shape=[
            *[jax.ShapeDtypeStruct((dp_size * own.shape[0], own.shape[1]), own.dtype) for own in owns],
            jax.ShapeDtypeStruct((2 * grads.shape[0], grads.shape[1]), grads.dtype),
        ],
        scratch_shapes=[
            pltpu.SemaphoreType.DMA((11,)),
            pltpu.SemaphoreType.DMA((3, line)),
            pltpu.SemaphoreType.DMA((3, line)),
            pltpu.SemaphoreType.DMA((3, 2, line)),
            pltpu.SemaphoreType.DMA((3, 2, line)),
            pltpu.SemaphoreType.DMA((4,)),
            pltpu.SemaphoreType.DMA((4,)),
            pltpu.VMEM(grads.shape, grads.dtype),
        ],
        compiler_params=pltpu.CompilerParams(
            collective_id=4, has_side_effects=True, vmem_limit_bytes=16 * 2**20
        ),
        cost_estimate=lasting(120),
        name="gather_weights",
    )(*owns, grads)


def combine_all(line, early_ref, small_ref, gate_up_ref, out_ref, *exchange):
    everyone = Everyone(line, *exchange)
    greet(everyone.partners())
    lanes = lax.broadcasted_iota(jnp.int32, early_ref.shape, 1)
    adds = lax.broadcasted_iota(jnp.int32, early_ref.shape, 0) < 8
    fold = lambda left, right: jnp.where(adds, left + right, jnp.maximum(left, right))
    value = early_ref[...]
    gate_up = jnp.sum(jnp.sum(gate_up_ref[...], 0, keepdims=True), 1, keepdims=True)
    terms = [small_ref[k : k + 1, :] for k in range(SMALL)] + [jnp.broadcast_to(gate_up, (1, HEAD))]
    for term, number in zip(terms, (0, 1, 2, 3, 6, 4)):
        value = jnp.where(adds & (lanes == 7 + number), term, value)
    everyone.near_ref[everyone.code] = value
    everyone.send_near()
    everyone.send_line(fold)
    out_ref[...] = everyone.result(fold)


def call_combine_all(dp_size, early, small, gate_up):
    line = dp_size // 2
    return pl.pallas_call(
        functools.partial(combine_all, line),
        in_specs=[WHOLE] * 3,
        out_specs=WHOLE,
        out_shape=jax.ShapeDtypeStruct(early.shape, F32),
        scratch_shapes=Everyone.scratch(line, early.shape),
        compiler_params=pltpu.CompilerParams(collective_id=6, has_side_effects=True),
        cost_estimate=lasting(10),
        name="combine_all",
    )(early, small, gate_up)


class Links:
    def __init__(self, dp_size, mp_size):
        self.dp, self.mp, self.line = dp_size, mp_size, dp_size // 2
        self.index = lax.axis_index("dp")
        self.place, self.side, self.rank = self.index // 2, self.index % 2, lax.axis_index("mp")
        self.lines = [[place * 2 + side for place in range(self.line)] for side in range(2)]

    def swap_mp(self, value, bit):
        return lax.ppermute(value, "mp", [(i, i ^ bit) for i in range(self.mp)])

    def swap_side(self, value):
        return lax.ppermute(value, "dp", [(i, i ^ 1) for i in range(self.dp)])

    def gather_line(self, own):
        return lax.all_gather(own, "dp", axis=0, tiled=True, axis_index_groups=self.lines)

    def sum_line(self, parts):
        return lax.psum_scatter(parts, "dp", scatter_dimension=0, tiled=True, axis_index_groups=self.lines)


    def to_slots(self, values):
        rows = values.shape[0] // self.mp
        return jnp.concatenate(
            [lax.dynamic_slice_in_dim(values, (self.rank ^ k) * rows, rows, 0) for k in range(self.mp)], 0
        )

    def from_slots(self, values):
        rows = values.shape[0] // self.mp
        cuts = [values[k * rows : (k + 1) * rows] for k in range(self.mp)]
        odd = (self.rank & 1) == 1
        high = (self.rank & 2) == 2
        cuts = [jnp.where(odd, cuts[k ^ 1], cuts[k]) for k in range(self.mp)]
        cuts = [jnp.where(high, cuts[k ^ 2], cuts[k]) for k in range(self.mp)]
        return jnp.concatenate(cuts, 0)

    def gather_core(self, quarter, far):
        rows = quarter.shape[0]
        near = self.swap_mp(jnp.concatenate([quarter, far], 0), 1)
        return jnp.concatenate([quarter, near[:rows], far, near[rows:]], 0)

    def swap_core(self, slots):
        rows = slots.shape[0] // 8
        picked = lambda ks: jnp.concatenate([slots[k * rows : (k + 1) * rows] for k in ks], 0)
        return slots, self.swap_mp(picked((1, 3, 5, 7)), 1)

    def sum_core(self, slots, near):
        rows = slots.shape[0] // 8
        add = lambda ks, low: jnp.concatenate(
            [
                slots[k * rows : (k + 1) * rows].astype(F32) + near[i * rows : (i + 1) * rows].astype(F32)
                for i, k in enumerate(ks, low)
            ],
            0,
        ).astype(BF16)
        return add((0, 2), 0), add((4,), 2), add((6,), 3)


def after(value, *others):
    return lax.optimization_barrier((value, *others))[0]


def inverse_rms(values):
    return lax.rsqrt(jnp.mean(values * values, -1, keepdims=True) + NORM_EPS)


def body(
    dp_size,
    mp_size,
    tokens,
    cotangent,
    segment_ids,
    w_query,
    w_key,
    w_value,
    w_out,
    w_gate_up,
    w_down,
    norm_gains,
    query_moments,
    key_moments,
    value_moments,
    out_moments,
    gate_up_moments,
    down_moments,
    gains_moments,
):
    links = Links(dp_size, mp_size)
    line, side = links.line, links.side
    heads = w_query.shape[1] // HEAD
    kvs = w_key.shape[1] // HEAD
    group = heads // kvs
    width = tokens.shape[1]
    shard = w_query.shape[0]
    units = w_gate_up.shape[2]
    block = units // (line * 2)

    def interleave(query, key, value):
        parts = []
        for kv in range(kvs):
            parts.append(query[..., kv * group * HEAD : (kv + 1) * group * HEAD])
            parts.append(key[..., kv * HEAD : (kv + 1) * HEAD])
            parts.append(value[..., kv * HEAD : (kv + 1) * HEAD])
        return jnp.concatenate(parts, -1)

    by_side = w_gate_up.reshape(2, shard, line, 2, block)

    def side_units(which):
        cut = lax.dynamic_index_in_dim(by_side, which, 3, keepdims=False).astype(BF16)
        return jnp.concatenate([cut[0].reshape(shard, -1), cut[1].reshape(shard, -1)], 1)

    token_slots = links.to_slots(tokens)
    inputs = token_slots.astype(F32)
    scale_one = inverse_rms(inputs)
    down_full = links.gather_line(w_down.astype(BF16))
    own_units = side_units(side)
    sent_units = links.swap_side(side_units(1 - side))
    rows_pair = jnp.zeros((2 * shard, own_units.shape[1]), BF16)
    rows_pair = lax.dynamic_update_slice(rows_pair, own_units, (side * shard, 0))
    rows_pair = lax.dynamic_update_slice(rows_pair, sent_units, ((1 - side) * shard, 0))
    gate_up_full = after(links.gather_line(rows_pair), down_full)
    gains_low = norm_gains.astype(BF16).astype(F32)
    gains_rows = jnp.concatenate([gains_low, jnp.zeros((6, gains_low.shape[1]), F32)], 0)
    qkv_full, out_full, gains_shards, grad_rows = call_gather_weights(
        dp_size,
        cotangent,
        after(interleave(w_query, w_key, w_value).astype(BF16), rows_pair, scale_one, token_slots),
        w_out.astype(BF16),
        gains_rows,
    )
    gains_full = jnp.transpose(gains_shards.reshape(dp_size, 8, -1), (1, 0, 2)).reshape(8, width)

    quarter = tokens.shape[0] // 4

    cosine, sine = rope_tables(segment_ids.shape[1])
    normed_one = (inputs * scale_one * gains_full[0]).astype(BF16)
    qkv = jnp.dot(normed_one, qkv_full, preferred_element_type=F32)
    rank_ref = links.rank.astype(jnp.int32).reshape(1)
    mixed_slots, rotated, lse, peaks = attention_forward(rank_ref, qkv, cosine, sine, segment_ids, group, kvs)
    tokens_own = token_slots[:quarter]
    rows_two, middle, grad_hidden = call_spread_forward(
        jnp.dot(mixed_slots, out_full, preferred_element_type=F32).astype(BF16),
        tokens_own,
        gains_full[1:2],
        grad_rows,
        down_full,
    )

    columns = line * block
    both = jnp.dot(rows_two, gate_up_full, preferred_element_type=F32)
    hidden, grad_both = call_gate_rows(both, grad_hidden)
    grad_down_part = dot_tn(hidden, grad_rows).astype(BF16)
    output_part = jnp.dot(after(hidden, grad_down_part), down_full, preferred_element_type=F32).astype(BF16)
    output_part, output_near = links.swap_core(output_part)
    output_mine, output_other, output_theirs = links.sum_core(output_part, after(output_near, grad_down_part))
    output_second = links.swap_side(output_theirs)
    grad_gate_part = dot_tn(rows_two, grad_both[:, :columns]).astype(BF16)
    output_first = links.swap_side(output_other)
    back = dot_nt(after(grad_both, grad_gate_part), gate_up_full).astype(BF16)
    grad_middle_slots, grad_middle, gain_two, grad_up_part = call_spread_backward(
        back, middle, grad_rows[:quarter], gains_full[1:2], rows_two, grad_both, output_second
    )
    output_second = output_mine[quarter:].astype(F32) + after(output_second, back).astype(F32)
    output_far = links.swap_mp(after(output_second.astype(BF16), grad_middle_slots), 2)
    grad_down_low = links.sum_line(grad_down_part)
    gate_sum = after(links.sum_line(grad_gate_part), grad_down_low)
    up_sum = after(links.sum_line(grad_up_part), gate_sum)
    grad_mixed = dot_nt(grad_middle_slots, out_full).astype(BF16)

    grad_down = grad_down_low.astype(F32)
    down_second, down_direction = lamb_direction(w_down, down_moments[0], down_moments[1], grad_down)
    down_sum = jnp.sum(down_direction * down_direction)

    local_peak = peaks[:, :group, 0].reshape(heads)
    peak_vector = lax.dynamic_update_slice(
        jnp.full((HEADS,), MASKED, F32), local_peak, (links.rank * heads,)
    )
    owner = (links.rank == 0).astype(F32)
    lanes = lax.broadcasted_iota(jnp.int32, (16, HEAD), 1)
    lower = lax.broadcasted_iota(jnp.int32, (16, HEAD), 0) < 8
    early = jnp.broadcast_to(jnp.pad(peak_vector, (0, HEAD - HEADS), constant_values=MASKED), (16, HEAD))
    early = jnp.where(lower, 0.0, early)
    masters = (w_query, w_key, w_value, w_out, w_gate_up, w_down, norm_gains)
    for number, master in enumerate(masters):
        square = jnp.sum(master * master) * (owner if number == 6 else 1.0)
        early = jnp.where(lower & (lanes == number), square, early)
    early = jnp.where(lower & (lanes == 12), down_sum, early)

    grad_qkv = attention_backward(rank_ref, rotated, grad_mixed, lse, cosine, sine, segment_ids, group, kvs)
    grad_qkv_part = dot_tn(normed_one, grad_qkv).astype(BF16)
    grad_out_part = dot_tn(mixed_slots, grad_middle_slots).astype(BF16)
    grad_normed_one = dot_nt(grad_qkv, qkv_full).astype(BF16)
    side_ref = side.astype(jnp.int32).reshape(1)
    gate_theirs = links.swap_side(call_pick_rows(side_ref, gate_sum, grad_qkv))
    input_grad, gain_terms, grad_qkv_own, grad_out = call_finish(
        dp_size,
        after(grad_normed_one, gate_sum),
        tokens_own,
        grad_middle,
        gains_full[0:1],
        gain_two,
        (output_first, down_direction, early, gate_theirs),
        grad_qkv_part,
        grad_out_part,
    )
    output_far = after(output_far, input_grad).astype(F32)
    output_low = (middle + output_mine[:quarter].astype(F32) + output_first.astype(F32) + output_far).astype(BF16)
    output_far = links.swap_mp(output_low, 2)

    summed = [gate_sum, up_sum]
    theirs = [gate_theirs, links.swap_side(call_pick_rows(side_ref, up_sum, gain_terms))]
    gain_terms = gain_terms.reshape(2, width)
    gain_width = norm_gains.shape[1]
    grad_gains = lax.dynamic_slice_in_dim(gain_terms, links.index * gain_width, gain_width, 1)

    small = (w_query, w_key, w_value, w_out, norm_gains)
    small_moments = (query_moments, key_moments, value_moments, out_moments, gains_moments)
    grad_query, grad_key, grad_value, *rest = call_small_step(
        group, kvs, jnp.full((1, HEAD), owner), grad_qkv_own, grad_out, grad_gains, small, small_moments
    )
    theirs = [after(value, grad_query, down_direction, early, output_low) for value in theirs]
    small_seconds, small_directions, small_sums = rest[:SMALL], rest[SMALL : 2 * SMALL], rest[2 * SMALL]
    if block % HEAD == 0:
        grad_gate_up, gate_up_second, gate_up_direction, gate_up_sums = call_gate_up_step(
            line, side.astype(jnp.int32).reshape(1), w_gate_up, gate_up_moments, summed, theirs
        )
    else:
        parts = []
        for j in range(2):
            mine = lax.dynamic_slice_in_dim(summed[j], side * shard, shard, 0)
            sides = [jnp.where(side == 0, mine, theirs[j]), jnp.where(side == 0, theirs[j], mine)]
            parts.append(jnp.stack([value.reshape(shard, line, block) for value in sides], 2))
        grad_gate_up = jnp.stack(parts, 0).reshape(w_gate_up.shape)
        grad_gate_up = grad_gate_up.astype(F32)
        gate_up_second, gate_up_direction = lamb_direction(
            w_gate_up, gate_up_moments[0], gate_up_moments[1], grad_gate_up
        )
        gate_up_sums = jnp.sum((gate_up_direction * gate_up_direction).reshape(-1, 8, 2 * HEAD), 0)
    output_far = after(output_far, gate_up_sums)
    block_output = links.from_slots(links.gather_core(output_low, output_far))
    packed = call_combine_all(dp_size, early, small_sums, gate_up_sums)
    updated = call_small_update(
        group, kvs, links.rank.astype(jnp.int32).reshape(1), packed, small, small_directions
    )
    flat_rows = lambda value: value.reshape(2 * shard, units)
    new_gate_up, copy_gate_up = (
        value.reshape(w_gate_up.shape)
        for value in call_large_update(4, packed, flat_rows(w_gate_up), flat_rows(gate_up_direction))
    )
    new_down, copy_down = call_large_update(5, packed, w_down, down_direction)
    grads = (grad_query, grad_key, grad_value, grad_out, grad_gate_up, grad_down, grad_gains)
    place_large = lambda values, gate_up, down: (*values[:4], gate_up, down, values[4])
    norms = jnp.sqrt(jnp.stack([packed[0, :7], packed[0, 7:14]]))
    return (
        block_output,
        input_grad,
        *grads,
        *place_large(small_seconds, gate_up_second, down_second),
        *place_large(updated[:SMALL], new_gate_up, new_down),
        *place_large(updated[SMALL:], copy_gate_up, copy_down),
        norms,
        packed[8, :HEADS],
    )


def solution(mesh):
    column = P("dp", "mp")
    row = P(("mp", "dp"), None)
    gate_up = P(None, "dp", "mp")
    gains = P(None, "dp")
    params = (column, column, column, row, gate_up, row, gains)
    moments = (
        P(None, "dp", "mp"),
        P(None, "dp", "mp"),
        P(None, "dp", "mp"),
        P(None, ("mp", "dp"), None),
        P(None, None, "dp", "mp"),
        P(None, ("mp", "dp"), None),
        P(None, None, "dp"),
    )
    tokens = P("dp", None)
    return jax.shard_map(
        functools.partial(body, mesh.shape["dp"], mesh.shape["mp"]),
        mesh=mesh,
        in_specs=(tokens, tokens, tokens, *params, *moments),
        out_specs=(tokens, tokens, *params, *params, *params, *params, P(), P()),
        check_vma=False,
    )
```
